32 devices in a mesh: gx: 8 (over z, y), gy: 4 (over x, core).
Axes of the slice: x: 2, y: 2, z: 4, core: 2. Of those that a mesh axis runs over, the one named last changes fastest.
Arguments:
- features: bfloat16 [256, 64, 512], P(('gx', 'gy')), may hold values from -6 to 6
- neighbours: int32 [256, 6], P(('gx', 'gy')), may hold values from 0 to 16, as said below
- counts: int32 [32], P(('gx', 'gy')), may hold values from 1 to 8, as said below
- conv_weight: bfloat16 [64, 448], replicated, may hold values from -0.25 to 0.25
- down_weight: bfloat16 [128, 512], replicated, may hold values from -0.25 to 0.25
- head_weight: bfloat16 [128, 128], replicated, may hold values from -0.5 to 0.5
- coarse_map: int32 [32, 8], P(('gx', 'gy')), may hold values from 0 to 32, as said below
- latent_grad: bfloat16 [32, 512, 128], P(('gx', 'gy')), may hold values from -6 to 6
Outputs:
- latent: bfloat16 [32, 512, 128], P(('gx', 'gy'))
- features_grad: bfloat16 [256, 64, 512], P(('gx', 'gy'))
- conv_grad: float32 [64, 448], replicated
- down_grad: float32 [128, 512], replicated
- head_grad: float32 [128, 128], replicated
The draws below stay inside these ranges and needn't reach their ends.
Inputs may be any that keep to these rules, and one draw needn't show every extreme that they name: `counts`: in every draw, max(1, (devices along gx times devices along gy) // 8) columns have exactly 8 active blocks; each other column has between 1 and 4. 16 means no neighbour; a value below 8 is an active slot of the same column; a value v of 8 or more is the active slot v - 8 of the adjacent column in that direction; the z directions never name another column; inactive slots have no neighbours. `coarse_map`: 32 marks an empty octant; every other entry names an active block's octant, and each such octant is named at most once among the four columns that share a merged list.
All inputs are finite; a program needn't handle non-finite values.
Results may differ from the reference program's by a relative error of at most 0.013.
Values may be sent and summed in bfloat16 or wider, within the bound.
No kernel may reach another device: no remote copies, remote signals or barrier semaphores. Data moves between devices by JAX's collectives and lax.ppermute only.
A program may use at most 128 MiB of HBM per device.

```python
import jax
import jax.numpy as jnp
from jax import lax

C1 = 64
C2 = 128
NB = 8
NC = 1
BLOCKS = 256
CBLOCKS = 32
N_GX = 8
N_GY = 4


def group_counts(key):
    devices = N_GX * N_GY
    base = jax.random.randint(jax.random.fold_in(key, 101), (devices,), NB // 8, NB // 2 + 1)
    order = jax.random.permutation(jax.random.fold_in(key, 102), devices)
    return jnp.where(order < max(1, devices // 8), NB, base).astype(jnp.int32)


def draw_counts(key, part):
    return group_counts(key)


def draw_neighbours(key, part):
    devices = N_GX * N_GY
    counts = group_counts(key)
    blocks = jnp.arange(devices * NB)
    column = blocks // NB
    slots = blocks % NB
    column_x = column // N_GY
    column_y = column % N_GY
    is_live = slots < counts[column]
    empty = 2 * NB
    offsets = ((-N_GY, column_x > 0), (N_GY, column_x < N_GX - 1), (-1, column_y > 0), (1, column_y < N_GY - 1))
    entries = []
    for direction in range(6):
        dir_key = jax.random.fold_in(key, 200 + direction)
        category = jax.random.randint(jax.random.fold_in(dir_key, 1), (devices * NB,), 0, 10)
        nearby = jax.random.randint(jax.random.fold_in(dir_key, 2), (devices * NB,), 0, counts[column])
        if direction < 4:
            other = jnp.clip(column + offsets[direction][0], 0, devices - 1)
            remote = NB + jax.random.randint(jax.random.fold_in(dir_key, 3), (devices * NB,), 0, counts[other])
            entry_value = jnp.where(category < 4, nearby, jnp.where((category < 8) & offsets[direction][1], remote, empty))
        else:
            entry_value = jnp.where(category < 7, nearby, empty)
        entries.append(jnp.where(is_live, entry_value, empty))
    return jnp.stack(entries, axis=1).astype(jnp.int32)


def draw_coarse_map(key, part):
    counts = group_counts(key)
    half_x = N_GX // 2
    half_y = N_GY // 2
    groups = half_x * half_y
    octant_total = 4 * NB
    octant_ids = jnp.arange(octant_total)
    member = octant_ids // NB
    slots = octant_ids % NB
    member_x = member // 2
    member_y = member % 2

    def one_group(group_index, group_key):
        start_x = 2 * (group_index // half_y)
        start_y = 2 * (group_index % half_y)
        column = (start_x + member_x) * N_GY + start_y + member_y
        is_live = slots < counts[column]
        order_rank = jnp.cumsum(is_live.astype(jnp.int32)) - 1
        places = jax.random.permutation(group_key, octant_total)
        target = jnp.where(is_live, places[jnp.clip(order_rank, 0, octant_total - 1)], octant_total)
        owner = target // (NC * 8)
        relation = (member_x ^ owner // 2) + 2 * (member_y ^ owner % 2)
        entry_value = (relation * NB + slots).astype(jnp.int32)
        lookup = jnp.full((octant_total + 1,), 4 * NB, jnp.int32).at[target].set(entry_value)
        return lookup[:octant_total]
    group_keys = jax.random.split(jax.random.fold_in(key, 300), groups)
    tables = jax.vmap(one_group)(jnp.arange(groups), group_keys)
    tables = tables.reshape(half_x, half_y, 2, 2, NC, 8).transpose(0, 2, 1, 3, 4, 5)
    return tables.reshape(N_GX * N_GY * NC, 8).astype(jnp.int32)


def levels(own_key, extent, cuts, smallest, largest):
    def one(position, blocks):
        heights = jax.random.uniform(jax.random.fold_in(jax.random.fold_in(own_key, 6), position), (blocks,), jnp.float32, smallest / len(cuts), largest / len(cuts))
        return jnp.repeat(jnp.exp(heights), extent[position] // blocks).reshape((-1,) + (1,) * (len(extent) - position - 1))

    level = one(*cuts[0])
    for cut in cuts[1:]:
        level = level * one(*cut)
    return level


def bell_draw(rng, dims, scale, limit, shards=(), kind=jnp.bfloat16):
    array = jax.random.normal(rng, dims, jnp.float32) * scale
    if len(shards) > 0:
        array = levels(rng, dims, shards, -0.22, 0.18) * array
    return jnp.clip(array, min=-limit, max=limit).astype(kind)


def setup_inputs(seed: int = 0) -> dict:
    splits = jax.random.split(jax.random.key(seed), 9)
    return {
        "features": bell_draw(splits[0], (BLOCKS, C1, 512), 1.0, 6.0, ((0, 32),)),
        "neighbours": draw_neighbours(jax.random.fold_in(splits[8], 71), 0),
        "counts": draw_counts(jax.random.fold_in(splits[8], 71), 0),
        "conv_weight": bell_draw(splits[3], (C1, 7 * C1), (7 * C1) ** -0.5, 0.25),
        "down_weight": bell_draw(splits[4], (C2, 8 * C1), (8 * C1) ** -0.5, 0.25),
        "head_weight": bell_draw(splits[5], (C2, C2), C2 ** -0.5, 0.5),
        "coarse_map": draw_coarse_map(jax.random.fold_in(splits[8], 71), 0),
        "latent_grad": bell_draw(splits[7], (CBLOCKS, 512, C2), 1.0, 6.0, ((0, 32),)),
    }


def silu_grad(values):
    sigmoid_value = jax.nn.sigmoid(values)
    return sigmoid_value * (1.0 + values * (1.0 - sigmoid_value))

def face_layers(volume):
    number, channels = (volume.shape[0], volume.shape[1])

    def flatten(plane):
        return plane.reshape(number, channels * 64)
    return (flatten(volume[:, :, 7]), flatten(volume[:, :, 0]), flatten(volume[:, :, :, 7]), flatten(volume[:, :, :, 0]), flatten(volume[:, :, :, :, 7]), flatten(volume[:, :, :, :, 0]))

def pick_rows(local_rows, remote_rows, index):
    width = local_rows.shape[1]
    pooled = jnp.concatenate([local_rows, remote_rows, jnp.zeros((1, width), local_rows.dtype)], axis=0)
    return pooled[index]

def neighbour_stack(volume, remotes, links):
    number, channels = (volume.shape[0], volume.shape[1])
    faces = face_layers(volume)
    blank = jnp.zeros_like(faces[4])
    sources = (remotes[0], remotes[1], remotes[2], remotes[3], blank, blank)
    picked = [pick_rows(faces[direction], sources[direction], links[:, direction]).reshape(number, channels, 8, 8) for direction in range(6)]
    x_minus = jnp.concatenate([picked[0][:, :, None], volume[:, :, :7]], axis=2)
    x_plus = jnp.concatenate([volume[:, :, 1:], picked[1][:, :, None]], axis=2)
    y_minus = jnp.concatenate([picked[2][:, :, :, None], volume[:, :, :, :7]], axis=3)
    y_plus = jnp.concatenate([volume[:, :, :, 1:], picked[3][:, :, :, None]], axis=3)
    z_minus = jnp.concatenate([picked[4][..., None], volume[..., :7]], axis=4)
    z_plus = jnp.concatenate([volume[..., 1:], picked[5][..., None]], axis=4)
    joined = jnp.concatenate([volume, x_minus, x_plus, y_minus, y_plus, z_minus, z_plus], axis=1)
    return joined.reshape(number, 7 * channels, 512)

def stack_grad(taps_grad, links):
    number, channels = (taps_grad.shape[0], taps_grad.shape[1] // 7)
    parts = taps_grad.reshape(number, 7, channels, 8, 8, 8)
    grad_volume = parts[:, 0]
    grad_volume = grad_volume + jnp.pad(parts[:, 1, :, 1:], ((0, 0), (0, 0), (0, 1), (0, 0), (0, 0)))
    grad_volume = grad_volume + jnp.pad(parts[:, 2, :, :7], ((0, 0), (0, 0), (1, 0), (0, 0), (0, 0)))
    grad_volume = grad_volume + jnp.pad(parts[:, 3, :, :, 1:], ((0, 0), (0, 0), (0, 0), (0, 1), (0, 0)))
    grad_volume = grad_volume + jnp.pad(parts[:, 4, :, :, :7], ((0, 0), (0, 0), (0, 0), (1, 0), (0, 0)))
    grad_volume = grad_volume + jnp.pad(parts[:, 5, :, :, :, 1:], ((0, 0), (0, 0), (0, 0), (0, 0), (0, 1)))
    grad_volume = grad_volume + jnp.pad(parts[:, 6, :, :, :, :7], ((0, 0), (0, 0), (0, 0), (0, 0), (1, 0)))
    face_grads = (parts[:, 1, :, 0], parts[:, 2, :, 7], parts[:, 3, :, :, 0], parts[:, 4, :, :, 7], parts[:, 5, :, :, :, 0], parts[:, 6, :, :, :, 7])
    pools = [jnp.zeros((2 * number + 1, channels * 64), jnp.float32).at[links[:, direction]].add(face_grads[direction].reshape(number, channels * 64)) for direction in range(6)]
    shaped = [pools[direction][:number].reshape(number, channels, 8, 8) for direction in range(6)]
    grad_volume = grad_volume.at[:, :, 7].add(shaped[0])
    grad_volume = grad_volume.at[:, :, 0].add(shaped[1])
    grad_volume = grad_volume.at[:, :, :, 7].add(shaped[2])
    grad_volume = grad_volume.at[:, :, :, 0].add(shaped[3])
    grad_volume = grad_volume.at[:, :, :, :, 7].add(shaped[4])
    grad_volume = grad_volume.at[:, :, :, :, 0].add(shaped[5])
    far_rows = jnp.stack([pools[direction][number:2 * number] for direction in range(4)]).astype(jnp.bfloat16)
    return (grad_volume, far_rows)

def add_faces(grad_volume, into_xhigh, into_xlow, into_yhigh, into_ylow):
    number, channels = (grad_volume.shape[0], grad_volume.shape[1])

    def planes(rows):
        return rows.astype(jnp.float32).reshape(number, channels, 8, 8)
    grad_volume = grad_volume.at[:, :, 7].add(planes(into_xhigh))
    grad_volume = grad_volume.at[:, :, 0].add(planes(into_xlow))
    grad_volume = grad_volume.at[:, :, :, 7].add(planes(into_yhigh))
    grad_volume = grad_volume.at[:, :, :, 0].add(planes(into_ylow))
    return grad_volume

def to_patches(volume):
    number, channels = (volume.shape[0], volume.shape[1])
    split = volume.reshape(number, channels, 4, 2, 4, 2, 4, 2).transpose(0, 1, 3, 5, 7, 2, 4, 6)
    return split.reshape(number, channels * 8, 64)

def from_patches(patch):
    number, channels = (patch.shape[0], patch.shape[1] // 8)
    split = patch.reshape(number, channels, 2, 2, 2, 4, 4, 4).transpose(0, 1, 5, 2, 6, 3, 7, 4)
    return split.reshape(number, channels, 512)

def shift_grid(values, axis_number, steps):
    grid = values.reshape(N_GX, N_GY, NB, values.shape[-1])
    length = grid.shape[axis_number]
    first = lax.slice_in_dim(grid, 0, 1, axis=axis_number)
    if steps == 1:
        moved = jnp.concatenate([jnp.zeros_like(first), lax.slice_in_dim(grid, 0, length - 1, axis=axis_number)], axis=axis_number)
    else:
        moved = jnp.concatenate([lax.slice_in_dim(grid, 1, length, axis=axis_number), jnp.zeros_like(first)], axis=axis_number)
    return moved.reshape(values.shape)

def reference(features, neighbours, counts, conv_weight, down_weight, head_weight, coarse_map, latent_grad):
    devices = N_GX * N_GY
    slot_owner = jnp.arange(BLOCKS) // NB
    active = jnp.arange(BLOCKS) % NB < counts[slot_owner]
    masked_parity = jnp.where(active[:, None, None], features, jnp.zeros((), jnp.bfloat16))
    masked = from_patches(masked_parity.reshape(BLOCKS, C1 * 8, 64))
    faces = face_layers(masked.reshape(BLOCKS, C1, 8, 8, 8))
    remotes = (shift_grid(faces[0], 0, 1), shift_grid(faces[1], 0, -1), shift_grid(faces[2], 1, 1), shift_grid(faces[3], 1, -1))
    conv_f = conv_weight.astype(jnp.float32)
    down_f = down_weight.astype(jnp.float32)
    head_f = head_weight.astype(jnp.float32)

    def per_device(values):
        return values.reshape((devices, values.shape[0] // devices) + values.shape[1:])

    def level_one(items):
        local_rows, remote_a, remote_b, remote_c, remote_d, links = items
        taps = neighbour_stack(local_rows.reshape(NB, C1, 8, 8, 8), (remote_a, remote_b, remote_c, remote_d), links)
        hidden = jnp.einsum('ok,bkv->bov', conv_f, taps.astype(jnp.float32))
        act = jax.nn.silu(hidden).astype(jnp.bfloat16)
        return (taps, hidden, act)

    def forward_one(items):
        taps, hidden, act = level_one(items)
        octants = jnp.einsum('ok,bkv->bvo', down_f, to_patches(act).astype(jnp.float32)).astype(jnp.bfloat16)
        return octants.reshape(NB, 64 * C2)
    level_inputs = (per_device(masked), per_device(remotes[0]), per_device(remotes[1]), per_device(remotes[2]), per_device(remotes[3]), per_device(neighbours))
    octants = lax.map(forward_one, level_inputs)
    grid = octants.reshape(N_GX // 2, 2, N_GY // 2, 2, NB, 64 * C2)
    across_x = jnp.flip(grid, 1)
    across_y = jnp.flip(grid, 3)
    across_both = jnp.flip(across_x, 3)
    merged = jnp.concatenate([grid, across_x, across_y, across_both], axis=4).reshape(devices, 4 * NB, 64 * C2)

    def coarse_one(items):
        merged_rows, links, grad_rows = items
        padded = jnp.concatenate([merged_rows, jnp.zeros((1, 64 * C2), jnp.bfloat16)], axis=0)
        coarse = padded[links].reshape(NC, 512, C2)
        coarse_act = jax.nn.silu(coarse.astype(jnp.float32)).astype(jnp.bfloat16)
        latent = jnp.einsum('oi,cvi->cvo', head_f, coarse_act.astype(jnp.float32)).astype(jnp.bfloat16)
        grad_f = grad_rows.astype(jnp.float32)
        act_grad = jnp.einsum('oi,cvo->cvi', head_f, grad_f)
        coarse_grad = (act_grad * silu_grad(coarse.astype(jnp.float32))).astype(jnp.bfloat16)
        head_part = jnp.einsum('cvo,cvi->oi', grad_f, coarse_act.astype(jnp.float32))
        back_rows = jnp.zeros((4 * NB + 1, 64 * C2), jnp.float32).at[links.reshape(-1)].add(coarse_grad.reshape(NC * 8, 64 * C2).astype(jnp.float32))
        return (latent, back_rows[:4 * NB].astype(jnp.bfloat16), head_part)
    latent, merged_grad, head_parts = lax.map(coarse_one, (merged, per_device(coarse_map), per_device(latent_grad)))
    back = merged_grad.astype(jnp.float32).reshape(N_GX // 2, 2, N_GY // 2, 2, 4, NB, 64 * C2)
    octant_grad = back[:, :, :, :, 0] + jnp.flip(back[:, :, :, :, 1], 1) + jnp.flip(back[:, :, :, :, 2], 3) + jnp.flip(jnp.flip(back[:, :, :, :, 3], 1), 3)
    octant_grad = octant_grad.astype(jnp.bfloat16).reshape(devices, NB, 64, C2)

    def backward_one(items):
        level_items, grad_octant = items
        taps, hidden, act = level_one(level_items)
        grad_f = grad_octant.astype(jnp.float32)
        down_part = jnp.einsum('bvo,bkv->ok', grad_f, to_patches(act).astype(jnp.float32))
        patch_grad = jnp.einsum('ok,bvo->bkv', down_f, grad_f)
        hidden_grad = (from_patches(patch_grad) * silu_grad(hidden)).astype(jnp.bfloat16)
        conv_part = jnp.einsum('bov,bkv->ok', hidden_grad.astype(jnp.float32), taps.astype(jnp.float32))
        taps_grad = jnp.einsum('ok,bov->bkv', conv_f, hidden_grad.astype(jnp.float32))
        near_grad, far_rows = stack_grad(taps_grad, level_items[5])
        return (near_grad, far_rows, conv_part, down_part)
    near_grad, far_rows, conv_parts, down_parts = lax.map(backward_one, (level_inputs, octant_grad))
    into_xhigh = shift_grid(far_rows[:, 0].reshape(BLOCKS, C1 * 64), 0, -1)
    into_xlow = shift_grid(far_rows[:, 1].reshape(BLOCKS, C1 * 64), 0, 1)
    into_yhigh = shift_grid(far_rows[:, 2].reshape(BLOCKS, C1 * 64), 1, -1)
    into_ylow = shift_grid(far_rows[:, 3].reshape(BLOCKS, C1 * 64), 1, 1)

    def final_one(items):
        grad_volume, part_a, part_b, part_c, part_d, active_rows = items
        total = add_faces(grad_volume, part_a, part_b, part_c, part_d).reshape(NB, C1, 512)
        total = to_patches(total).reshape(NB, C1, 512)
        return jnp.where(active_rows[:, None, None], total, 0.0).astype(jnp.bfloat16)
    features_grad = lax.map(final_one, (near_grad, per_device(into_xhigh), per_device(into_xlow), per_device(into_yhigh), per_device(into_ylow), per_device(active)))
    scale = float(BLOCKS) ** (-0.5)
    return (latent.reshape(CBLOCKS, 512, C2), features_grad.reshape(BLOCKS, C1, 512), lax.optimization_barrier(jnp.sum(conv_parts, axis=0)) * scale, lax.optimization_barrier(jnp.sum(down_parts, axis=0)) * scale, lax.optimization_barrier(jnp.sum(head_parts, axis=0)) * scale)
```

```python
import jax
import jax.numpy as jnp
import numpy as np
from jax import lax
from jax.experimental import pallas as pl
from jax.experimental.pallas import tpu as pltpu
from jax.sharding import PartitionSpec as P

BF = jnp.bfloat16
F32 = jnp.float32
C = 64
SLOTS = 8
LIMIT = 48 * 1024 * 1024
NT = (((1,), (1,)), ((), ()))


def tables():
    lane = np.arange(128)
    r, a, b, c = lane // 64, lane // 16 % 4, lane // 4 % 4, lane % 4

    def one_hot(source, count):
        out = np.zeros((count, source.size), np.float32)
        out[source, np.arange(source.size)] = 1
        return out

    def at(r, a, b, c):
        return r * 64 + a % 4 * 16 + b % 4 * 4 + c % 4

    x_minus = one_hot(at(r, a - 1, b, c), 128)
    x_plus = one_hot(at(r, a + 1, b, c), 128)
    y_minus = one_hot(at(r, a, b - 1, c), 128)
    y_plus = one_hot(at(r, a, b + 1, c), 128)
    z_minus = one_hot(at(1 - r, a, b, c - (r == 0)), 128)
    z_plus = one_hot(at(1 - r, a, b, c + (r == 1)), 128)
    turn_z = np.concatenate([z_minus, z_plus], 1)
    turn_xy = np.stack(
        [
            np.concatenate([(x_plus, x_minus)[k // 2], (y_plus, y_minus)[k % 2]], 1)
            for k in range(4)
        ]
    )
    wide = np.arange(256)
    half = wide // 128
    r, a, b, c = wide // 64 % 2, wide // 16 % 4, wide // 4 % 4, wide % 4
    spread_x = one_hot(half * 32 + r * 16 + b * 4 + c, 64)
    spread_y = one_hot(half * 32 + r * 16 + a * 4 + c, 64)

    def folded(spread):
        zero = np.zeros_like(spread)
        return np.concatenate(
            [np.concatenate([spread, zero], 0), np.concatenate([zero, spread], 0)], 1
        )

    packs = []
    for spread, place, want in ((spread_x, a, 3), (spread_x, a, 0), (spread_y, b, 3), (spread_y, b, 0)):
        pack = (spread * (place == want)).T
        packs.append(np.concatenate([pack, pack], 1))
    index = np.arange(512)
    regroup = np.zeros((512, 512), np.float32)
    regroup[index, index % 64 * 8 + index // 64] = 1
    return [
        np.asarray(t, BF)
        for t in (
            turn_z,
            turn_xy,
            np.stack([folded(spread_x), folded(spread_y)]),
            np.stack(packs),
            regroup,
        )
    ]


def dot(left, right, dims=None):
    if dims is None:
        return jnp.dot(left, right, preferred_element_type=F32)
    return lax.dot_general(left, right, dims, preferred_element_type=F32)


def lane_of(shape):
    return lax.broadcasted_iota(jnp.int32, shape, len(shape) - 1)


def parts(block, direction):
    if direction == 0:
        return block[:, 256:512]
    if direction == 1:
        return block[:, 0:256]
    first = 128 if direction == 2 else 0
    return jnp.concatenate([block[:, first : first + 128], block[:, first + 256 : first + 384]], 1)


def roll_blocks(source, turn_z, turn_xy, pool, pool_z):
    for k in range(4):
        chunk = source[:, k * 128 : (k + 1) * 128]
        moved = dot(chunk, turn_xy[k]).astype(BF).reshape(SLOTS, C, 256)
        x_dir, y_dir = 1 - k // 2, 3 - k % 2
        x_at, y_at = k % 2 * 128, k // 2 * 128
        pool[x_dir, 0:SLOTS, :, x_at : x_at + 128] = moved[:, :, 0:128]
        pool[y_dir, 0:SLOTS, :, y_at : y_at + 128] = moved[:, :, 128:256]
        moved = dot(chunk, turn_z[...]).astype(BF).reshape(SLOTS, C, 256)
        pool_z[0, 0:SLOTS, :, k * 128 : (k + 1) * 128] = moved[:, :, 0:128]
        pool_z[1, 0:SLOTS, :, k * 128 : (k + 1) * 128] = moved[:, :, 128:256]


def rim_masks():
    lane = lane_of((C, 256))
    a, b = lane // 16 % 4, lane // 4 % 4
    masks = [a == 0, a == 3, b == 0, b == 3]
    lane = lane_of((C, 512))
    r, c = lane // 64 % 2, lane % 4
    return masks, [(r == 0) & (c == 0), (r == 1) & (c == 3)]


def weave(direction, moved, block):
    if direction == 0:
        return [moved[:, 0:128], moved[:, 128:256], block[:, 0:128], block[:, 128:256]]
    if direction == 1:
        return [block[:, 256:384], block[:, 384:512], moved[:, 0:128], moved[:, 128:256]]
    if direction == 2:
        return [moved[:, 0:128], block[:, 0:128], moved[:, 128:256], block[:, 256:384]]
    return [block[:, 128:256], moved[:, 0:128], block[:, 384:512], moved[:, 128:256]]


def parities():
    return lax.rem(lax.axis_index("gx"), 2), lax.rem(lax.axis_index("gy"), 2)


def pack_kernel(counts, cmap, x_ref, lat_ref, pack_ref, send_xa, send_xb, send_ya, send_yb):
    px, py = parities()
    masked = jnp.concatenate(
        [
            jnp.where(b < counts[0], x_ref[b * C : (b + 1) * C, :], jnp.zeros((C, 512), BF))
            for b in range(SLOTS)
        ],
        0,
    )
    low = lane_of((256, 128)) < 64
    faces = []
    for d in range(4):
        packed = dot(parts(masked, d), pack_ref[d])
        faces.append(jnp.where(low, packed[0:256], packed[256:512]))
    even = px == 0
    send_xa[0:256, :] = jnp.where(even, faces[0], faces[1]).astype(BF)
    send_xb[...] = jnp.where(even, faces[1], faces[0]).astype(BF)
    even = py == 0
    send_ya[0:256, :] = jnp.where(even, faces[2], faces[3]).astype(BF)
    send_yb[...] = jnp.where(even, faces[3], faces[2]).astype(BF)
    row = lax.broadcasted_iota(jnp.int32, (16, 128), 0)
    named = jnp.zeros((16, 128), jnp.int32)
    for k in range(8):
        named = jnp.where(row == k, cmap[0, k], named)
    named = named.astype(F32).astype(BF)
    lat = lat_ref[...]
    send_xa[256:768, :] = lat
    send_ya[256:768, :] = lat
    send_xa[768:784, :] = named
    send_ya[768:784, :] = named


def main_kernel(
    counts, nb, cmap,
    x_ref, lat_ref, got_xa, got_xb, got_ya, got_yb, got_xy,
    conv_ref, down_ref, head_ref, turn_z, turn_xy, spread, pack, regroup,
    hg_ref, sums_ref, send_xa, send_xb, send_ya, send_yb,
    xm, pool, pool_z, taps, slope, act2, routed, far, maps_v, maps_s, sem,
):
    px, py = parities()
    for j, got in enumerate((got_xa, got_ya)):
        maps_v[j] = got[768:784, :].astype(F32).astype(jnp.int32)
    maps_v[2] = got_xy[512:528, :].astype(F32).astype(jnp.int32)
    copy = pltpu.make_async_copy(maps_v, maps_s, sem)
    copy.start()

    for b in range(SLOTS):
        rows = slice(b * C, (b + 1) * C)
        xm[rows, :] = jnp.where(b < counts[0], x_ref[rows, :], jnp.zeros((C, 512), BF))
    roll_blocks(xm, turn_z, turn_xy, pool, pool_z)
    for got, axis, direction in (
        (got_xa, 0, 1 - px), (got_xb, 0, px), (got_ya, 1, 3 - py), (got_yb, 1, 2 + py),
    ):
        wide = dot(got[0:256, :], spread[axis]).astype(BF).reshape(4, C, 512)
        pool[direction, 8:12] = wide[:, :, 0:256]
        pool[direction, 12:16] = wide[:, :, 256:512]
    for d in range(4):
        pool[d, 16] = jnp.zeros((C, 256), BF)
    for d in range(2):
        pool_z[d, 8] = jnp.zeros((C, 512), BF)

    masks, masks_z = rim_masks()
    low = lane_of((C, 128)) < 64
    conv = conv_ref[...]
    for pair in range(SLOTS // 2):
        acts = []
        for b in (2 * pair, 2 * pair + 1):
            block = xm[b * C : (b + 1) * C, :]
            taps[b, 0:C, :] = block
            for d in range(4):
                moved = jnp.where(masks[d], pool[d, nb[b, d]], pool[d, b])
                for k, piece in enumerate(weave(d, moved, block)):
                    taps[b, (d + 1) * C : (d + 2) * C, k * 128 : (k + 1) * 128] = piece
            for d in range(2):
                near = jnp.minimum(nb[b, d + 4], SLOTS)
                taps[b, (d + 5) * C : (d + 6) * C, :] = jnp.where(
                    masks_z[d], pool_z[d, near], pool_z[d, b]
                )
            hidden = dot(conv, taps[b])
            gate = 0.5 * jnp.tanh(0.5 * hidden) + 0.5
            slope[b] = gate * (1.0 + hidden * (1.0 - gate))
            acts.append(hidden * gate)
        lanes = slice(pair * 128, (pair + 1) * 128)
        for k in range(4):
            one, two = (v[:, k * 128 : (k + 1) * 128] for v in acts)
            first = jnp.where(low, one, pltpu.roll(two, 64, 1))
            second = jnp.where(low, pltpu.roll(one, 64, 1), two)
            act2[2 * k * C : (2 * k + 1) * C, lanes] = first.astype(BF)
            act2[(2 * k + 1) * C : (2 * k + 2) * C, lanes] = second.astype(BF)

    down = dot(down_ref[...], regroup[...], NT).astype(BF)
    down_back = dot(regroup[...], down_ref[...], NT).astype(BF)
    octants = dot(down, act2[...]).astype(BF).astype(F32)
    gate = 0.5 * jnp.tanh(0.5 * octants) + 0.5
    oct_act = (octants * gate).astype(BF)
    oct_slope = gate * (1.0 + octants * (1.0 - gate))
    projected = dot(head_ref[...], oct_act).T.astype(BF)
    send_xa[256:768, :] = projected
    send_ya[256:768, :] = projected

    copy.wait()
    for s in range(SLOTS):
        routed[s] = jnp.zeros((C, 128), BF)
    for j, (got, start) in enumerate(((lat_ref, 0), (got_xa, 256), (got_ya, 256), (got_xy, 0))):
        for k in range(8):
            name = cmap[0, k] if j == 0 else maps_s[j - 1, k, 0]
            name = name - j * SLOTS
            name = jnp.where((name >= 0) & (name < SLOTS), name, SLOTS)
            routed[name] = got[start + k * C : start + (k + 1) * C, :]
    grad = routed[0:SLOTS].reshape(SLOTS * C, 128)
    head_back = head_ref[...].astype(F32).T.astype(BF)
    oct_grad = (dot(head_back, grad, NT) * oct_slope).astype(BF)
    sums_ref[768:896, :] = dot(oct_act, grad).T
    down_sum = dot(oct_grad, act2[...], NT)
    for k in range(4):
        sums_ref[256 + k * 128 : 256 + (k + 1) * 128, :] = down_sum[:, k * 128 : (k + 1) * 128]
    conv_sum = jnp.zeros((C, 448), F32)
    for pair in range(SLOTS // 2):
        patch = dot(down_back, oct_grad[:, pair * 128 : (pair + 1) * 128])
        for side in range(2):
            b = 2 * pair + side
            for k in range(4):
                first = patch[2 * k * C : (2 * k + 1) * C]
                second = patch[(2 * k + 1) * C : (2 * k + 2) * C]
                if side == 0:
                    both = jnp.where(low, first, pltpu.roll(second, 64, 1))
                else:
                    both = jnp.where(low, pltpu.roll(first, 64, 1), second)
                lanes = slice(k * 128, (k + 1) * 128)
                hg_ref[b * C : (b + 1) * C, lanes] = (both * slope[b, :, lanes]).astype(BF)
            conv_sum = conv_sum + dot(hg_ref[b * C : (b + 1) * C, :], taps[b], NT)
    for k in range(3):
        sums_ref[k * C : (k + 1) * C, :] = conv_sum[:, k * 128 : (k + 1) * 128]
    sums_ref[3 * C : 4 * C, 0:C] = conv_sum[:, 384:448]
    sums_ref[3 * C : 4 * C, C:128] = jnp.zeros((C, C), F32)

    for d in range(4):
        for s in range(5):
            far[d, s] = jnp.zeros((C, 128), F32)
    high = lane_of((C, 128)) // 64
    for d in range(4):
        face = dot(parts(hg_ref[...], d ^ 1), pack[d ^ 1])
        for b in range(SLOTS):
            name = nb[b, d] - SLOTS
            away = (name >= 0) & (name < SLOTS)
            row = jnp.where(away, lax.rem(name, 4), 4)
            side = jnp.where(name >= 4, 1, 0)
            far[d, row] += jnp.where(high == side, face[b * C : (b + 1) * C, :], 0.0)
    send_xa[0:256, :] = far[1 - px, 0:4].reshape(256, 128).astype(BF)
    send_xb[...] = far[px, 0:4].reshape(256, 128).astype(BF)
    send_ya[0:256, :] = far[3 - py, 0:4].reshape(256, 128).astype(BF)
    send_yb[...] = far[2 + py, 0:4].reshape(256, 128).astype(BF)


def last_kernel(
    counts, nb,
    hg_ref, got_xa, got_xb, got_ya, got_yb, conv_ref, turn_z, turn_xy, spread,
    out_ref,
    pool, pool_z, total, total_z, fields,
):
    px, py = parities()
    roll_blocks(hg_ref, turn_z, turn_xy, pool, pool_z)
    for got, axis, direction in (
        (got_xa, 0, px), (got_xb, 0, 1 - px), (got_ya, 1, 2 + py), (got_yb, 1, 3 - py),
    ):
        wide = dot(got[0:256, :], spread[axis]).reshape(4, C, 512)
        total[direction, 0:4] = wide[:, :, 0:256]
        total[direction, 4:8] = wide[:, :, 256:512]
    for d in range(2):
        for s in range(SLOTS):
            total_z[d, s] = jnp.zeros((C, 512), F32)
    for b in range(SLOTS):
        for d in range(4):
            near = jnp.minimum(nb[b, d], SLOTS)
            total[d, near] += pool[d ^ 1, b].astype(F32)
        for d in range(2):
            near = jnp.minimum(nb[b, d + 4], SLOTS)
            total_z[d, near] += pool_z[1 - d, b].astype(F32)
    masks, masks_z = rim_masks()
    conv = conv_ref[...]
    for b in range(SLOTS):
        block = hg_ref[b * C : (b + 1) * C, :]
        fields[0:C, :] = block
        for d in range(4):
            moved = jnp.where(masks[d ^ 1], total[d, b].astype(BF), pool[d ^ 1, b])
            for k, piece in enumerate(weave(d ^ 1, moved, block)):
                fields[(d + 1) * C : (d + 2) * C, k * 128 : (k + 1) * 128] = piece
        for d in range(2):
            fields[(d + 5) * C : (d + 6) * C, :] = jnp.where(
                masks_z[1 - d], total_z[d, b].astype(BF), pool_z[1 - d, b]
            )
        near = dot(conv, fields[...])
        out_ref[b * C : (b + 1) * C, :] = jnp.where(b < counts[0], near, 0.0).astype(BF)


def latent_kernel(cmap, own, got_xa, got_ya, got_xy, out_ref, rows):
    rows[0:8] = own[256:768, :].reshape(8, C, 128)
    rows[8:16] = got_xa[256:768, :].reshape(8, C, 128)
    rows[16:24] = got_ya[256:768, :].reshape(8, C, 128)
    rows[24:32] = got_xy[...].reshape(8, C, 128)
    rows[32] = jnp.zeros((C, 128), BF)
    for k in range(8):
        out_ref[k * C : (k + 1) * C, :] = rows[cmap[0, k]]


def scale_kernel(scale, conv_in, regroup, conv_out, down_out, head_out):
    for k in range(3):
        conv_out[:, k * 128 : (k + 1) * 128] = conv_in[k * C : (k + 1) * C, :].astype(F32) * scale
    conv_out[:, 384:448] = conv_in[3 * C : 4 * C, 0:C].astype(F32) * scale
    down = jnp.concatenate([conv_in[256 + k * 128 : 384 + k * 128, :] for k in range(4)], 1)
    down_out[...] = dot(down, regroup[...]) * scale
    head_out[...] = conv_in[768:896, :].astype(F32) * scale


def swap(value, axis, bit):
    count = lax.axis_size(axis)
    return lax.ppermute(value, axis, [(i, i ^ bit) for i in range(count)])


def swap_odd(value, axis):
    count = lax.axis_size(axis)
    route = []
    for low in range(1, count - 1, 2):
        route += [(low, low + 1), (low + 1, low)]
    return lax.ppermute(value, axis, route)


def total_of(sums):
    rows = sums.shape[0] // 2
    bit = lax.rem(lax.axis_index("gy"), 2)
    mine = lax.dynamic_slice_in_dim(sums, bit * rows, rows)
    other = lax.dynamic_slice_in_dim(sums, (1 - bit) * rows, rows)
    mine = mine + swap(other.astype(BF), "gy", 1).astype(F32)
    for axis, first in (("gy", 2), ("gx", 1)):
        step = first
        while step < lax.axis_size(axis):
            mine = mine + swap(mine.astype(BF), axis, step).astype(F32)
            step *= 2
    mine = mine.astype(BF)
    theirs = swap(mine, "gy", 1)
    return jnp.where(
        bit == 0, jnp.concatenate([mine, theirs]), jnp.concatenate([theirs, mine])
    )


def call(kernel, outs, ins, scalars=0, scratch=()):
    smem = pl.BlockSpec(memory_space=pltpu.SMEM)
    vmem = pl.BlockSpec(memory_space=pltpu.VMEM)
    return pl.pallas_call(
        kernel,
        out_shape=[jax.ShapeDtypeStruct(shape, kind) for shape, kind in outs],
        in_specs=[smem] * scalars + [vmem] * (len(ins) - scalars),
        out_specs=[vmem] * len(outs),
        scratch_shapes=list(scratch),
        compiler_params=pltpu.CompilerParams(vmem_limit_bytes=LIMIT),
    )(*ins)


def body(
    features, neighbours, counts, conv_weight, down_weight, head_weight, coarse_map, latent_grad
):
    turn_z, turn_xy, spread, pack, regroup = (jnp.asarray(t) for t in tables())
    flat = features.reshape(SLOTS * C, 512)
    lat = latent_grad.reshape(512, 128)
    send_xa, send_xb, send_ya, send_yb = call(
        pack_kernel,
        [((784, 128), BF), ((256, 128), BF), ((784, 128), BF), ((256, 128), BF)],
        (counts, coarse_map, flat, lat, pack),
        2,
    )
    got_xa = swap(send_xa, "gx", 1)
    got_xb = swap_odd(send_xb, "gx")
    got_yb = swap_odd(send_yb, "gy")
    got_ya = swap(send_ya, "gy", 1)
    got_xy = swap(got_xa[256:784], "gy", 1)
    hg, sums, send_xa, send_xb, send_ya, send_yb = call(
        main_kernel,
        [
            ((512, 512), BF), ((896, 128), F32),
            ((768, 128), BF), ((256, 128), BF), ((768, 128), BF), ((256, 128), BF),
        ],
        (
            counts, neighbours, coarse_map, flat, lat, got_xa, got_xb, got_ya, got_yb, got_xy,
            conv_weight, down_weight, head_weight, turn_z, turn_xy, spread, pack, regroup,
        ),
        3,
        [
            pltpu.VMEM((512, 512), BF),
            pltpu.VMEM((4, 17, C, 256), BF),
            pltpu.VMEM((2, 9, C, 512), BF),
            pltpu.VMEM((SLOTS, 448, 512), BF),
            pltpu.VMEM((SLOTS, C, 512), F32),
            pltpu.VMEM((512, 512), BF),
            pltpu.VMEM((SLOTS + 1, C, 128), BF),
            pltpu.VMEM((4, 5, C, 128), F32),
            pltpu.VMEM((3, 16, 128), jnp.int32),
            pltpu.SMEM((3, 16, 128), jnp.int32),
            pltpu.SemaphoreType.DMA,
        ],
    )
    own = send_xa
    got_xa = swap(send_xa, "gx", 1)
    got_xb = swap_odd(send_xb, "gx")
    got_yb = swap_odd(send_yb, "gy")
    got_ya = swap(send_ya, "gy", 1)
    got_xy = swap(got_xa[256:768], "gy", 1)
    summed = total_of(sums)
    conv_back = conv_weight.reshape(C, 7, C).transpose(2, 1, 0).reshape(C, 448)
    (grad,) = call(
        last_kernel,
        [((512, 512), BF)],
        (counts, neighbours, hg, got_xa, got_xb, got_ya, got_yb, conv_back, turn_z, turn_xy, spread),
        2,
        [
            pltpu.VMEM((4, 8, C, 256), BF),
            pltpu.VMEM((2, 8, C, 512), BF),
            pltpu.VMEM((4, 9, C, 256), F32),
            pltpu.VMEM((2, 9, C, 512), F32),
            pltpu.VMEM((448, 512), BF),
        ],
    )
    (latent,) = call(
        latent_kernel,
        [((512, 128), BF)],
        (coarse_map, own, got_xa, got_ya, got_xy),
        1,
        [pltpu.VMEM((33, C, 128), BF)],
    )
    scale = float(SLOTS * lax.axis_size("gx") * lax.axis_size("gy")) ** (-0.5)
    conv_grad, down_grad, head_grad = call(
        lambda *refs: scale_kernel(scale, *refs),
        [((C, 448), F32), ((128, 512), F32), ((128, 128), F32)],
        (summed, regroup),
    )
    return (
        latent.reshape(1, 512, 128), grad.reshape(SLOTS, C, 512), conv_grad, down_grad, head_grad,
    )


def solution(mesh):
    both = ("gx", "gy")
    placed = (
        P(both, None, None), P(both, None), P(both), P(), P(), P(), P(both, None),
        P(both, None, None),
    )
    return jax.shard_map(
        body,
        mesh=mesh,
        in_specs=placed,
        out_specs=(P(both, None, None), P(both, None, None), P(), P(), P()),
        check_vma=False,
    )
```

```python
import jax
import jax.numpy as jnp
from jax import lax
from jax.experimental import pallas as pl
from jax.experimental.pallas import tpu as pltpu
from jax.sharding import PartitionSpec as P

BF = jnp.bfloat16
F32 = jnp.float32
C = 64
SLOTS = 8
NT = (((1,), (1,)), ((), ()))
TN = (((0,), (0,)), ((), ()))


def one_hot(source, rows):
    row = lax.broadcasted_iota(jnp.int32, (rows, source.shape[1]), 0)
    return jnp.where(row == source, 1.0, 0.0).astype(BF)


def lanes_of(count):
    lane = lax.broadcasted_iota(jnp.int32, (1, count), 1)
    return lane, lane // 64 % 2, lane // 16 % 4, lane // 4 % 4, lane % 4


def cell(r, a, b, c):
    return r * 64 + (a + 4) % 4 * 16 + (b + 4) % 4 * 4 + (c + 4) % 4


def turn_z():
    lane, r, a, b, c = lanes_of(256)
    step = jnp.where(lane < 128, jnp.where(r == 0, -1, 0), jnp.where(r == 1, 1, 0))
    return one_hot(cell(1 - r, a, b, c + step), 128)


def turn_xy(k):
    lane, r, a, b, c = lanes_of(256)
    x = 1 - 2 * (k // 2)
    y = 1 - 2 * (k % 2)
    first = lane < 128
    return one_hot(cell(r, a + jnp.where(first, x, 0), b + jnp.where(first, 0, y), c), 128)


def spread(axis, want=None):
    lane, r, a, b, c = lanes_of(512)
    place, other = (a, b) if axis == 0 else (b, a)
    source = lane // 256 * 64 + lane // 128 % 2 * 32 + r * 16 + other * 4 + c
    if want is not None:
        source = jnp.where(place == want, source, -1)
    return one_hot(source, 128)


def pack(direction):
    lane = lanes_of(128)[0] % 64
    want = 3 * (1 - direction % 2)
    half, r, other, c = lane // 32, lane // 16 % 2, lane // 4 % 4, lane % 4
    a, b = (want, other) if direction < 2 else (other, want)
    return one_hot(half * 128 + cell(r, a, b, c), 256)


def regroup():
    lane = lanes_of(512)[0]
    return one_hot(lane % 8 * 64 + lane // 8, 512)


CONV, DOWN, DOWN_BACK, POOL, POOL_Z, STORE = 0, 64, 192, 704, 1728, 2880


def pool_at(store, d, slot):
    rows = pl.ds(pl.multiple_of(POOL + (d // 2 * SLOTS + slot) * C, C), C)
    return store[rows, d % 2 * 256 : d % 2 * 256 + 256]


def pool_z_at(store, d, slot):
    return store[pl.ds(pl.multiple_of(POOL_Z + (d * 9 + slot) * C, C), C), :]


def dot(left, right, dims=None):
    if dims is None:
        return jnp.dot(left, right, preferred_element_type=F32)
    return lax.dot_general(left, right, dims, preferred_element_type=F32)


def lane_of(shape):
    return lax.broadcasted_iota(jnp.int32, shape, len(shape) - 1)


def parts(block, direction):
    if direction == 0:
        return block[:, 256:512]
    if direction == 1:
        return block[:, 0:256]
    first = 128 if direction == 2 else 0
    return jnp.concatenate([block[:, first : first + 128], block[:, first + 256 : first + 384]], 1)


def roll_blocks(source, put, put_z):
    up = turn_z()
    for k in range(4):
        chunk = source[:, k * 128 : (k + 1) * 128]
        moved = dot(chunk, turn_xy(k)).astype(BF)
        x_dir, y_dir = 1 - k // 2, 3 - k % 2
        put(x_dir, k % 2 * 128, moved[:, 0:128])
        put(y_dir, k // 2 * 128, moved[:, 128:256])
        moved = dot(chunk, up).astype(BF)
        put_z(0, k * 128, moved[:, 0:128])
        put_z(1, k * 128, moved[:, 128:256])


def rim_masks():
    lane = lane_of((C, 256))
    a, b = lane // 16 % 4, lane // 4 % 4
    masks = [a == 0, a == 3, b == 0, b == 3]
    lane = lane_of((C, 512))
    r, c = lane // 64 % 2, lane % 4
    return masks, [(r == 0) & (c == 0), (r == 1) & (c == 3)]


def weave(direction, moved, block):
    if direction == 0:
        return [moved[:, 0:128], moved[:, 128:256], block[:, 0:128], block[:, 128:256]]
    if direction == 1:
        return [block[:, 256:384], block[:, 384:512], moved[:, 0:128], moved[:, 128:256]]
    if direction == 2:
        return [moved[:, 0:128], block[:, 0:128], moved[:, 128:256], block[:, 256:384]]
    return [block[:, 128:256], moved[:, 0:128], block[:, 384:512], moved[:, 128:256]]


def parities():
    return lax.rem(lax.axis_index("gx"), 2), lax.rem(lax.axis_index("gy"), 2)


def load(pairs, sems):
    copies = [pltpu.make_async_copy(src, dst, sems.at[i]) for i, (src, dst) in enumerate(pairs)]
    for copy in copies:
        copy.start()
    return copies


def pack_kernel(
    counts, cmap_hbm, x_hbm, lat_hbm,
    xm, send_xa, send_xb, send_ya, send_yb,
    cmap, sems,
):
    copies = load(
        [
            (cmap_hbm, cmap), (x_hbm, xm),
            (lat_hbm, send_xa.at[256:768]), (lat_hbm, send_ya.at[256:768]),
        ],
        sems,
    )
    px, py = parities()
    packs = [pack(d) for d in range(4)]
    for copy in copies[:2]:
        copy.wait()
    for b in range(1, SLOTS):
        @pl.when(b >= counts[0])
        def _():
            xm[b * C : (b + 1) * C, :] = jnp.zeros((C, 512), BF)
    masked = xm[...]
    low = lane_of((256, 128)) < 64
    faces = []
    for d in range(4):
        packed = dot(parts(masked, d), packs[d])
        faces.append(jnp.where(low, packed[0:256], packed[256:512]))
    even = px == 0
    send_xa[0:256, :] = jnp.where(even, faces[0], faces[1]).astype(BF)
    send_xb[...] = jnp.where(even, faces[1], faces[0]).astype(BF)
    even = py == 0
    send_ya[0:256, :] = jnp.where(even, faces[2], faces[3]).astype(BF)
    send_yb[...] = jnp.where(even, faces[3], faces[2]).astype(BF)
    row = lax.broadcasted_iota(jnp.int32, (16, 128), 0)
    named = jnp.zeros((16, 128), jnp.int32)
    for k in range(8):
        named = jnp.where(row == k, cmap[0, k], named)
    named = named.astype(F32).astype(BF)
    send_xa[768:784, :] = named
    send_ya[768:784, :] = named
    for copy in copies[2:]:
        copy.wait()


def prep_kernel(xm, conv_hbm, down_hbm, head_hbm, store, conv, sems):
    copies = load(
        [
            (down_hbm, store.at[DOWN : DOWN + 128]),
            (conv_hbm, conv),
            (head_hbm, store.at[DOWN_BACK : DOWN_BACK + 128, 128:256]),
        ],
        sems,
    )
    for d in range(2):
        start = POOL_Z + (d * 9 + SLOTS) * C
        store[start : start + C, :] = jnp.zeros((C, 512), BF)

    def put(d, lane, value):
        rows = slice(POOL + d // 2 * 512, POOL + d // 2 * 512 + 512)
        store[rows, d % 2 * 256 + lane : d % 2 * 256 + lane + 128] = value

    def put_z(d, lane, value):
        start = POOL_Z + d * 9 * C
        store[start : start + 512, lane : lane + 128] = value

    roll_blocks(xm, put, put_z)
    copies[0].wait()
    down = store[DOWN : DOWN + 128, :]
    table = regroup()
    store[DOWN : DOWN + 128, :] = dot(down, table, NT).astype(BF)
    store[DOWN_BACK : DOWN_BACK + 512, 0:128] = dot(table, down, NT).astype(BF)
    copies[1].wait()
    store[CONV : CONV + C, 0:448] = conv[...]
    copies[2].wait()


YA, OCT, XA, XB, YB, SEND = 0, 256, 768, 1024, 1280, 1536


def main_kernel(
    nb, cmap, lat_hbm,
    xm, got_xa, got_xb, got_ya, got_yb, got_xy, store,
    hg_ref, mine_ref, other_ref, send,
    sums_ref, lat_ref, lat_sem, reach, taps, slope, act2, routed, far, maps_v, maps_s, sem,
):
    px, py = parities()
    for j, got in enumerate((got_xa, got_ya)):
        maps_v[j] = got[768:784, :].astype(F32).astype(jnp.int32)
    maps_v[2] = got_xy[512:528, :].astype(F32).astype(jnp.int32)
    copy = pltpu.make_async_copy(maps_v, maps_s, sem)
    copy.start()
    lat_copy = pltpu.make_async_copy(lat_hbm, lat_ref, lat_sem)
    lat_copy.start()
    head = store[DOWN_BACK : DOWN_BACK + 128, 128:256]

    spreads = [spread(axis) for axis in range(2)]
    for got, axis, direction in (
        (got_xa, 0, 1 - px), (got_xb, 0, px), (got_ya, 1, 3 - py), (got_yb, 1, 2 + py),
    ):
        wide = dot(got[0:256, :], spreads[axis]).astype(BF).reshape(4, C, 512)
        reach[direction, 8:12] = wide[:, :, 0:256]
        reach[direction, 12:16] = wide[:, :, 256:512]
    for d in range(4):
        for b in range(SLOTS):
            reach[d, b] = pool_at(store, d, b)
        reach[d, 16] = jnp.zeros((C, 256), BF)

    masks, masks_z = rim_masks()
    low = lane_of((C, 128)) < 64
    conv = store[CONV : CONV + C, 0:448]
    for pair in range(SLOTS // 2):
        acts = []
        for b in (2 * pair, 2 * pair + 1):
            block = xm[b * C : (b + 1) * C, :]
            taps[b, 0:C, :] = block
            for d in range(4):
                moved = jnp.where(masks[d], reach[d, nb[b, d]], reach[d, b])
                for k, piece in enumerate(weave(d, moved, block)):
                    taps[b, (d + 1) * C : (d + 2) * C, k * 128 : (k + 1) * 128] = piece
            for d in range(2):
                near = jnp.minimum(nb[b, d + 4], SLOTS)
                taps[b, (d + 5) * C : (d + 6) * C, :] = jnp.where(
                    masks_z[d], pool_z_at(store, d, near), pool_z_at(store, d, b)
                )
            hidden = dot(conv, taps[b])
            gate = 0.5 * jnp.tanh(0.5 * hidden) + 0.5
            slope[b] = gate * (1.0 + hidden * (1.0 - gate))
            acts.append(hidden * gate)
        lanes = slice(pair * 128, (pair + 1) * 128)
        for k in range(4):
            one, two = (v[:, k * 128 : (k + 1) * 128] for v in acts)
            first = jnp.where(low, one, pltpu.roll(two, 64, 1))
            second = jnp.where(low, pltpu.roll(one, 64, 1), two)
            act2[2 * k * C : (2 * k + 1) * C, lanes] = first.astype(BF)
            act2[(2 * k + 1) * C : (2 * k + 2) * C, lanes] = second.astype(BF)

    octants = dot(store[DOWN : DOWN + 128, :], act2[...]).astype(BF).astype(F32)
    gate = 0.5 * jnp.tanh(0.5 * octants) + 0.5
    oct_act = (octants * gate).astype(BF)
    oct_slope = gate * (1.0 + octants * (1.0 - gate))
    projected = dot(head, oct_act).T.astype(BF)
    send[OCT : OCT + 512, :] = projected

    copy.wait()
    lat_copy.wait()
    for s in range(SLOTS):
        routed[s] = jnp.zeros((C, 128), BF)
    for j, (got, start) in enumerate(((lat_ref, 0), (got_xa, 256), (got_ya, 256), (got_xy, 0))):
        for k in range(8):
            name = cmap[0, k] if j == 0 else maps_s[j - 1, k, 0]
            name = name - j * SLOTS
            name = jnp.where((name >= 0) & (name < SLOTS), name, SLOTS)
            routed[name] = got[start + k * C : start + (k + 1) * C, :]
    grad = routed[0:SLOTS].reshape(SLOTS * C, 128)
    head_back = head.astype(F32).T.astype(BF)
    oct_grad = (dot(head_back, grad, NT) * oct_slope).astype(BF)
    sums_ref[768:896, :] = dot(oct_act, grad).T
    down_sum = dot(oct_grad, act2[...], NT)
    for k in range(4):
        sums_ref[256 + k * 128 : 256 + (k + 1) * 128, :] = down_sum[:, k * 128 : (k + 1) * 128]
    conv_sum = jnp.zeros((C, 448), F32)
    for pair in range(SLOTS // 2):
        patch = dot(store[DOWN_BACK : DOWN_BACK + 512, 0:128], oct_grad[:, pair * 128 : (pair + 1) * 128])
        for side in range(2):
            b = 2 * pair + side
            for k in range(4):
                first = patch[2 * k * C : (2 * k + 1) * C]
                second = patch[(2 * k + 1) * C : (2 * k + 2) * C]
                if side == 0:
                    both = jnp.where(low, first, pltpu.roll(second, 64, 1))
                else:
                    both = jnp.where(low, pltpu.roll(first, 64, 1), second)
                lanes = slice(k * 128, (k + 1) * 128)
                hg_ref[b * C : (b + 1) * C, lanes] = (both * slope[b, :, lanes]).astype(BF)
            conv_sum = conv_sum + dot(hg_ref[b * C : (b + 1) * C, :], taps[b], NT)
    for k in range(3):
        sums_ref[k * C : (k + 1) * C, :] = conv_sum[:, k * 128 : (k + 1) * 128]
    sums_ref[3 * C : 4 * C, 0:C] = conv_sum[:, 384:448]
    sums_ref[3 * C : 4 * C, C:128] = jnp.zeros((C, C), F32)

    first, second = sums_ref[0:448, :].astype(BF), sums_ref[448:896, :].astype(BF)
    mine_ref[...] = jnp.where(py == 0, first, second)
    other_ref[...] = jnp.where(py == 0, second, first)

    for d in range(4):
        for s in range(5):
            far[d, s] = jnp.zeros((C, 128), F32)
    high = lane_of((C, 128)) // 64
    for d in range(4):
        face = dot(parts(hg_ref[...], d ^ 1), pack(d ^ 1))
        for b in range(SLOTS):
            name = nb[b, d] - SLOTS
            away = (name >= 0) & (name < SLOTS)
            row = jnp.where(away, lax.rem(name, 4), 4)
            side = jnp.where(name >= 4, 1, 0)
            far[d, row] += jnp.where(high == side, face[b * C : (b + 1) * C, :], 0.0)
    for at, d in ((XA, 1 - px), (XB, px), (YA, 3 - py), (YB, 2 + py)):
        send[at : at + 256, :] = far[d, 0:4].reshape(256, 128).astype(BF)


def roll_kernel(nb, hg_ref, moved_ref, pool, pool_z, total, total_z):
    def put(d, lane, value):
        pool[d, :, :, lane : lane + 128] = value.reshape(SLOTS, C, 128)

    def put_z(d, lane, value):
        pool_z[d, :, :, lane : lane + 128] = value.reshape(SLOTS, C, 128)

    roll_blocks(hg_ref, put, put_z)
    for s in range(SLOTS):
        for d in range(4):
            total[d, s] = jnp.zeros((C, 256), F32)
        for d in range(2):
            total_z[d, s] = jnp.zeros((C, 512), F32)
    for b in range(SLOTS):
        for d in range(4):
            slot = jnp.minimum(nb[b, d], SLOTS)
            total[d, slot] += pool[d ^ 1, b].astype(F32)
        for d in range(2):
            slot = jnp.minimum(nb[b, d + 4], SLOTS)
            total_z[d, slot] += pool_z[1 - d, b].astype(F32)
    masks, masks_z = rim_masks()
    for b in range(SLOTS):
        for d in range(4):
            rows = slice((d // 2 * SLOTS + b) * C, (d // 2 * SLOTS + b + 1) * C)
            moved_ref[rows, d % 2 * 256 : d % 2 * 256 + 256] = jnp.where(
                masks[d ^ 1], total[d, b].astype(BF), pool[d ^ 1, b]
            )
        for d in range(2):
            rows = slice(((d + 2) * SLOTS + b) * C, ((d + 2) * SLOTS + b + 1) * C)
            moved_ref[rows, :] = jnp.where(
                masks_z[1 - d], total_z[d, b].astype(BF), pool_z[1 - d, b]
            )


def near_kernel(hg_ref, moved_ref, conv_ref, near_ref, fields):
    conv = jnp.concatenate([conv_ref[:, d * C : (d + 1) * C] for d in range(7)], 0)
    for b in range(SLOTS):
        block = hg_ref[b * C : (b + 1) * C, :]
        fields[0:C, :] = block
        for d in range(4):
            rows = slice((d // 2 * SLOTS + b) * C, (d // 2 * SLOTS + b + 1) * C)
            moved = moved_ref[rows, d % 2 * 256 : d % 2 * 256 + 256]
            for k, piece in enumerate(weave(d ^ 1, moved, block)):
                fields[(d + 1) * C : (d + 2) * C, k * 128 : (k + 1) * 128] = piece
        for d in range(2):
            rows = slice(((d + 2) * SLOTS + b) * C, ((d + 2) * SLOTS + b + 1) * C)
            fields[(d + 5) * C : (d + 6) * C, :] = moved_ref[rows, :]
        near_ref[b * C : (b + 1) * C, :] = dot(conv, fields[...], TN)


def far_kernel(counts, near_ref, got_xa, got_xb, got_ya, got_yb, conv_ref, out_ref, rows):
    px, py = parities()
    for got, direction in ((got_xa, px), (got_xb, 1 - px), (got_ya, 2 + py), (got_yb, 3 - py)):
        rows[direction] = got[0:256, :]
    fields = []
    for d in range(4):
        conv = conv_ref[:, (d + 1) * C : (d + 2) * C]
        moved = [dot(conv, rows[d, k * C : (k + 1) * C, :], TN).astype(BF) for k in range(4)]
        table = spread(d // 2, 3 * (1 - d % 2))
        fields.append(dot(jnp.concatenate(moved, 0), table))
    for b in range(SLOTS):
        x_low, x_high, y_low, y_high = (
            fields[d][b % 4 * C : (b % 4 + 1) * C, b // 4 * 256 : b // 4 * 256 + 256]
            for d in (1, 0, 3, 2)
        )
        for k in range(4):
            lanes = slice(k * 128, (k + 1) * 128)
            x, y = (x_low, x_high)[k // 2], (y_low, y_high)[k % 2]
            x, y = (v[:, i * 128 : (i + 1) * 128] for v, i in ((x, k % 2), (y, k // 2)))
            grad = near_ref[b * C : (b + 1) * C, lanes] + (x + y)
            out_ref[b * C : (b + 1) * C, lanes] = jnp.where(b < counts[0], grad, 0.0).astype(BF)


def latent_kernel(cmap, own, got_x, got_ya, got_xy, out_ref, rows):
    rows[0:8] = own[OCT : OCT + 512, :].reshape(8, C, 128)
    rows[8:16] = got_x[...].reshape(8, C, 128)
    rows[16:24] = got_ya[256:768, :].reshape(8, C, 128)
    rows[24:32] = got_xy[...].reshape(8, C, 128)
    rows[32] = jnp.zeros((C, 128), BF)
    for k in range(8):
        out_ref[k * C : (k + 1) * C, :] = rows[cmap[0, k]]


def scale_kernel(scale, conv_in, conv_out, down_out, head_out):
    for k in range(3):
        conv_out[:, k * 128 : (k + 1) * 128] = conv_in[k * C : (k + 1) * C, :].astype(F32) * scale
    conv_out[:, 384:448] = conv_in[3 * C : 4 * C, 0:C].astype(F32) * scale
    down = jnp.concatenate([conv_in[256 + k * 128 : 384 + k * 128, :] for k in range(4)], 1)
    down_out[...] = dot(down, regroup()) * scale
    head_out[...] = conv_in[768:896, :].astype(F32) * scale


def swap(value, axis, bit):
    count = lax.axis_size(axis)
    return lax.ppermute(value, axis, [(i, i ^ bit) for i in range(count)])


def swap_odd(value, axis):
    count = lax.axis_size(axis)
    route = []
    for low in range(1, count - 1, 2):
        route += [(low, low + 1), (low + 1, low)]
    return lax.ppermute(value, axis, route)


def tie(value, *others):
    return lax.optimization_barrier((value, *others))[0]


def core_swap(value, first, second):
    nx, ny = lax.axis_size("gx"), lax.axis_size("gy")
    route = []
    for i in range(nx):
        for j in range(ny):
            axis, bit = (first, second)[j % 2]
            there = (i ^ bit, j) if axis == "gx" else (i, j ^ bit)
            route.append((i * ny + j, there[0] * ny + there[1]))
    return lax.ppermute(value, ("gx", "gy"), route)


def weight_sums(mine, other):
    bit = lax.rem(lax.axis_index("gy"), 2)
    steps = []
    for axis, first in (("gy", 2), ("gx", 1)):
        step = first
        while step < lax.axis_size(axis):
            steps.append((axis, step))
            step *= 2
    steps.append(steps.pop(0))
    turned = []
    for at in range(0, len(steps) - 1, 2):
        turned += [steps[at + 1], steps[at]]
    turned += steps[len(turned) :]
    state = {"sum": mine}

    def step(at, waits):
        sent = tie(state["sum"], *waits) if waits else state["sum"]
        if at > len(steps):
            theirs = swap(sent, "gy", 1)
            return jnp.where(
                bit == 0, jnp.concatenate([sent, theirs]), jnp.concatenate([theirs, sent])
            )
        if at == 0:
            there = swap(other, "gy", 1)
        else:
            there = core_swap(sent, steps[at - 1], turned[at - 1])
        state["sum"] = (sent.astype(F32) + there.astype(F32)).astype(BF)
        return state["sum"]

    return step, len(steps) + 1


def call(kernel, outs, ins, spaces="", scratch=(), last=0, us=1.0):
    kinds = {"s": pltpu.SMEM, "h": pltpu.HBM, "v": pltpu.VMEM}
    spaces = spaces + "v" * (len(ins) - len(spaces))
    ins = [
        pltpu.with_memory_space_constraint(value, pltpu.HBM) if space == "h" else value
        for value, space in zip(ins, spaces)
    ]
    keep = len(outs) - last
    return pl.pallas_call(
        kernel,
        out_shape=[
            pltpu.VMEM(shape, kind) if at < keep else jax.ShapeDtypeStruct(shape, kind)
            for at, (shape, kind) in enumerate(outs)
        ],
        in_specs=[pl.BlockSpec(memory_space=kinds[k]) for k in spaces],
        out_specs=[pl.BlockSpec(memory_space=pltpu.VMEM)] * len(outs),
        scratch_shapes=list(scratch),
        compiler_params=pltpu.CompilerParams(vmem_limit_bytes=32 * 1024 * 1024),
        cost_estimate=pl.CostEstimate(
            flops=int(us * 1e9), bytes_accessed=int(us * 3e6), transcendentals=0
        ),
    )(*ins)


def body(
    features, neighbours, counts, conv_weight, down_weight, head_weight, coarse_map, latent_grad
):
    flat = features.reshape(SLOTS * C, 512)
    lat = latent_grad.reshape(512, 128)
    xm, send_xa, send_xb, send_ya, send_yb = call(
        pack_kernel,
        [
            ((512, 512), BF),
            ((784, 128), BF), ((256, 128), BF), ((784, 128), BF), ((256, 128), BF),
        ],
        (counts, coarse_map, flat, lat),
        "shhh",
        [pltpu.SMEM((1, 8), jnp.int32), pltpu.SemaphoreType.DMA((4,))],
        us=1.5,
    )
    got_xa = swap(send_xa, "gx", 1)
    got_xb = swap_odd(send_xb, "gx")
    got_ya = swap(send_ya, "gy", 1)
    got_yb = swap_odd(send_yb, "gy")
    (store,) = call(
        prep_kernel,
        [((STORE, 512), BF)],
        (xm, conv_weight, down_weight, head_weight),
        "vhhh",
        [pltpu.VMEM((C, 448), BF), pltpu.SemaphoreType.DMA((3,))],
        us=1.5,
    )
    got_xy = swap(tie(got_xa[256:784], got_xb, got_yb, got_ya), "gy", 1)
    hg, mine, other, send = call(
        main_kernel,
        [((512, 512), BF), ((448, 128), BF), ((448, 128), BF), ((SEND, 128), BF)],
        (neighbours, coarse_map, lat, xm, got_xa, got_xb, got_ya, got_yb, got_xy, store),
        "ssh",
        [
            pltpu.VMEM((896, 128), F32),
            pltpu.VMEM((512, 128), BF),
            pltpu.SemaphoreType.DMA,
            pltpu.VMEM((4, 17, C, 256), BF),
            pltpu.VMEM((SLOTS, 448, 512), BF),
            pltpu.VMEM((SLOTS, C, 512), F32),
            pltpu.VMEM((512, 512), BF),
            pltpu.VMEM((SLOTS + 1, C, 128), BF),
            pltpu.VMEM((4, 5, C, 128), F32),
            pltpu.VMEM((3, 16, 128), jnp.int32),
            pltpu.SMEM((3, 16, 128), jnp.int32),
            pltpu.SemaphoreType.DMA,
        ],
        us=6.0,
    )

    sum_step, steps = weight_sums(mine, other)
    mine = sum_step(0, ())
    got_xa = swap(tie(send[XA : XA + 256], mine), "gx", 1)
    got_xb = swap_odd(tie(send[XB : XB + 256], mine), "gx")
    got_yb = swap_odd(tie(send[YB : YB + 256], mine), "gy")
    (moved,) = call(
        roll_kernel,
        [((2048, 512), BF)],
        (neighbours, tie(hg, mine, got_yb)),
        "s",
        [
            pltpu.VMEM((4, 8, C, 256), BF),
            pltpu.VMEM((2, 8, C, 512), BF),
            pltpu.VMEM((4, 9, C, 256), F32),
            pltpu.VMEM((2, 9, C, 512), F32),
        ],
        us=2.5,
    )
    mine = sum_step(1, ())
    got_ya = swap(tie(send[YA : OCT + 512], mine), "gy", 1)
    (near,) = call(
        near_kernel,
        [((512, 512), F32)],
        (hg, tie(moved, mine), conv_weight),
        "",
        [pltpu.VMEM((448, 512), BF)],
        us=1.0,
    )
    mine = sum_step(2, (got_xa, got_xb, got_yb, moved))
    (grad,) = call(
        far_kernel,
        [((512, 512), BF)],
        (counts, tie(near, mine), got_xa, got_xb, got_ya, got_yb, conv_weight),
        "s",
        [pltpu.VMEM((4, 256, 128), BF)],
        1,
        us=1.8,
    )
    got_x = swap(tie(send[OCT : OCT + 512], grad), "gx", 1)
    mine = sum_step(3, (near, got_ya))
    got_xy = swap(tie(got_x, mine), "gy", 1)
    (latent,) = call(
        latent_kernel,
        [((512, 128), BF)],
        (coarse_map, send, got_x, got_ya, got_xy),
        "s",
        [pltpu.VMEM((33, C, 128), BF)],
        1,
        us=1.2,
    )
    mine = sum_step(4, (grad,))
    for at in range(5, steps):
        mine = sum_step(at, ())
    summed = sum_step(steps, (got_xy,))
    scale = float(SLOTS * lax.axis_size("gx") * lax.axis_size("gy")) ** (-0.5)
    conv_grad, down_grad, head_grad = call(
        lambda *refs: scale_kernel(scale, *refs),
        [((C, 448), F32), ((128, 512), F32), ((128, 128), F32)],
        (summed,),
        last=3,
    )
    return (
        latent.reshape(1, 512, 128), grad.reshape(SLOTS, C, 512), conv_grad, down_grad, head_grad,
    )


def solution(mesh):
    both = ("gx", "gy")
    placed = (
        P(both, None, None), P(both, None), P(both), P(), P(), P(), P(both, None),
        P(both, None, None),
    )
    return jax.shard_map(
        body,
        mesh=mesh,
        in_specs=placed,
        out_specs=(P(both, None, None), P(both, None, None), P(), P(), P()),
        check_vma=False,
    )
```

```python
import jax
import jax.numpy as jnp
from jax import lax
from jax.experimental import pallas as pl
from jax.experimental.pallas import tpu as pltpu
from jax.sharding import PartitionSpec as P

BF = jnp.bfloat16
F32 = jnp.float32
C = 64
SLOTS = 8
NT = (((1,), (1,)), ((), ()))
TN = (((0,), (0,)), ((), ()))


def one_hot(source, rows):
    row = lax.broadcasted_iota(jnp.int32, (rows, source.shape[1]), 0)
    return jnp.where(row == source, 1.0, 0.0).astype(BF)


def lanes_of(count):
    lane = lax.broadcasted_iota(jnp.int32, (1, count), 1)
    return lane, lane // 64 % 2, lane // 16 % 4, lane // 4 % 4, lane % 4


def cell(r, a, b, c):
    return r * 64 + (a + 4) % 4 * 16 + (b + 4) % 4 * 4 + (c + 4) % 4


def turn_z():
    lane, r, a, b, c = lanes_of(256)
    step = jnp.where(lane < 128, jnp.where(r == 0, -1, 0), jnp.where(r == 1, 1, 0))
    return one_hot(cell(1 - r, a, b, c + step), 128)


def turn_xy(k):
    lane, r, a, b, c = lanes_of(256)
    x = 1 - 2 * (k // 2)
    y = 1 - 2 * (k % 2)
    first = lane < 128
    return one_hot(cell(r, a + jnp.where(first, x, 0), b + jnp.where(first, 0, y), c), 128)


def spread(axis, want=None):
    lane, r, a, b, c = lanes_of(512)
    place, other = (a, b) if axis == 0 else (b, a)
    source = lane // 256 * 64 + lane // 128 % 2 * 32 + r * 16 + other * 4 + c
    if want is not None:
        source = jnp.where(place == want, source, -1)
    return one_hot(source, 128)


def pack(direction):
    lane = lanes_of(128)[0] % 64
    want = 3 * (1 - direction % 2)
    half, r, other, c = lane // 32, lane // 16 % 2, lane // 4 % 4, lane % 4
    a, b = (want, other) if direction < 2 else (other, want)
    return one_hot(half * 128 + cell(r, a, b, c), 256)


def regroup():
    lane = lanes_of(512)[0]
    return one_hot(lane % 8 * 64 + lane // 8, 512)


CONV, DOWN, DOWN_BACK, POOL, POOL_Z, STORE = 0, 64, 192, 704, 1728, 2880


def pool_at(store, d, slot):
    rows = pl.ds(pl.multiple_of(POOL + (d // 2 * SLOTS + slot) * C, C), C)
    return store[rows, d % 2 * 256 : d % 2 * 256 + 256]


def pool_z_at(store, d, slot):
    return store[pl.ds(pl.multiple_of(POOL_Z + (d * 9 + slot) * C, C), C), :]


def dot(left, right, dims=None):
    if dims is None:
        return jnp.dot(left, right, preferred_element_type=F32)
    return lax.dot_general(left, right, dims, preferred_element_type=F32)


def lane_of(shape):
    return lax.broadcasted_iota(jnp.int32, shape, len(shape) - 1)


def parts(block, direction):
    if direction == 0:
        return block[:, 256:512]
    if direction == 1:
        return block[:, 0:256]
    first = 128 if direction == 2 else 0
    return jnp.concatenate([block[:, first : first + 128], block[:, first + 256 : first + 384]], 1)


def roll_blocks(source, put, put_z):
    up = turn_z()
    for k in range(4):
        chunk = source[:, k * 128 : (k + 1) * 128]
        moved = dot(chunk, turn_xy(k)).astype(BF)
        x_dir, y_dir = 1 - k // 2, 3 - k % 2
        put(x_dir, k % 2 * 128, moved[:, 0:128])
        put(y_dir, k // 2 * 128, moved[:, 128:256])
        moved = dot(chunk, up).astype(BF)
        put_z(0, k * 128, moved[:, 0:128])
        put_z(1, k * 128, moved[:, 128:256])


def rim_masks():
    lane = lane_of((C, 256))
    a, b = lane // 16 % 4, lane // 4 % 4
    masks = [a == 0, a == 3, b == 0, b == 3]
    lane = lane_of((C, 512))
    r, c = lane // 64 % 2, lane % 4
    return masks, [(r == 0) & (c == 0), (r == 1) & (c == 3)]


def weave(direction, moved, block):
    if direction == 0:
        return [moved[:, 0:128], moved[:, 128:256], block[:, 0:128], block[:, 128:256]]
    if direction == 1:
        return [block[:, 256:384], block[:, 384:512], moved[:, 0:128], moved[:, 128:256]]
    if direction == 2:
        return [moved[:, 0:128], block[:, 0:128], moved[:, 128:256], block[:, 256:384]]
    return [block[:, 128:256], moved[:, 0:128], block[:, 384:512], moved[:, 128:256]]


def parities():
    return lax.rem(lax.axis_index("gx"), 2), lax.rem(lax.axis_index("gy"), 2)


def load(pairs, sems):
    copies = [pltpu.make_async_copy(src, dst, sems.at[i]) for i, (src, dst) in enumerate(pairs)]
    for copy in copies:
        copy.start()
    return copies


def pack_kernel(
    counts, cmap_hbm, x_hbm, lat_hbm,
    xm, send_xa, send_xb, send_ya, send_yb,
    cmap, sems,
):
    copies = load(
        [
            (cmap_hbm, cmap), (x_hbm, xm),
            (lat_hbm, send_xa.at[256:768]), (lat_hbm, send_ya.at[256:768]),
        ],
        sems,
    )
    px, py = parities()
    packs = [pack(d) for d in range(4)]
    for copy in copies[:2]:
        copy.wait()
    for b in range(1, SLOTS):
        @pl.when(b >= counts[0])
        def _():
            xm[b * C : (b + 1) * C, :] = jnp.zeros((C, 512), BF)
    masked = xm[...]
    low = lane_of((256, 128)) < 64
    faces = []
    for d in range(4):
        packed = dot(parts(masked, d), packs[d])
        faces.append(jnp.where(low, packed[0:256], packed[256:512]))
    even = px == 0
    send_xa[0:256, :] = jnp.where(even, faces[0], faces[1]).astype(BF)
    send_xb[...] = jnp.where(even, faces[1], faces[0]).astype(BF)
    even = py == 0
    send_ya[0:256, :] = jnp.where(even, faces[2], faces[3]).astype(BF)
    send_yb[...] = jnp.where(even, faces[3], faces[2]).astype(BF)
    row = lax.broadcasted_iota(jnp.int32, (16, 128), 0)
    named = jnp.zeros((16, 128), jnp.int32)
    for k in range(8):
        named = jnp.where(row == k, cmap[0, k], named)
    named = named.astype(F32).astype(BF)
    send_xa[768:784, :] = named
    send_ya[768:784, :] = named
    for copy in copies[2:]:
        copy.wait()


def prep_kernel(xm, conv_hbm, down_hbm, head_hbm, store, conv, sems):
    copies = load(
        [
            (down_hbm, store.at[DOWN : DOWN + 128]),
            (conv_hbm, conv),
            (head_hbm, store.at[DOWN_BACK : DOWN_BACK + 128, 128:256]),
        ],
        sems,
    )
    for d in range(2):
        start = POOL_Z + (d * 9 + SLOTS) * C
        store[start : start + C, :] = jnp.zeros((C, 512), BF)

    def put(d, lane, value):
        rows = slice(POOL + d // 2 * 512, POOL + d // 2 * 512 + 512)
        store[rows, d % 2 * 256 + lane : d % 2 * 256 + lane + 128] = value

    def put_z(d, lane, value):
        start = POOL_Z + d * 9 * C
        store[start : start + 512, lane : lane + 128] = value

    roll_blocks(xm, put, put_z)
    copies[0].wait()
    down = store[DOWN : DOWN + 128, :]
    table = regroup()
    store[DOWN : DOWN + 128, :] = dot(down, table, NT).astype(BF)
    store[DOWN_BACK : DOWN_BACK + 512, 0:128] = dot(table, down, NT).astype(BF)
    copies[1].wait()
    store[CONV : CONV + C, 0:448] = conv[...]
    copies[2].wait()


YA, OCT, XA, XB, YB, SEND = 0, 256, 768, 1024, 1280, 1536


def main_kernel(
    nb, cmap, lat_hbm,
    xm, got_xa, got_xb, got_ya, got_yb, got_xy, store,
    hg_ref, mine_ref, other_ref, send,
    sums_ref, lat_ref, lat_sem, reach, taps, slope, act2, routed, far, maps_v, maps_s, sem,
):
    px, py = parities()
    for j, got in enumerate((got_xa, got_ya, got_xy)):
        maps_v[j] = got[768:784, :].astype(F32).astype(jnp.int32)
    copy = pltpu.make_async_copy(maps_v, maps_s, sem)
    copy.start()
    lat_copy = pltpu.make_async_copy(lat_hbm, lat_ref, lat_sem)
    lat_copy.start()
    head = store[DOWN_BACK : DOWN_BACK + 128, 128:256]

    spreads = [spread(axis) for axis in range(2)]
    for got, axis, direction in (
        (got_xa, 0, 1 - px), (got_xb, 0, px), (got_ya, 1, 3 - py), (got_yb, 1, 2 + py),
    ):
        wide = dot(got[0:256, :], spreads[axis]).astype(BF)
        if got is got_xb or got is got_yb:
            wide = jnp.where(inner(("gx", "gy")[axis]), wide, jnp.zeros_like(wide))
        wide = wide.reshape(4, C, 512)
        reach[direction, 8:12] = wide[:, :, 0:256]
        reach[direction, 12:16] = wide[:, :, 256:512]
    for d in range(4):
        for b in range(SLOTS):
            reach[d, b] = pool_at(store, d, b)
        reach[d, 16] = jnp.zeros((C, 256), BF)

    masks, masks_z = rim_masks()
    low = lane_of((C, 128)) < 64
    conv = store[CONV : CONV + C, 0:448]
    for pair in range(SLOTS // 2):
        acts = []
        for b in (2 * pair, 2 * pair + 1):
            block = xm[b * C : (b + 1) * C, :]
            taps[b, 0:C, :] = block
            for d in range(4):
                moved = jnp.where(masks[d], reach[d, nb[b, d]], reach[d, b])
                for k, piece in enumerate(weave(d, moved, block)):
                    taps[b, (d + 1) * C : (d + 2) * C, k * 128 : (k + 1) * 128] = piece
            for d in range(2):
                near = jnp.minimum(nb[b, d + 4], SLOTS)
                taps[b, (d + 5) * C : (d + 6) * C, :] = jnp.where(
                    masks_z[d], pool_z_at(store, d, near), pool_z_at(store, d, b)
                )
            hidden = dot(conv, taps[b])
            gate = 0.5 * jnp.tanh(0.5 * hidden) + 0.5
            slope[b] = gate * (1.0 + hidden * (1.0 - gate))
            acts.append(hidden * gate)
        lanes = slice(pair * 128, (pair + 1) * 128)
        for k in range(4):
            one, two = (v[:, k * 128 : (k + 1) * 128] for v in acts)
            first = jnp.where(low, one, pltpu.roll(two, 64, 1))
            second = jnp.where(low, pltpu.roll(one, 64, 1), two)
            act2[2 * k * C : (2 * k + 1) * C, lanes] = first.astype(BF)
            act2[(2 * k + 1) * C : (2 * k + 2) * C, lanes] = second.astype(BF)

    octants = dot(store[DOWN : DOWN + 128, :], act2[...]).astype(BF).astype(F32)
    gate = 0.5 * jnp.tanh(0.5 * octants) + 0.5
    oct_act = (octants * gate).astype(BF)
    oct_slope = gate * (1.0 + octants * (1.0 - gate))
    projected = dot(head, oct_act).T.astype(BF)
    send[OCT : OCT + 512, :] = projected

    copy.wait()
    lat_copy.wait()
    for s in range(SLOTS):
        routed[s] = jnp.zeros((C, 128), BF)
    for j, (got, start) in enumerate(((lat_ref, 0), (got_xa, 256), (got_ya, 256), (got_xy, 256))):
        for k in range(8):
            name = cmap[0, k] if j == 0 else maps_s[j - 1, k, 0]
            name = name - j * SLOTS
            name = jnp.where((name >= 0) & (name < SLOTS), name, SLOTS)
            routed[name] = got[start + k * C : start + (k + 1) * C, :]
    grad = routed[0:SLOTS].reshape(SLOTS * C, 128)
    head_back = head.astype(F32).T.astype(BF)
    oct_grad = (dot(head_back, grad, NT) * oct_slope).astype(BF)
    sums_ref[768:896, :] = dot(oct_act, grad).T
    down_sum = dot(oct_grad, act2[...], NT)
    for k in range(4):
        sums_ref[256 + k * 128 : 256 + (k + 1) * 128, :] = down_sum[:, k * 128 : (k + 1) * 128]
    conv_sum = jnp.zeros((C, 448), F32)
    for pair in range(SLOTS // 2):
        patch = dot(store[DOWN_BACK : DOWN_BACK + 512, 0:128], oct_grad[:, pair * 128 : (pair + 1) * 128])
        for side in range(2):
            b = 2 * pair + side
            for k in range(4):
                first = patch[2 * k * C : (2 * k + 1) * C]
                second = patch[(2 * k + 1) * C : (2 * k + 2) * C]
                if side == 0:
                    both = jnp.where(low, first, pltpu.roll(second, 64, 1))
                else:
                    both = jnp.where(low, pltpu.roll(first, 64, 1), second)
                lanes = slice(k * 128, (k + 1) * 128)
                hg_ref[b * C : (b + 1) * C, lanes] = (both * slope[b, :, lanes]).astype(BF)
            conv_sum = conv_sum + dot(hg_ref[b * C : (b + 1) * C, :], taps[b], NT)
    for k in range(3):
        sums_ref[k * C : (k + 1) * C, :] = conv_sum[:, k * 128 : (k + 1) * 128]
    sums_ref[3 * C : 4 * C, 0:C] = conv_sum[:, 384:448]
    sums_ref[3 * C : 4 * C, C:128] = jnp.zeros((C, C), F32)

    first, second = sums_ref[0:448, :].astype(BF), sums_ref[448:896, :].astype(BF)
    even = parity() == 0
    mine_ref[...] = jnp.where(even, first, second)
    other_ref[...] = jnp.where(even, second, first)

    for d in range(4):
        for s in range(5):
            far[d, s] = jnp.zeros((C, 128), F32)
    high = lane_of((C, 128)) // 64
    for d in range(4):
        face = dot(parts(hg_ref[...], d ^ 1), pack(d ^ 1))
        for b in range(SLOTS):
            name = nb[b, d] - SLOTS
            away = (name >= 0) & (name < SLOTS)
            row = jnp.where(away, lax.rem(name, 4), 4)
            side = jnp.where(name >= 4, 1, 0)
            far[d, row] += jnp.where(high == side, face[b * C : (b + 1) * C, :], 0.0)
    for at, d in ((XA, 1 - px), (XB, px), (YA, 3 - py), (YB, 2 + py)):
        send[at : at + 256, :] = far[d, 0:4].reshape(256, 128).astype(BF)


def roll_kernel(nb, hg_ref, moved_ref, pool, pool_z, total, total_z):
    def put(d, lane, value):
        pool[d, :, :, lane : lane + 128] = value.reshape(SLOTS, C, 128)

    def put_z(d, lane, value):
        pool_z[d, :, :, lane : lane + 128] = value.reshape(SLOTS, C, 128)

    roll_blocks(hg_ref, put, put_z)
    for s in range(SLOTS):
        for d in range(4):
            total[d, s] = jnp.zeros((C, 256), F32)
        for d in range(2):
            total_z[d, s] = jnp.zeros((C, 512), F32)
    for b in range(SLOTS):
        for d in range(4):
            slot = jnp.minimum(nb[b, d], SLOTS)
            total[d, slot] += pool[d ^ 1, b].astype(F32)
        for d in range(2):
            slot = jnp.minimum(nb[b, d + 4], SLOTS)
            total_z[d, slot] += pool_z[1 - d, b].astype(F32)
    masks, masks_z = rim_masks()
    for b in range(SLOTS):
        for d in range(4):
            rows = slice((d // 2 * SLOTS + b) * C, (d // 2 * SLOTS + b + 1) * C)
            moved_ref[rows, d % 2 * 256 : d % 2 * 256 + 256] = jnp.where(
                masks[d ^ 1], total[d, b].astype(BF), pool[d ^ 1, b]
            )
        for d in range(2):
            rows = slice(((d + 2) * SLOTS + b) * C, ((d + 2) * SLOTS + b + 1) * C)
            moved_ref[rows, :] = jnp.where(
                masks_z[1 - d], total_z[d, b].astype(BF), pool_z[1 - d, b]
            )


def near_kernel(hg_ref, moved_ref, conv_ref, near_ref, fields):
    conv = jnp.concatenate([conv_ref[:, d * C : (d + 1) * C] for d in range(7)], 0)
    for b in range(SLOTS):
        block = hg_ref[b * C : (b + 1) * C, :]
        fields[0:C, :] = block
        for d in range(4):
            rows = slice((d // 2 * SLOTS + b) * C, (d // 2 * SLOTS + b + 1) * C)
            moved = moved_ref[rows, d % 2 * 256 : d % 2 * 256 + 256]
            for k, piece in enumerate(weave(d ^ 1, moved, block)):
                fields[(d + 1) * C : (d + 2) * C, k * 128 : (k + 1) * 128] = piece
        for d in range(2):
            rows = slice(((d + 2) * SLOTS + b) * C, ((d + 2) * SLOTS + b + 1) * C)
            fields[(d + 5) * C : (d + 6) * C, :] = moved_ref[rows, :]
        near_ref[b * C : (b + 1) * C, :] = dot(conv, fields[...], TN)


def far_kernel(counts, near_ref, got_xa, got_xb, got_ya, got_yb, conv_ref, out_ref, rows):
    px, py = parities()
    for got, direction in ((got_xa, px), (got_xb, 1 - px), (got_ya, 2 + py), (got_yb, 3 - py)):
        value = got[0:256, :]
        if got is got_xb or got is got_yb:
            value = jnp.where(inner("gx" if got is got_xb else "gy"), value, jnp.zeros_like(value))
        rows[direction] = value
    fields = []
    for d in range(4):
        conv = conv_ref[:, (d + 1) * C : (d + 2) * C]
        moved = [dot(conv, rows[d, k * C : (k + 1) * C, :], TN).astype(BF) for k in range(4)]
        table = spread(d // 2, 3 * (1 - d % 2))
        fields.append(dot(jnp.concatenate(moved, 0), table))
    for b in range(SLOTS):
        x_low, x_high, y_low, y_high = (
            fields[d][b % 4 * C : (b % 4 + 1) * C, b // 4 * 256 : b // 4 * 256 + 256]
            for d in (1, 0, 3, 2)
        )
        for k in range(4):
            lanes = slice(k * 128, (k + 1) * 128)
            x, y = (x_low, x_high)[k // 2], (y_low, y_high)[k % 2]
            x, y = (v[:, i * 128 : (i + 1) * 128] for v, i in ((x, k % 2), (y, k // 2)))
            grad = near_ref[b * C : (b + 1) * C, lanes] + (x + y)
            out_ref[b * C : (b + 1) * C, lanes] = jnp.where(b < counts[0], grad, 0.0).astype(BF)


def latent_kernel(cmap, own, got_x, got_ya, got_xy, out_ref, rows):
    rows[0:8] = own[OCT : OCT + 512, :].reshape(8, C, 128)
    rows[8:16] = got_x[...].reshape(8, C, 128)
    rows[16:24] = got_ya[256:768, :].reshape(8, C, 128)
    rows[24:32] = got_xy[...].reshape(8, C, 128)
    rows[32] = jnp.zeros((C, 128), BF)
    for k in range(8):
        out_ref[k * C : (k + 1) * C, :] = rows[cmap[0, k]]


def scale_kernel(scale, mine, theirs, conv_out, down_out, head_out):
    even = parity() == 0
    conv_in = jnp.concatenate(
        [
            jnp.where(even, mine[...], theirs[...]),
            jnp.where(even, theirs[...], mine[...]),
        ],
        0,
    )
    for k in range(3):
        conv_out[:, k * 128 : (k + 1) * 128] = conv_in[k * C : (k + 1) * C, :].astype(F32) * scale
    conv_out[:, 384:448] = conv_in[3 * C : 4 * C, 0:C].astype(F32) * scale
    down = jnp.concatenate([conv_in[256 + k * 128 : 384 + k * 128, :] for k in range(4)], 1)
    down_out[...] = dot(down, regroup()) * scale
    head_out[...] = conv_in[768:896, :].astype(F32) * scale


def route(there):
    nx, ny = lax.axis_size("gx"), lax.axis_size("gy")
    pairs = []
    for i in range(nx):
        for j in range(ny):
            x, y = there(i, j)
            pairs.append((i * ny + j, x * ny + y))
    return pairs


def send_to(value, there):
    return lax.ppermute(value, ("gx", "gy"), route(there))


def beside_x(value):
    return send_to(value, lambda i, j: (i ^ 1, j))


def beside_core(value):
    return send_to(value, lambda i, j: (i, j ^ 1))


def beside_both(value):
    return send_to(value, lambda i, j: (i ^ 1, j ^ 1))


def odd_partner(i, count):
    return min(max(i + 2 * (i % 2) - 1, -1), count)


def odd_x(value):
    nx = lax.axis_size("gx")
    return send_to(value, lambda i, j: (odd_partner(i, nx), j) if 0 < i < nx - 1 else (i, j ^ 1))


def odd_y(value):
    ny = lax.axis_size("gy")
    return send_to(value, lambda i, j: (i, odd_partner(j, ny) if 0 < j < ny - 1 else ny - 1 - j))


def inner(axis):
    at = lax.axis_index(axis)
    return (at > 0) & (at < lax.axis_size(axis) - 1)


def parity():
    bits = lax.axis_index("gx") * lax.axis_size("gy") + lax.axis_index("gy")
    count = 0
    for k in range((lax.axis_size("gx") * lax.axis_size("gy") - 1).bit_length()):
        count = count + lax.rem(lax.div(bits, 1 << k), 2)
    return lax.rem(count, 2)


def tie(value, *others):
    return lax.optimization_barrier((value, *others))[0]


def weight_sums(mine, other):
    bits = []
    for axis, first in (("gy", 2), ("gx", 1)):
        bit = first
        while bit < lax.axis_size(axis):
            bits.append((axis, bit))
            bit *= 2
    turned = []
    for at in range(0, len(bits) - 1, 2):
        turned += [bits[at + 1], bits[at]]
    turned += bits[len(turned) :]
    state = {"sum": mine}

    def there(at, i, j):
        axis, bit = (bits, turned)[(i.bit_count() + j.bit_count()) % 2][at]
        return (i ^ bit, j ^ 1) if axis == "gx" else (i, j ^ bit ^ 1)

    def step(at, waits):
        sent = tie(state["sum"], *waits) if waits else state["sum"]
        if at > len(bits):
            return sent, beside_core(sent)
        if at == 0:
            got = beside_core(other)
        else:
            got = send_to(sent, lambda i, j: there(at - 1, i, j))
        state["sum"] = (sent.astype(F32) + got.astype(F32)).astype(BF)
        return state["sum"]

    return step, len(bits) + 1


def call(kernel, outs, ins, spaces="", scratch=(), last=0, us=1.0):
    kinds = {"s": pltpu.SMEM, "h": pltpu.HBM, "v": pltpu.VMEM}
    spaces = spaces + "v" * (len(ins) - len(spaces))
    ins = [
        pltpu.with_memory_space_constraint(value, pltpu.HBM) if space == "h" else value
        for value, space in zip(ins, spaces)
    ]
    keep = len(outs) - last
    return pl.pallas_call(
        kernel,
        out_shape=[
            pltpu.VMEM(shape, kind) if at < keep else jax.ShapeDtypeStruct(shape, kind)
            for at, (shape, kind) in enumerate(outs)
        ],
        in_specs=[pl.BlockSpec(memory_space=kinds[k]) for k in spaces],
        out_specs=[pl.BlockSpec(memory_space=pltpu.VMEM)] * len(outs),
        scratch_shapes=list(scratch),
        compiler_params=pltpu.CompilerParams(vmem_limit_bytes=32 * 1024 * 1024),
        cost_estimate=pl.CostEstimate(
            flops=int(us * 1e9), bytes_accessed=int(us * 3e6), transcendentals=0
        ),
    )(*ins)


def body(
    features, neighbours, counts, conv_weight, down_weight, head_weight, coarse_map, latent_grad
):
    flat = features.reshape(SLOTS * C, 512)
    lat = latent_grad.reshape(512, 128)
    xm, send_xa, send_xb, send_ya, send_yb = call(
        pack_kernel,
        [
            ((512, 512), BF),
            ((784, 128), BF), ((256, 128), BF), ((784, 128), BF), ((256, 128), BF),
        ],
        (counts, coarse_map, flat, lat),
        "shhh",
        [pltpu.SMEM((1, 8), jnp.int32), pltpu.SemaphoreType.DMA((4,))],
        us=1.5,
    )
    got_xy = beside_both(send_xa)
    got_xb = odd_x(send_xb)
    got_ya = beside_core(send_ya)
    got_yb = odd_y(send_yb)
    (store,) = call(
        prep_kernel,
        [((STORE, 512), BF)],
        (xm, conv_weight, down_weight, head_weight),
        "vhhh",
        [pltpu.VMEM((C, 448), BF), pltpu.SemaphoreType.DMA((3,))],
        us=1.5,
    )
    got_xa = beside_core(tie(got_xy, got_xb, got_yb, got_ya))
    hg, mine, other, send = call(
        main_kernel,
        [((512, 512), BF), ((448, 128), BF), ((448, 128), BF), ((SEND, 128), BF)],
        (neighbours, coarse_map, lat, xm, got_xa, got_xb, got_ya, got_yb, got_xy, store),
        "ssh",
        [
            pltpu.VMEM((896, 128), F32),
            pltpu.VMEM((512, 128), BF),
            pltpu.SemaphoreType.DMA,
            pltpu.VMEM((4, 17, C, 256), BF),
            pltpu.VMEM((SLOTS, 448, 512), BF),
            pltpu.VMEM((SLOTS, C, 512), F32),
            pltpu.VMEM((512, 512), BF),
            pltpu.VMEM((SLOTS + 1, C, 128), BF),
            pltpu.VMEM((4, 5, C, 128), F32),
            pltpu.VMEM((3, 16, 128), jnp.int32),
            pltpu.SMEM((3, 16, 128), jnp.int32),
            pltpu.SemaphoreType.DMA,
        ],
        us=6.0,
    )

    sum_step, steps = weight_sums(mine, other)
    mine = sum_step(0, ())
    got_xa = beside_x(tie(send[XA : XA + 256], mine))
    got_xb = odd_x(tie(send[XB : XB + 256], mine))
    got_yb = odd_y(tie(send[YB : YB + 256], mine))
    (moved,) = call(
        roll_kernel,
        [((2048, 512), BF)],
        (neighbours, tie(hg, mine, got_yb)),
        "s",
        [
            pltpu.VMEM((4, 8, C, 256), BF),
            pltpu.VMEM((2, 8, C, 512), BF),
            pltpu.VMEM((4, 9, C, 256), F32),
            pltpu.VMEM((2, 9, C, 512), F32),
        ],
        us=2.5,
    )
    mine = sum_step(1, ())
    got_ya = beside_core(tie(send[YA : OCT + 512], mine))
    (near,) = call(
        near_kernel,
        [((512, 512), F32)],
        (hg, tie(moved, mine), conv_weight),
        "",
        [pltpu.VMEM((448, 512), BF)],
        us=1.0,
    )
    mine = sum_step(2, (got_xa, got_xb, got_yb, moved))
    (grad,) = call(
        far_kernel,
        [((512, 512), BF)],
        (counts, tie(near, mine), got_xa, got_xb, got_ya, got_yb, conv_weight),
        "s",
        [pltpu.VMEM((4, 256, 128), BF)],
        1,
        us=1.8,
    )
    got_xy = beside_both(tie(send[OCT : OCT + 512], grad))
    mine = sum_step(3, (near, got_ya))
    got_x = beside_core(tie(got_xy, mine))
    (latent,) = call(
        latent_kernel,
        [((512, 128), BF)],
        (coarse_map, send, got_x, got_ya, got_xy),
        "s",
        [pltpu.VMEM((33, C, 128), BF)],
        1,
        us=1.2,
    )
    mine = sum_step(4, (grad,))
    for at in range(5, steps):
        mine = sum_step(at, ())
    mine, theirs = sum_step(steps, (got_x,))
    scale = float(SLOTS * lax.axis_size("gx") * lax.axis_size("gy")) ** (-0.5)
    conv_grad, down_grad, head_grad = call(
        lambda *refs: scale_kernel(scale, *refs),
        [((C, 448), F32), ((128, 512), F32), ((128, 128), F32)],
        (mine, theirs),
        last=3,
    )
    return (
        latent.reshape(1, 512, 128), grad.reshape(SLOTS, C, 512), conv_grad, down_grad, head_grad,
    )


def solution(mesh):
    both = ("gx", "gy")
    placed = (
        P(both, None, None), P(both, None), P(both), P(), P(), P(), P(both, None),
        P(both, None, None),
    )
    return jax.shard_map(
        body,
        mesh=mesh,
        in_specs=placed,
        out_specs=(P(both, None, None), P(both, None, None), P(), P(), P()),
        check_vma=False,
    )
```

```python
import jax
import jax.numpy as jnp
from jax import lax
from jax.experimental import pallas as pl
from jax.experimental.pallas import tpu as pltpu
from jax.sharding import PartitionSpec as P

BF = jnp.bfloat16
F32 = jnp.float32
C = 64
SLOTS = 8
NT = (((1,), (1,)), ((), ()))
TN = (((0,), (0,)), ((), ()))


def one_hot(source, rows):
    row = lax.broadcasted_iota(jnp.int32, (rows, source.shape[1]), 0)
    return jnp.where(row == source, 1.0, 0.0).astype(BF)


def lanes_of(count):
    lane = lax.broadcasted_iota(jnp.int32, (1, count), 1)
    return lane, lane // 64 % 2, lane // 16 % 4, lane // 4 % 4, lane % 4


def cell(r, a, b, c):
    return r * 64 + (a + 4) % 4 * 16 + (b + 4) % 4 * 4 + (c + 4) % 4


def turn_z():
    lane, r, a, b, c = lanes_of(256)
    step = jnp.where(lane < 128, jnp.where(r == 0, -1, 0), jnp.where(r == 1, 1, 0))
    return one_hot(cell(1 - r, a, b, c + step), 128)


def turn_xy(k):
    lane, r, a, b, c = lanes_of(256)
    x = 1 - 2 * (k // 2)
    y = 1 - 2 * (k % 2)
    first = lane < 128
    return one_hot(cell(r, a + jnp.where(first, x, 0), b + jnp.where(first, 0, y), c), 128)


def spread(axis, want=None):
    lane, r, a, b, c = lanes_of(512)
    place, other = (a, b) if axis == 0 else (b, a)
    source = lane // 256 * 64 + lane // 128 % 2 * 32 + r * 16 + other * 4 + c
    if want is not None:
        source = jnp.where(place == want, source, -1)
    return one_hot(source, 128)


def pack(direction):
    lane = lanes_of(128)[0] % 64
    want = 3 * (1 - direction % 2)
    half, r, other, c = lane // 32, lane // 16 % 2, lane // 4 % 4, lane % 4
    a, b = (want, other) if direction < 2 else (other, want)
    return one_hot(half * 128 + cell(r, a, b, c), 256)


def regroup():
    lane = lanes_of(512)[0]
    return one_hot(lane % 8 * 64 + lane // 8, 512)


CONV, DOWN, DOWN_BACK, POOL, POOL_Z, STORE = 0, 64, 192, 704, 1728, 2880


def pool_at(store, d, slot):
    rows = pl.ds(pl.multiple_of(POOL + (d // 2 * SLOTS + slot) * C, C), C)
    return store[rows, d % 2 * 256 : d % 2 * 256 + 256]


def pool_z_at(store, d, slot):
    return store[pl.ds(pl.multiple_of(POOL_Z + (d * 9 + slot) * C, C), C), :]


def dot(left, right, dims=None):
    if dims is None:
        return jnp.dot(left, right, preferred_element_type=F32)
    return lax.dot_general(left, right, dims, preferred_element_type=F32)


def lane_of(shape):
    return lax.broadcasted_iota(jnp.int32, shape, len(shape) - 1)


def parts(block, direction):
    if direction == 0:
        return block[:, 256:512]
    if direction == 1:
        return block[:, 0:256]
    first = 128 if direction == 2 else 0
    return jnp.concatenate([block[:, first : first + 128], block[:, first + 256 : first + 384]], 1)


def roll_blocks(source, put, put_z):
    up = turn_z()
    for k in range(4):
        chunk = source[:, k * 128 : (k + 1) * 128]
        moved = dot(chunk, turn_xy(k)).astype(BF)
        x_dir, y_dir = 1 - k // 2, 3 - k % 2
        put(x_dir, k % 2 * 128, moved[:, 0:128])
        put(y_dir, k // 2 * 128, moved[:, 128:256])
        moved = dot(chunk, up).astype(BF)
        put_z(0, k * 128, moved[:, 0:128])
        put_z(1, k * 128, moved[:, 128:256])


def rim_masks():
    lane = lane_of((C, 256))
    a, b = lane // 16 % 4, lane // 4 % 4
    masks = [a == 0, a == 3, b == 0, b == 3]
    lane = lane_of((C, 512))
    r, c = lane // 64 % 2, lane % 4
    return masks, [(r == 0) & (c == 0), (r == 1) & (c == 3)]


def weave(direction, moved, block):
    if direction == 0:
        return [moved[:, 0:128], moved[:, 128:256], block[:, 0:128], block[:, 128:256]]
    if direction == 1:
        return [block[:, 256:384], block[:, 384:512], moved[:, 0:128], moved[:, 128:256]]
    if direction == 2:
        return [moved[:, 0:128], block[:, 0:128], moved[:, 128:256], block[:, 256:384]]
    return [block[:, 128:256], moved[:, 0:128], block[:, 384:512], moved[:, 128:256]]


def parities():
    return lax.rem(lax.axis_index("gx"), 2), lax.rem(lax.axis_index("gy"), 2)


def load(pairs, sems):
    copies = [pltpu.make_async_copy(src, dst, sems.at[i]) for i, (src, dst) in enumerate(pairs)]
    for copy in copies:
        copy.start()
    return copies


def pack_kernel(
    counts, cmap_hbm, x_hbm, lat_hbm,
    xm, send_xa, send_xb, send_ya, send_yb,
    cmap, sems,
):
    copies = load(
        [
            (cmap_hbm, cmap), (x_hbm, xm),
            (lat_hbm, send_xa.at[256:768]), (lat_hbm, send_ya.at[256:768]),
        ],
        sems,
    )
    px, py = parities()
    packs = [pack(d) for d in range(4)]
    for copy in copies[:2]:
        copy.wait()
    for b in range(1, SLOTS):
        @pl.when(b >= counts[0])
        def _():
            xm[b * C : (b + 1) * C, :] = jnp.zeros((C, 512), BF)
    masked = xm[...]
    low = lane_of((256, 128)) < 64
    faces = []
    for d in range(4):
        packed = dot(parts(masked, d), packs[d])
        faces.append(jnp.where(low, packed[0:256], packed[256:512]))
    even = px == 0
    send_xa[0:256, :] = jnp.where(even, faces[0], faces[1]).astype(BF)
    send_xb[...] = jnp.where(even, faces[1], faces[0]).astype(BF)
    even = py == 0
    send_ya[0:256, :] = jnp.where(even, faces[2], faces[3]).astype(BF)
    send_yb[...] = jnp.where(even, faces[3], faces[2]).astype(BF)
    row = lax.broadcasted_iota(jnp.int32, (16, 128), 0)
    named = jnp.zeros((16, 128), jnp.int32)
    for k in range(8):
        named = jnp.where(row == k, cmap[0, k], named)
    named = named.astype(F32).astype(BF)
    send_xa[768:784, :] = named
    send_ya[768:784, :] = named
    for copy in copies[2:]:
        copy.wait()


def prep_kernel(xm, conv_hbm, down_hbm, head_hbm, store, conv, sems):
    copies = load(
        [
            (down_hbm, store.at[DOWN : DOWN + 128]),
            (conv_hbm, conv),
            (head_hbm, store.at[DOWN_BACK : DOWN_BACK + 128, 128:256]),
        ],
        sems,
    )
    for d in range(2):
        start = POOL_Z + (d * 9 + SLOTS) * C
        store[start : start + C, :] = jnp.zeros((C, 512), BF)

    def put(d, lane, value):
        rows = slice(POOL + d // 2 * 512, POOL + d // 2 * 512 + 512)
        store[rows, d % 2 * 256 + lane : d % 2 * 256 + lane + 128] = value

    def put_z(d, lane, value):
        start = POOL_Z + d * 9 * C
        store[start : start + 512, lane : lane + 128] = value

    roll_blocks(xm, put, put_z)
    copies[0].wait()
    down = store[DOWN : DOWN + 128, :]
    table = regroup()
    store[DOWN : DOWN + 128, :] = dot(down, table, NT).astype(BF)
    store[DOWN_BACK : DOWN_BACK + 512, 0:128] = dot(table, down, NT).astype(BF)
    copies[1].wait()
    store[CONV : CONV + C, 0:448] = conv[...]
    copies[2].wait()


YA, OCT, XA, XB, YB, SEND = 0, 256, 768, 1024, 1280, 1536


def main_kernel(
    nb_hbm, cmap_hbm, lat_hbm,
    xm, got_xa, got_xb, got_ya, got_yb, got_xy, store,
    hg_ref, mine_ref, other_ref, send,
    nb, cmap, sems, sums_ref, lat_ref, reach, taps, hg_row, slope, act2, routed, far, maps_v, maps_s, sem,
):
    px, py = parities()
    for j, got in enumerate((got_xa, got_ya, got_xy)):
        maps_v[j] = got[768:784, :].astype(F32).astype(jnp.int32)
    copy = pltpu.make_async_copy(maps_v, maps_s, sem)
    copy.start()
    copies = load([(nb_hbm, nb), (cmap_hbm, cmap), (lat_hbm, lat_ref)], sems)
    head = store[DOWN_BACK : DOWN_BACK + 128, 128:256]

    spreads = [spread(axis) for axis in range(2)]
    for got, axis, direction in (
        (got_xa, 0, 1 - px), (got_xb, 0, px), (got_ya, 1, 3 - py), (got_yb, 1, 2 + py),
    ):
        wide = dot(got[0:256, :], spreads[axis]).astype(BF)
        if got is got_xb or got is got_yb:
            wide = jnp.where(inner(("gx", "gy")[axis]), wide, jnp.zeros_like(wide))
        wide = wide.reshape(4, C, 512)
        reach[direction, 8:12] = wide[:, :, 0:256]
        reach[direction, 12:16] = wide[:, :, 256:512]
    for d in range(4):
        for b in range(SLOTS):
            reach[d, b] = pool_at(store, d, b)
        reach[d, 16] = jnp.zeros((C, 256), BF)

    masks, masks_z = rim_masks()
    low = lane_of((C, 128)) < 64
    copies[0].wait()
    conv = store[CONV : CONV + C, 0:448]
    for pair in range(SLOTS // 2):
        acts = []
        for b in (2 * pair, 2 * pair + 1):
            block = xm[b * C : (b + 1) * C, :]
            at = b * 512
            taps[0:C, at : at + 512] = block
            for d in range(4):
                moved = jnp.where(masks[d], reach[d, nb[b, d]], reach[d, b])
                for k, piece in enumerate(weave(d, moved, block)):
                    lanes = slice(at + k * 128, at + (k + 1) * 128)
                    taps[(d + 1) * C : (d + 2) * C, lanes] = piece
            for d in range(2):
                near = jnp.minimum(nb[b, d + 4], SLOTS)
                taps[(d + 5) * C : (d + 6) * C, at : at + 512] = jnp.where(
                    masks_z[d], pool_z_at(store, d, near), pool_z_at(store, d, b)
                )
            hidden = dot(conv, taps[:, at : at + 512])
            gate = 0.5 * jnp.tanh(0.5 * hidden) + 0.5
            slope[b] = gate * (1.0 + hidden * (1.0 - gate))
            acts.append(hidden * gate)
        lanes = slice(pair * 128, (pair + 1) * 128)
        for k in range(4):
            one, two = (v[:, k * 128 : (k + 1) * 128] for v in acts)
            first = jnp.where(low, one, pltpu.roll(two, 64, 1))
            second = jnp.where(low, pltpu.roll(one, 64, 1), two)
            act2[2 * k * C : (2 * k + 1) * C, lanes] = first.astype(BF)
            act2[(2 * k + 1) * C : (2 * k + 2) * C, lanes] = second.astype(BF)

    octants = dot(store[DOWN : DOWN + 128, :], act2[...]).astype(BF).astype(F32)
    gate = 0.5 * jnp.tanh(0.5 * octants) + 0.5
    oct_act = (octants * gate).astype(BF)
    oct_slope = gate * (1.0 + octants * (1.0 - gate))
    projected = dot(head, oct_act).T.astype(BF)
    send[OCT : OCT + 512, :] = projected

    copy.wait()
    copies[1].wait()
    copies[2].wait()
    for s in range(SLOTS):
        routed[s] = jnp.zeros((C, 128), BF)
    for j, (got, start) in enumerate(((lat_ref, 0), (got_xa, 256), (got_ya, 256), (got_xy, 256))):
        for k in range(8):
            name = cmap[0, k] if j == 0 else maps_s[j - 1, k, 0]
            name = name - j * SLOTS
            name = jnp.where((name >= 0) & (name < SLOTS), name, SLOTS)
            routed[name] = got[start + k * C : start + (k + 1) * C, :]
    grad = routed[0:SLOTS].reshape(SLOTS * C, 128)
    head_back = head.astype(F32).T.astype(BF)
    oct_grad = (dot(head_back, grad, NT) * oct_slope).astype(BF)
    sums_ref[768:896, :] = dot(oct_act, grad).T
    down_sum = dot(oct_grad, act2[...], NT)
    for k in range(4):
        sums_ref[256 + k * 128 : 256 + (k + 1) * 128, :] = down_sum[:, k * 128 : (k + 1) * 128]
    for pair in range(SLOTS // 2):
        patch = dot(store[DOWN_BACK : DOWN_BACK + 512, 0:128], oct_grad[:, pair * 128 : (pair + 1) * 128])
        for side in range(2):
            b = 2 * pair + side
            for k in range(4):
                first = patch[2 * k * C : (2 * k + 1) * C]
                second = patch[(2 * k + 1) * C : (2 * k + 2) * C]
                if side == 0:
                    both = jnp.where(low, first, pltpu.roll(second, 64, 1))
                else:
                    both = jnp.where(low, pltpu.roll(first, 64, 1), second)
                lanes = slice(k * 128, (k + 1) * 128)
                both = (both * slope[b, :, lanes]).astype(BF)
                hg_ref[b * C : (b + 1) * C, lanes] = both
                hg_row[:, b * 512 + k * 128 : b * 512 + (k + 1) * 128] = both
    conv_sum = dot(hg_row[...], taps[...], NT)
    for k in range(3):
        sums_ref[k * C : (k + 1) * C, :] = conv_sum[:, k * 128 : (k + 1) * 128]
    sums_ref[3 * C : 4 * C, 0:C] = conv_sum[:, 384:448]
    sums_ref[3 * C : 4 * C, C:128] = jnp.zeros((C, C), F32)

    first, second = sums_ref[0:448, :].astype(BF), sums_ref[448:896, :].astype(BF)
    even = parity() == 0
    mine_ref[...] = jnp.where(even, first, second)
    other_ref[...] = jnp.where(even, second, first)

    for d in range(4):
        for s in range(5):
            far[d, s] = jnp.zeros((C, 128), F32)
    high = lane_of((C, 128)) // 64
    for d in range(4):
        face = dot(parts(hg_ref[...], d ^ 1), pack(d ^ 1))
        for b in range(SLOTS):
            name = nb[b, d] - SLOTS
            away = (name >= 0) & (name < SLOTS)
            row = jnp.where(away, lax.rem(name, 4), 4)
            side = jnp.where(name >= 4, 1, 0)
            far[d, row] += jnp.where(high == side, face[b * C : (b + 1) * C, :], 0.0)
    for at, d in ((XA, 1 - px), (XB, px), (YA, 3 - py), (YB, 2 + py)):
        send[at : at + 256, :] = far[d, 0:4].reshape(256, 128).astype(BF)


def roll_kernel(nb_hbm, hg_ref, moved_ref, pool, pool_z, total, total_z, nb, sem):
    copy = pltpu.make_async_copy(nb_hbm, nb, sem)
    copy.start()

    def put(d, lane, value):
        pool[d, :, :, lane : lane + 128] = value.reshape(SLOTS, C, 128)

    def put_z(d, lane, value):
        pool_z[d, :, :, lane : lane + 128] = value.reshape(SLOTS, C, 128)

    roll_blocks(hg_ref, put, put_z)
    for s in range(SLOTS):
        for d in range(4):
            total[d, s] = jnp.zeros((C, 256), F32)
        for d in range(2):
            total_z[d, s] = jnp.zeros((C, 512), F32)
    copy.wait()
    for b in range(SLOTS):
        for d in range(4):
            slot = jnp.minimum(nb[b, d], SLOTS)
            total[d, slot] += pool[d ^ 1, b].astype(F32)
        for d in range(2):
            slot = jnp.minimum(nb[b, d + 4], SLOTS)
            total_z[d, slot] += pool_z[1 - d, b].astype(F32)
    masks, masks_z = rim_masks()
    for b in range(SLOTS):
        for d in range(4):
            rows = slice((d // 2 * SLOTS + b) * C, (d // 2 * SLOTS + b + 1) * C)
            moved_ref[rows, d % 2 * 256 : d % 2 * 256 + 256] = jnp.where(
                masks[d ^ 1], total[d, b].astype(BF), pool[d ^ 1, b]
            )
        for d in range(2):
            rows = slice(((d + 2) * SLOTS + b) * C, ((d + 2) * SLOTS + b + 1) * C)
            moved_ref[rows, :] = jnp.where(
                masks_z[1 - d], total_z[d, b].astype(BF), pool_z[1 - d, b]
            )


def near_kernel(hg_ref, moved_ref, conv_ref, near_ref, fields):
    conv = jnp.concatenate([conv_ref[:, d * C : (d + 1) * C] for d in range(7)], 0)
    for b in range(SLOTS):
        block = hg_ref[b * C : (b + 1) * C, :]
        fields[0:C, :] = block
        for d in range(4):
            rows = slice((d // 2 * SLOTS + b) * C, (d // 2 * SLOTS + b + 1) * C)
            moved = moved_ref[rows, d % 2 * 256 : d % 2 * 256 + 256]
            for k, piece in enumerate(weave(d ^ 1, moved, block)):
                fields[(d + 1) * C : (d + 2) * C, k * 128 : (k + 1) * 128] = piece
        for d in range(2):
            rows = slice(((d + 2) * SLOTS + b) * C, ((d + 2) * SLOTS + b + 1) * C)
            fields[(d + 5) * C : (d + 6) * C, :] = moved_ref[rows, :]
        near_ref[b * C : (b + 1) * C, :] = dot(conv, fields[...], TN)


def far_kernel(counts, near_ref, got_xa, got_xb, got_ya, got_yb, conv_ref, out_ref, rows):
    px, py = parities()
    for got, direction in ((got_xa, px), (got_xb, 1 - px), (got_ya, 2 + py), (got_yb, 3 - py)):
        value = got[0:256, :]
        if got is got_xb or got is got_yb:
            value = jnp.where(inner("gx" if got is got_xb else "gy"), value, jnp.zeros_like(value))
        rows[direction] = value
    fields = []
    for d in range(4):
        conv = conv_ref[:, (d + 1) * C : (d + 2) * C]
        moved = [dot(conv, rows[d, k * C : (k + 1) * C, :], TN).astype(BF) for k in range(4)]
        table = spread(d // 2, 3 * (1 - d % 2))
        fields.append(dot(jnp.concatenate(moved, 0), table))
    for b in range(SLOTS):
        x_low, x_high, y_low, y_high = (
            fields[d][b % 4 * C : (b % 4 + 1) * C, b // 4 * 256 : b // 4 * 256 + 256]
            for d in (1, 0, 3, 2)
        )
        for k in range(4):
            lanes = slice(k * 128, (k + 1) * 128)
            x, y = (x_low, x_high)[k // 2], (y_low, y_high)[k % 2]
            x, y = (v[:, i * 128 : (i + 1) * 128] for v, i in ((x, k % 2), (y, k // 2)))
            grad = near_ref[b * C : (b + 1) * C, lanes] + (x + y)
            out_ref[b * C : (b + 1) * C, lanes] = jnp.where(b < counts[0], grad, 0.0).astype(BF)


def latent_kernel(cmap, own, got_x, got_ya, got_xy, out_ref, rows):
    rows[0:8] = own[OCT : OCT + 512, :].reshape(8, C, 128)
    rows[8:16] = got_x[...].reshape(8, C, 128)
    rows[16:24] = got_ya[256:768, :].reshape(8, C, 128)
    rows[24:32] = got_xy[...].reshape(8, C, 128)
    rows[32] = jnp.zeros((C, 128), BF)
    for k in range(8):
        out_ref[k * C : (k + 1) * C, :] = rows[cmap[0, k]]


def scale_kernel(scale, mine, theirs, conv_out, down_out, head_out):
    even = parity() == 0
    conv_in = jnp.concatenate(
        [
            jnp.where(even, mine[...], theirs[...]),
            jnp.where(even, theirs[...], mine[...]),
        ],
        0,
    )
    for k in range(3):
        conv_out[:, k * 128 : (k + 1) * 128] = conv_in[k * C : (k + 1) * C, :].astype(F32) * scale
    conv_out[:, 384:448] = conv_in[3 * C : 4 * C, 0:C].astype(F32) * scale
    down = jnp.concatenate([conv_in[256 + k * 128 : 384 + k * 128, :] for k in range(4)], 1)
    down_out[...] = dot(down, regroup()) * scale
    head_out[...] = conv_in[768:896, :].astype(F32) * scale


def route(there):
    nx, ny = lax.axis_size("gx"), lax.axis_size("gy")
    pairs = []
    for i in range(nx):
        for j in range(ny):
            x, y = there(i, j)
            pairs.append((i * ny + j, x * ny + y))
    return pairs


def send_to(value, there):
    return lax.ppermute(value, ("gx", "gy"), route(there))


def beside_x(value):
    return send_to(value, lambda i, j: (i ^ 1, j))


def beside_core(value):
    return send_to(value, lambda i, j: (i, j ^ 1))


def beside_both(value):
    return send_to(value, lambda i, j: (i ^ 1, j ^ 1))


def odd_partner(i, count):
    return min(max(i + 2 * (i % 2) - 1, -1), count)


def odd_x(value):
    nx = lax.axis_size("gx")
    return send_to(value, lambda i, j: (odd_partner(i, nx), j) if 0 < i < nx - 1 else (i, j ^ 1))


def odd_y(value):
    ny = lax.axis_size("gy")
    return send_to(value, lambda i, j: (i, odd_partner(j, ny) if 0 < j < ny - 1 else ny - 1 - j))


def inner(axis):
    at = lax.axis_index(axis)
    return (at > 0) & (at < lax.axis_size(axis) - 1)


def parity():
    bits = lax.axis_index("gx") * lax.axis_size("gy") + lax.axis_index("gy")
    count = 0
    for k in range((lax.axis_size("gx") * lax.axis_size("gy") - 1).bit_length()):
        count = count + lax.rem(lax.div(bits, 1 << k), 2)
    return lax.rem(count, 2)


def tie(value, *others):
    return lax.optimization_barrier((value, *others))[0]


def weight_sums(mine, other):
    bits = []
    for axis, first in (("gy", 2), ("gx", 1)):
        bit = first
        while bit < lax.axis_size(axis):
            bits.append((axis, bit))
            bit *= 2
    turned = []
    for at in range(0, len(bits) - 1, 2):
        turned += [bits[at + 1], bits[at]]
    turned += bits[len(turned) :]
    state = {"sum": mine}

    def there(at, i, j):
        axis, bit = (bits, turned)[(i.bit_count() + j.bit_count()) % 2][at]
        return (i ^ bit, j ^ 1) if axis == "gx" else (i, j ^ bit ^ 1)

    def step(at, waits):
        sent = tie(state["sum"], *waits) if waits else state["sum"]
        if at > len(bits):
            return sent, beside_core(sent)
        if at == 0:
            got = beside_core(other)
        else:
            got = send_to(sent, lambda i, j: there(at - 1, i, j))
        state["sum"] = (sent.astype(F32) + got.astype(F32)).astype(BF)
        return state["sum"]

    return step, len(bits) + 1


def call(kernel, outs, ins, spaces="", scratch=(), last=0, us=1.0):
    kinds = {"s": pltpu.SMEM, "h": pltpu.HBM, "v": pltpu.VMEM}
    spaces = spaces + "v" * (len(ins) - len(spaces))
    ins = [
        pltpu.with_memory_space_constraint(value, pltpu.HBM) if space == "h" else value
        for value, space in zip(ins, spaces)
    ]
    keep = len(outs) - last
    return pl.pallas_call(
        kernel,
        out_shape=[
            pltpu.VMEM(shape, kind) if at < keep else jax.ShapeDtypeStruct(shape, kind)
            for at, (shape, kind) in enumerate(outs)
        ],
        in_specs=[pl.BlockSpec(memory_space=kinds[k]) for k in spaces],
        out_specs=[pl.BlockSpec(memory_space=pltpu.VMEM)] * len(outs),
        scratch_shapes=list(scratch),
        compiler_params=pltpu.CompilerParams(vmem_limit_bytes=32 * 1024 * 1024),
        cost_estimate=pl.CostEstimate(
            flops=int(us * 1e9), bytes_accessed=int(us * 3e6), transcendentals=0
        ),
    )(*ins)


def body(
    features, neighbours, counts, conv_weight, down_weight, head_weight, coarse_map, latent_grad
):
    flat = features.reshape(SLOTS * C, 512)
    lat = latent_grad.reshape(512, 128)
    xm, send_xa, send_xb, send_ya, send_yb = call(
        pack_kernel,
        [
            ((512, 512), BF),
            ((784, 128), BF), ((256, 128), BF), ((784, 128), BF), ((256, 128), BF),
        ],
        (counts, coarse_map, flat, lat),
        "shhh",
        [pltpu.SMEM((1, 8), jnp.int32), pltpu.SemaphoreType.DMA((4,))],
        us=1.5,
    )
    got_xy = beside_both(send_xa)
    got_xb = odd_x(send_xb)
    got_ya = beside_core(send_ya)
    got_yb = odd_y(send_yb)
    (store,) = call(
        prep_kernel,
        [((STORE, 512), BF)],
        (xm, conv_weight, down_weight, head_weight),
        "vhhh",
        [pltpu.VMEM((C, 448), BF), pltpu.SemaphoreType.DMA((3,))],
        us=1.5,
    )
    got_xa = beside_core(tie(got_xy, got_xb, got_yb, got_ya, store))
    hg, mine, other, send = call(
        main_kernel,
        [((512, 512), BF), ((448, 128), BF), ((448, 128), BF), ((SEND, 128), BF)],
        (neighbours, coarse_map, lat, xm, got_xa, got_xb, got_ya, got_yb, got_xy, store),
        "hhh",
        [
            pltpu.SMEM((SLOTS, 6), jnp.int32),
            pltpu.SMEM((1, 8), jnp.int32),
            pltpu.SemaphoreType.DMA((3,)),
            pltpu.VMEM((896, 128), F32),
            pltpu.VMEM((512, 128), BF),
            pltpu.VMEM((4, 17, C, 256), BF),
            pltpu.VMEM((448, SLOTS * 512), BF),
            pltpu.VMEM((C, SLOTS * 512), BF),
            pltpu.VMEM((SLOTS, C, 512), F32),
            pltpu.VMEM((512, 512), BF),
            pltpu.VMEM((SLOTS + 1, C, 128), BF),
            pltpu.VMEM((4, 5, C, 128), F32),
            pltpu.VMEM((3, 16, 128), jnp.int32),
            pltpu.SMEM((3, 16, 128), jnp.int32),
            pltpu.SemaphoreType.DMA,
        ],
        us=6.0,
    )

    sum_step, steps = weight_sums(mine, other)
    mine = sum_step(0, ())
    got_xa = beside_x(tie(send[XA : XA + 256], mine))
    got_xb = odd_x(send[XB : XB + 256])
    got_yb = odd_y(tie(send[YB : YB + 256], mine))
    mine = sum_step(1, ())
    got_ya = beside_core(tie(send[YA : OCT + 512], mine))
    (moved,) = call(
        roll_kernel,
        [((2048, 512), BF)],
        (neighbours, tie(hg, mine, got_xb)),
        "h",
        [
            pltpu.VMEM((4, 8, C, 256), BF),
            pltpu.VMEM((2, 8, C, 512), BF),
            pltpu.VMEM((4, 9, C, 256), F32),
            pltpu.VMEM((2, 9, C, 512), F32),
            pltpu.SMEM((SLOTS, 6), jnp.int32),
            pltpu.SemaphoreType.DMA,
        ],
        us=2.5,
    )
    mine = sum_step(2, ())
    (near,) = call(
        near_kernel,
        [((512, 512), F32)],
        (hg, tie(moved, mine), conv_weight),
        "",
        [pltpu.VMEM((448, 512), BF)],
        us=1.0,
    )
    got_xy = beside_both(tie(send[OCT : OCT + 512], near))
    mine = sum_step(3, (moved, got_ya, got_xa, got_yb, got_xb,))
    (grad,) = call(
        far_kernel,
        [((512, 512), BF)],
        (counts, tie(near, mine), got_xa, got_xb, got_ya, got_yb, conv_weight),
        "s",
        [pltpu.VMEM((4, 256, 128), BF)],
        1,
        us=1.8,
    )
    got_x = beside_core(tie(got_xy, mine))
    (latent,) = call(
        latent_kernel,
        [((512, 128), BF)],
        (coarse_map, send, got_x, got_ya, got_xy),
        "s",
        [pltpu.VMEM((33, C, 128), BF)],
        1,
        us=1.2,
    )
    mine = sum_step(4, (near,))
    for at in range(5, steps):
        mine = sum_step(at, ())
    mine, theirs = sum_step(steps, (grad, got_x,))
    scale = float(SLOTS * lax.axis_size("gx") * lax.axis_size("gy")) ** (-0.5)
    conv_grad, down_grad, head_grad = call(
        lambda *refs: scale_kernel(scale, *refs),
        [((C, 448), F32), ((128, 512), F32), ((128, 128), F32)],
        (mine, theirs),
        last=3,
    )
    return (
        latent.reshape(1, 512, 128), grad.reshape(SLOTS, C, 512), conv_grad, down_grad, head_grad,
    )


def solution(mesh):
    both = ("gx", "gy")
    placed = (
        P(both, None, None), P(both, None), P(both), P(), P(), P(), P(both, None),
        P(both, None, None),
    )
    return jax.shard_map(
        body,
        mesh=mesh,
        in_specs=placed,
        out_specs=(P(both, None, None), P(both, None, None), P(), P(), P()),
        check_vma=False,
    )
```

```python
import jax
import jax.numpy as jnp
from jax import lax
from jax.experimental import pallas as pl
from jax.experimental.pallas import tpu as pltpu
from jax.sharding import PartitionSpec as P

BF = jnp.bfloat16
F32 = jnp.float32
C = 64
SLOTS = 8
NT = (((1,), (1,)), ((), ()))
TN = (((0,), (0,)), ((), ()))


def one_hot(source, rows):
    row = lax.broadcasted_iota(jnp.int32, (rows, source.shape[1]), 0)
    return jnp.where(row == source, 1.0, 0.0).astype(BF)


def lanes_of(count):
    lane = lax.broadcasted_iota(jnp.int32, (1, count), 1)
    return lane, lane // 64 % 2, lane // 16 % 4, lane // 4 % 4, lane % 4


def cell(r, a, b, c):
    return r * 64 + (a + 4) % 4 * 16 + (b + 4) % 4 * 4 + (c + 4) % 4


def turn_z():
    lane, r, a, b, c = lanes_of(256)
    step = jnp.where(lane < 128, jnp.where(r == 0, -1, 0), jnp.where(r == 1, 1, 0))
    return one_hot(cell(1 - r, a, b, c + step), 128)


def turn_xy(k):
    lane, r, a, b, c = lanes_of(256)
    x = 1 - 2 * (k // 2)
    y = 1 - 2 * (k % 2)
    first = lane < 128
    return one_hot(cell(r, a + jnp.where(first, x, 0), b + jnp.where(first, 0, y), c), 128)


def spread(axis, want=None):
    lane, r, a, b, c = lanes_of(512)
    place, other = (a, b) if axis == 0 else (b, a)
    source = lane // 256 * 64 + lane // 128 % 2 * 32 + r * 16 + other * 4 + c
    if want is not None:
        source = jnp.where(place == want, source, -1)
    return one_hot(source, 128)


def pack(direction):
    lane = lanes_of(128)[0] % 64
    want = 3 * (1 - direction % 2)
    half, r, other, c = lane // 32, lane // 16 % 2, lane // 4 % 4, lane % 4
    a, b = (want, other) if direction < 2 else (other, want)
    return one_hot(half * 128 + cell(r, a, b, c), 256)


def regroup():
    lane = lanes_of(512)[0]
    return one_hot(lane % 8 * 64 + lane // 8, 512)


CONV, DOWN, DOWN_BACK, POOL, POOL_Z, XM, STORE = 0, 64, 192, 704, 1728, 2880, 3392


def pool_at(store, d, slot):
    rows = pl.ds(pl.multiple_of(POOL + (d // 2 * SLOTS + slot) * C, C), C)
    return store[rows, d % 2 * 256 : d % 2 * 256 + 256]


def pool_z_at(store, d, slot):
    return store[pl.ds(pl.multiple_of(POOL_Z + (d * 9 + slot) * C, C), C), :]


def dot(left, right, dims=None):
    if dims is None:
        return jnp.dot(left, right, preferred_element_type=F32)
    return lax.dot_general(left, right, dims, preferred_element_type=F32)


def lane_of(shape):
    return lax.broadcasted_iota(jnp.int32, shape, len(shape) - 1)


def parts(block, direction):
    if direction == 0:
        return block[:, 256:512]
    if direction == 1:
        return block[:, 0:256]
    first = 128 if direction == 2 else 0
    return jnp.concatenate([block[:, first : first + 128], block[:, first + 256 : first + 384]], 1)


def roll_blocks(source, put, put_z):
    up = turn_z()
    for k in range(4):
        chunk = source[:, k * 128 : (k + 1) * 128]
        moved = dot(chunk, turn_xy(k)).astype(BF)
        x_dir, y_dir = 1 - k // 2, 3 - k % 2
        put(x_dir, k % 2 * 128, moved[:, 0:128])
        put(y_dir, k // 2 * 128, moved[:, 128:256])
        moved = dot(chunk, up).astype(BF)
        put_z(0, k * 128, moved[:, 0:128])
        put_z(1, k * 128, moved[:, 128:256])


def rim_masks():
    lane = lane_of((C, 256))
    a, b = lane // 16 % 4, lane // 4 % 4
    masks = [a == 0, a == 3, b == 0, b == 3]
    lane = lane_of((C, 512))
    r, c = lane // 64 % 2, lane % 4
    return masks, [(r == 0) & (c == 0), (r == 1) & (c == 3)]


def weave(direction, moved, block):
    if direction == 0:
        return [moved[:, 0:128], moved[:, 128:256], block[:, 0:128], block[:, 128:256]]
    if direction == 1:
        return [block[:, 256:384], block[:, 384:512], moved[:, 0:128], moved[:, 128:256]]
    if direction == 2:
        return [moved[:, 0:128], block[:, 0:128], moved[:, 128:256], block[:, 256:384]]
    return [block[:, 128:256], moved[:, 0:128], block[:, 384:512], moved[:, 128:256]]


def parities():
    return lax.rem(lax.axis_index("gx"), 2), lax.rem(lax.axis_index("gy"), 2)


def load(pairs, sems):
    copies = [pltpu.make_async_copy(src, dst, sems.at[i]) for i, (src, dst) in enumerate(pairs)]
    for copy in copies:
        copy.start()
    return copies


def pack_kernel(
    cmap_hbm, x_hbm, lat_hbm,
    send_xa, send_xb, send_ya, send_yb,
    x_ref, cmap, sems,
):
    copies = load(
        [
            (cmap_hbm, cmap), (x_hbm, x_ref),
            (lat_hbm, send_xa.at[256:768]), (lat_hbm, send_ya.at[256:768]),
        ],
        sems,
    )
    px, py = parities()
    packs = [pack(d) for d in range(4)]
    for copy in copies[:2]:
        copy.wait()
    cube = x_ref[...]
    low = lane_of((256, 128)) < 64
    faces = []
    for d in range(4):
        packed = dot(parts(cube, d), packs[d])
        faces.append(jnp.where(low, packed[0:256], packed[256:512]))
    even = px == 0
    send_xa[0:256, :] = jnp.where(even, faces[0], faces[1]).astype(BF)
    send_xb[...] = jnp.where(even, faces[1], faces[0]).astype(BF)
    even = py == 0
    send_ya[0:256, :] = jnp.where(even, faces[2], faces[3]).astype(BF)
    send_yb[...] = jnp.where(even, faces[3], faces[2]).astype(BF)
    row = lax.broadcasted_iota(jnp.int32, (16, 128), 0)
    named = jnp.zeros((16, 128), jnp.int32)
    for k in range(8):
        named = jnp.where(row == k, cmap[0, k], named)
    named = named.astype(F32).astype(BF)
    send_xa[768:784, :] = named
    send_ya[768:784, :] = named
    for copy in copies[2:]:
        copy.wait()


def prep_kernel(counts, x_hbm, conv_hbm, down_hbm, head_hbm, store, conv, sems):
    copies = load(
        [
            (x_hbm, store.at[XM : XM + 512]),
            (down_hbm, store.at[DOWN : DOWN + 128]),
            (conv_hbm, conv),
            (head_hbm, store.at[DOWN_BACK : DOWN_BACK + 128, 128:256]),
        ],
        sems,
    )
    for d in range(2):
        start = POOL_Z + (d * 9 + SLOTS) * C
        store[start : start + C, :] = jnp.zeros((C, 512), BF)

    def put(d, lane, value):
        rows = slice(POOL + d // 2 * 512, POOL + d // 2 * 512 + 512)
        store[rows, d % 2 * 256 + lane : d % 2 * 256 + lane + 128] = value

    def put_z(d, lane, value):
        start = POOL_Z + d * 9 * C
        store[start : start + 512, lane : lane + 128] = value

    copies[0].wait()
    for b in range(1, SLOTS):
        @pl.when(b >= counts[0])
        def _():
            store[XM + b * C : XM + (b + 1) * C, :] = jnp.zeros((C, 512), BF)
    roll_blocks(store.at[XM : XM + 512], put, put_z)
    copies[1].wait()
    down = store[DOWN : DOWN + 128, :]
    table = regroup()
    store[DOWN : DOWN + 128, :] = dot(down, table, NT).astype(BF)
    store[DOWN_BACK : DOWN_BACK + 512, 0:128] = dot(table, down, NT).astype(BF)
    copies[2].wait()
    store[CONV : CONV + C, 0:448] = conv[...]
    copies[3].wait()


YA, OCT, XA, XB, YB, SEND = 0, 256, 768, 1024, 1280, 1536


def main_kernel(
    nb_hbm, cmap_hbm, lat_hbm,
    got_xa, got_xb, got_ya, got_yb, got_xy, store,
    hg_ref, mine_ref, other_ref, send,
    nb, cmap, sems, sums_ref, lat_ref, reach, taps, hg_row, slope, act2, routed, far, maps_v, maps_s, sem,
):
    px, py = parities()
    for j, got in enumerate((got_xa, got_ya, got_xy)):
        maps_v[j] = got[768:784, :].astype(F32).astype(jnp.int32)
    copy = pltpu.make_async_copy(maps_v, maps_s, sem)
    copy.start()
    copies = load([(nb_hbm, nb), (cmap_hbm, cmap), (lat_hbm, lat_ref)], sems)
    head = store[DOWN_BACK : DOWN_BACK + 128, 128:256]

    spreads = [spread(axis) for axis in range(2)]
    for got, axis, direction in (
        (got_xa, 0, 1 - px), (got_xb, 0, px), (got_ya, 1, 3 - py), (got_yb, 1, 2 + py),
    ):
        wide = dot(got[0:256, :], spreads[axis]).astype(BF)
        if got is got_xb or got is got_yb:
            wide = jnp.where(inner(("gx", "gy")[axis]), wide, jnp.zeros_like(wide))
        wide = wide.reshape(4, C, 512)
        reach[direction, 8:12] = wide[:, :, 0:256]
        reach[direction, 12:16] = wide[:, :, 256:512]
    for d in range(4):
        for b in range(SLOTS):
            reach[d, b] = pool_at(store, d, b)
        reach[d, 16] = jnp.zeros((C, 256), BF)

    masks, masks_z = rim_masks()
    low = lane_of((C, 128)) < 64
    copies[0].wait()
    conv = store[CONV : CONV + C, 0:448]
    for pair in range(SLOTS // 2):
        acts = []
        for b in (2 * pair, 2 * pair + 1):
            block = store[XM + b * C : XM + (b + 1) * C, :]
            at = b * 512
            taps[0:C, at : at + 512] = block
            for d in range(4):
                moved = jnp.where(masks[d], reach[d, nb[b, d]], reach[d, b])
                for k, piece in enumerate(weave(d, moved, block)):
                    lanes = slice(at + k * 128, at + (k + 1) * 128)
                    taps[(d + 1) * C : (d + 2) * C, lanes] = piece
            for d in range(2):
                near = jnp.minimum(nb[b, d + 4], SLOTS)
                taps[(d + 5) * C : (d + 6) * C, at : at + 512] = jnp.where(
                    masks_z[d], pool_z_at(store, d, near), pool_z_at(store, d, b)
                )
            hidden = dot(conv, taps[:, at : at + 512])
            gate = 0.5 * jnp.tanh(0.5 * hidden) + 0.5
            slope[b] = gate * (1.0 + hidden * (1.0 - gate))
            acts.append(hidden * gate)
        lanes = slice(pair * 128, (pair + 1) * 128)
        for k in range(4):
            one, two = (v[:, k * 128 : (k + 1) * 128] for v in acts)
            first = jnp.where(low, one, pltpu.roll(two, 64, 1))
            second = jnp.where(low, pltpu.roll(one, 64, 1), two)
            act2[2 * k * C : (2 * k + 1) * C, lanes] = first.astype(BF)
            act2[(2 * k + 1) * C : (2 * k + 2) * C, lanes] = second.astype(BF)

    octants = dot(store[DOWN : DOWN + 128, :], act2[...]).astype(BF).astype(F32)
    gate = 0.5 * jnp.tanh(0.5 * octants) + 0.5
    oct_act = (octants * gate).astype(BF)
    oct_slope = gate * (1.0 + octants * (1.0 - gate))
    projected = dot(head, oct_act).T.astype(BF)
    send[OCT : OCT + 512, :] = projected

    copy.wait()
    copies[1].wait()
    copies[2].wait()
    for s in range(SLOTS):
        routed[s] = jnp.zeros((C, 128), BF)
    for j, (got, start) in enumerate(((lat_ref, 0), (got_xa, 256), (got_ya, 256), (got_xy, 256))):
        for k in range(8):
            name = cmap[0, k] if j == 0 else maps_s[j - 1, k, 0]
            name = name - j * SLOTS
            name = jnp.where((name >= 0) & (name < SLOTS), name, SLOTS)
            routed[name] = got[start + k * C : start + (k + 1) * C, :]
    grad = routed[0:SLOTS].reshape(SLOTS * C, 128)
    head_back = head.astype(F32).T.astype(BF)
    oct_grad = (dot(head_back, grad, NT) * oct_slope).astype(BF)
    sums_ref[768:896, :] = dot(oct_act, grad).T
    down_sum = dot(oct_grad, act2[...], NT)
    for k in range(4):
        sums_ref[256 + k * 128 : 256 + (k + 1) * 128, :] = down_sum[:, k * 128 : (k + 1) * 128]
    for pair in range(SLOTS // 2):
        patch = dot(store[DOWN_BACK : DOWN_BACK + 512, 0:128], oct_grad[:, pair * 128 : (pair + 1) * 128])
        for side in range(2):
            b = 2 * pair + side
            for k in range(4):
                first = patch[2 * k * C : (2 * k + 1) * C]
                second = patch[(2 * k + 1) * C : (2 * k + 2) * C]
                if side == 0:
                    both = jnp.where(low, first, pltpu.roll(second, 64, 1))
                else:
                    both = jnp.where(low, pltpu.roll(first, 64, 1), second)
                lanes = slice(k * 128, (k + 1) * 128)
                both = (both * slope[b, :, lanes]).astype(BF)
                hg_ref[b * C : (b + 1) * C, lanes] = both
                hg_row[:, b * 512 + k * 128 : b * 512 + (k + 1) * 128] = both
    conv_sum = dot(hg_row[...], taps[...], NT)
    for k in range(3):
        sums_ref[k * C : (k + 1) * C, :] = conv_sum[:, k * 128 : (k + 1) * 128]
    sums_ref[3 * C : 4 * C, 0:C] = conv_sum[:, 384:448]
    sums_ref[3 * C : 4 * C, C:128] = jnp.zeros((C, C), F32)

    first, second = sums_ref[0:448, :].astype(BF), sums_ref[448:896, :].astype(BF)
    even = parity() == 0
    mine_ref[...] = jnp.where(even, first, second)
    other_ref[...] = jnp.where(even, second, first)

    for d in range(4):
        for s in range(5):
            far[d, s] = jnp.zeros((C, 128), F32)
    high = lane_of((C, 128)) // 64
    for d in range(4):
        face = dot(parts(hg_ref[...], d ^ 1), pack(d ^ 1))
        for b in range(SLOTS):
            name = nb[b, d] - SLOTS
            away = (name >= 0) & (name < SLOTS)
            row = jnp.where(away, lax.rem(name, 4), 4)
            side = jnp.where(name >= 4, 1, 0)
            far[d, row] += jnp.where(high == side, face[b * C : (b + 1) * C, :], 0.0)
    for at, d in ((XA, 1 - px), (XB, px), (YA, 3 - py), (YB, 2 + py)):
        send[at : at + 256, :] = far[d, 0:4].reshape(256, 128).astype(BF)


def roll_kernel(nb_hbm, hg_ref, moved_ref, pool, pool_z, total, total_z, nb, sem):
    copy = pltpu.make_async_copy(nb_hbm, nb, sem)
    copy.start()

    def put(d, lane, value):
        pool[d, :, :, lane : lane + 128] = value.reshape(SLOTS, C, 128)

    def put_z(d, lane, value):
        pool_z[d, :, :, lane : lane + 128] = value.reshape(SLOTS, C, 128)

    roll_blocks(hg_ref, put, put_z)
    for s in range(SLOTS):
        for d in range(4):
            total[d, s] = jnp.zeros((C, 256), F32)
        for d in range(2):
            total_z[d, s] = jnp.zeros((C, 512), F32)
    copy.wait()
    for b in range(SLOTS):
        for d in range(4):
            slot = jnp.minimum(nb[b, d], SLOTS)
            total[d, slot] += pool[d ^ 1, b].astype(F32)
        for d in range(2):
            slot = jnp.minimum(nb[b, d + 4], SLOTS)
            total_z[d, slot] += pool_z[1 - d, b].astype(F32)
    masks, masks_z = rim_masks()
    for b in range(SLOTS):
        for d in range(4):
            rows = slice((d // 2 * SLOTS + b) * C, (d // 2 * SLOTS + b + 1) * C)
            moved_ref[rows, d % 2 * 256 : d % 2 * 256 + 256] = jnp.where(
                masks[d ^ 1], total[d, b].astype(BF), pool[d ^ 1, b]
            )
        for d in range(2):
            rows = slice(((d + 2) * SLOTS + b) * C, ((d + 2) * SLOTS + b + 1) * C)
            moved_ref[rows, :] = jnp.where(
                masks_z[1 - d], total_z[d, b].astype(BF), pool_z[1 - d, b]
            )


def near_kernel(hg_ref, moved_ref, conv_ref, near_ref, fields):
    conv = jnp.concatenate([conv_ref[:, d * C : (d + 1) * C] for d in range(7)], 0)
    for b in range(SLOTS):
        block = hg_ref[b * C : (b + 1) * C, :]
        fields[0:C, :] = block
        for d in range(4):
            rows = slice((d // 2 * SLOTS + b) * C, (d // 2 * SLOTS + b + 1) * C)
            moved = moved_ref[rows, d % 2 * 256 : d % 2 * 256 + 256]
            for k, piece in enumerate(weave(d ^ 1, moved, block)):
                fields[(d + 1) * C : (d + 2) * C, k * 128 : (k + 1) * 128] = piece
        for d in range(2):
            rows = slice(((d + 2) * SLOTS + b) * C, ((d + 2) * SLOTS + b + 1) * C)
            fields[(d + 5) * C : (d + 6) * C, :] = moved_ref[rows, :]
        near_ref[b * C : (b + 1) * C, :] = dot(conv, fields[...], TN)


def far_kernel(counts, near_ref, got_xa, got_xb, got_ya, got_yb, conv_ref, out_ref, rows):
    px, py = parities()
    for got, direction in ((got_xa, px), (got_xb, 1 - px), (got_ya, 2 + py), (got_yb, 3 - py)):
        value = got[0:256, :]
        if got is got_xb or got is got_yb:
            value = jnp.where(inner("gx" if got is got_xb else "gy"), value, jnp.zeros_like(value))
        rows[direction] = value
    fields = []
    for d in range(4):
        conv = conv_ref[:, (d + 1) * C : (d + 2) * C]
        moved = [dot(conv, rows[d, k * C : (k + 1) * C, :], TN).astype(BF) for k in range(4)]
        table = spread(d // 2, 3 * (1 - d % 2))
        fields.append(dot(jnp.concatenate(moved, 0), table))
    for b in range(SLOTS):
        x_low, x_high, y_low, y_high = (
            fields[d][b % 4 * C : (b % 4 + 1) * C, b // 4 * 256 : b // 4 * 256 + 256]
            for d in (1, 0, 3, 2)
        )
        for k in range(4):
            lanes = slice(k * 128, (k + 1) * 128)
            x, y = (x_low, x_high)[k // 2], (y_low, y_high)[k % 2]
            x, y = (v[:, i * 128 : (i + 1) * 128] for v, i in ((x, k % 2), (y, k // 2)))
            grad = near_ref[b * C : (b + 1) * C, lanes] + (x + y)
            out_ref[b * C : (b + 1) * C, lanes] = jnp.where(b < counts[0], grad, 0.0).astype(BF)


def latent_kernel(cmap, own, got_x, got_ya, got_xy, out_ref, rows):
    rows[0:8] = own[OCT : OCT + 512, :].reshape(8, C, 128)
    rows[8:16] = got_x[...].reshape(8, C, 128)
    rows[16:24] = got_ya[256:768, :].reshape(8, C, 128)
    rows[24:32] = got_xy[...].reshape(8, C, 128)
    rows[32] = jnp.zeros((C, 128), BF)
    for k in range(8):
        out_ref[k * C : (k + 1) * C, :] = rows[cmap[0, k]]


def scale_kernel(scale, mine, theirs, conv_out, down_out, head_out):
    even = parity() == 0
    conv_in = jnp.concatenate(
        [
            jnp.where(even, mine[...], theirs[...]),
            jnp.where(even, theirs[...], mine[...]),
        ],
        0,
    )
    for k in range(3):
        conv_out[:, k * 128 : (k + 1) * 128] = conv_in[k * C : (k + 1) * C, :].astype(F32) * scale
    conv_out[:, 384:448] = conv_in[3 * C : 4 * C, 0:C].astype(F32) * scale
    down = jnp.concatenate([conv_in[256 + k * 128 : 384 + k * 128, :] for k in range(4)], 1)
    down_out[...] = dot(down, regroup()) * scale
    head_out[...] = conv_in[768:896, :].astype(F32) * scale


def route(there):
    nx, ny = lax.axis_size("gx"), lax.axis_size("gy")
    pairs = []
    for i in range(nx):
        for j in range(ny):
            x, y = there(i, j)
            pairs.append((i * ny + j, x * ny + y))
    return pairs


def send_to(value, there):
    return lax.ppermute(value, ("gx", "gy"), route(there))


def beside_x(value):
    return send_to(value, lambda i, j: (i ^ 1, j))


def beside_core(value):
    return send_to(value, lambda i, j: (i, j ^ 1))


def beside_both(value):
    return send_to(value, lambda i, j: (i ^ 1, j ^ 1))


def odd_partner(i, count):
    return min(max(i + 2 * (i % 2) - 1, -1), count)


def odd_x(value):
    nx = lax.axis_size("gx")
    return send_to(value, lambda i, j: (odd_partner(i, nx), j) if 0 < i < nx - 1 else (i, j ^ 1))


def odd_y(value):
    ny = lax.axis_size("gy")
    return send_to(value, lambda i, j: (i, odd_partner(j, ny) if 0 < j < ny - 1 else ny - 1 - j))


def inner(axis):
    at = lax.axis_index(axis)
    return (at > 0) & (at < lax.axis_size(axis) - 1)


def parity():
    bits = lax.axis_index("gx") * lax.axis_size("gy") + lax.axis_index("gy")
    count = 0
    for k in range((lax.axis_size("gx") * lax.axis_size("gy") - 1).bit_length()):
        count = count + lax.rem(lax.div(bits, 1 << k), 2)
    return lax.rem(count, 2)


def tie(value, *others):
    return lax.optimization_barrier((value, *others))[0]


def weight_sums(mine, other):
    bits = []
    for axis, first in (("gy", 2), ("gx", 1)):
        bit = first
        while bit < lax.axis_size(axis):
            bits.append((axis, bit))
            bit *= 2
    if len(bits) > 2:
        bits.insert(1, bits.pop(2))
    turned = []
    for at in range(0, len(bits) - 1, 2):
        turned += [bits[at + 1], bits[at]]
    turned += bits[len(turned) :]
    state = {"sum": mine}

    def there(at, i, j):
        axis, bit = (bits, turned)[(i.bit_count() + j.bit_count()) % 2][at]
        return (i ^ bit, j ^ 1) if axis == "gx" else (i, j ^ bit ^ 1)

    def step(at, waits):
        sent = tie(state["sum"], *waits) if waits else state["sum"]
        if at > len(bits):
            return sent, beside_core(sent)
        if at == 0:
            got = beside_core(other)
        else:
            got = send_to(sent, lambda i, j: there(at - 1, i, j))
        state["sum"] = (sent.astype(F32) + got.astype(F32)).astype(BF)
        return state["sum"]

    return step, len(bits) + 1


def call(kernel, outs, ins, spaces="", scratch=(), last=0, us=1.0):
    kinds = {"s": pltpu.SMEM, "h": pltpu.HBM, "v": pltpu.VMEM}
    spaces = spaces + "v" * (len(ins) - len(spaces))
    ins = [
        pltpu.with_memory_space_constraint(value, pltpu.HBM) if space == "h" else value
        for value, space in zip(ins, spaces)
    ]
    keep = len(outs) - last
    return pl.pallas_call(
        kernel,
        out_shape=[
            pltpu.VMEM(shape, kind) if at < keep else jax.ShapeDtypeStruct(shape, kind)
            for at, (shape, kind) in enumerate(outs)
        ],
        in_specs=[pl.BlockSpec(memory_space=kinds[k]) for k in spaces],
        out_specs=[pl.BlockSpec(memory_space=pltpu.VMEM)] * len(outs),
        scratch_shapes=list(scratch),
        compiler_params=pltpu.CompilerParams(vmem_limit_bytes=32 * 1024 * 1024),
        cost_estimate=pl.CostEstimate(
            flops=int(us * 1e9), bytes_accessed=int(us * 3e6), transcendentals=0
        ),
    )(*ins)


def body(
    features, neighbours, counts, conv_weight, down_weight, head_weight, coarse_map, latent_grad
):
    flat = features.reshape(SLOTS * C, 512)
    lat = latent_grad.reshape(512, 128)
    send_xa, send_xb, send_ya, send_yb = call(
        pack_kernel,
        [
            ((784, 128), BF), ((256, 128), BF), ((784, 128), BF), ((256, 128), BF),
        ],
        (coarse_map, flat, lat),
        "hhh",
        [pltpu.VMEM((512, 512), BF), pltpu.SMEM((1, 8), jnp.int32), pltpu.SemaphoreType.DMA((4,))],
        us=1.5,
    )
    got_xy = beside_both(send_xa)
    got_xb = odd_x(send_xb)
    got_ya = beside_core(send_ya)
    got_yb = odd_y(send_yb)
    (store,) = call(
        prep_kernel,
        [((STORE, 512), BF)],
        (counts, flat, conv_weight, down_weight, head_weight),
        "shhhh",
        [pltpu.VMEM((C, 448), BF), pltpu.SemaphoreType.DMA((4,))],
        us=1.5,
    )
    got_xa = beside_core(tie(got_xy, got_xb, got_yb, got_ya, store))
    hg, mine, other, send = call(
        main_kernel,
        [((512, 512), BF), ((448, 128), BF), ((448, 128), BF), ((SEND, 128), BF)],
        (neighbours, coarse_map, lat, got_xa, got_xb, got_ya, got_yb, got_xy, store),
        "hhh",
        [
            pltpu.SMEM((SLOTS, 6), jnp.int32),
            pltpu.SMEM((1, 8), jnp.int32),
            pltpu.SemaphoreType.DMA((3,)),
            pltpu.VMEM((896, 128), F32),
            pltpu.VMEM((512, 128), BF),
            pltpu.VMEM((4, 17, C, 256), BF),
            pltpu.VMEM((448, SLOTS * 512), BF),
            pltpu.VMEM((C, SLOTS * 512), BF),
            pltpu.VMEM((SLOTS, C, 512), F32),
            pltpu.VMEM((512, 512), BF),
            pltpu.VMEM((SLOTS + 1, C, 128), BF),
            pltpu.VMEM((4, 5, C, 128), F32),
            pltpu.VMEM((3, 16, 128), jnp.int32),
            pltpu.SMEM((3, 16, 128), jnp.int32),
            pltpu.SemaphoreType.DMA,
        ],
        us=6.0,
    )

    sum_step, steps = weight_sums(mine, other)
    mine = sum_step(0, ())
    got_xa = beside_x(tie(send[XA : XA + 256], mine))
    got_xb = odd_x(send[XB : XB + 256])
    got_yb = odd_y(tie(send[YB : YB + 256], mine))
    mine = sum_step(1, ())
    got_ya = beside_core(tie(send[YA : OCT + 512], mine))
    (moved,) = call(
        roll_kernel,
        [((2048, 512), BF)],
        (neighbours, tie(hg, mine, got_xb)),
        "h",
        [
            pltpu.VMEM((4, 8, C, 256), BF),
            pltpu.VMEM((2, 8, C, 512), BF),
            pltpu.VMEM((4, 9, C, 256), F32),
            pltpu.VMEM((2, 9, C, 512), F32),
            pltpu.SMEM((SLOTS, 6), jnp.int32),
            pltpu.SemaphoreType.DMA,
        ],
        us=2.5,
    )
    mine = sum_step(2, ())
    (near,) = call(
        near_kernel,
        [((512, 512), F32)],
        (hg, tie(moved, mine), conv_weight),
        "",
        [pltpu.VMEM((448, 512), BF)],
        us=1.0,
    )
    got_xy = beside_both(tie(send[OCT : OCT + 512], near))
    mine = sum_step(3, (moved, got_ya, got_xa, got_yb, got_xb,))
    (grad,) = call(
        far_kernel,
        [((512, 512), BF)],
        (counts, tie(near, mine), got_xa, got_xb, got_ya, got_yb, conv_weight),
        "s",
        [pltpu.VMEM((4, 256, 128), BF)],
        1,
        us=1.8,
    )
    got_x = beside_core(tie(got_xy, mine))
    (latent,) = call(
        latent_kernel,
        [((512, 128), BF)],
        (coarse_map, send, got_x, got_ya, got_xy),
        "s",
        [pltpu.VMEM((33, C, 128), BF)],
        1,
        us=1.2,
    )
    mine = sum_step(4, (near,))
    for at in range(5, steps):
        mine = sum_step(at, ())
    mine, theirs = sum_step(steps, (grad, got_x,))
    scale = float(SLOTS * lax.axis_size("gx") * lax.axis_size("gy")) ** (-0.5)
    conv_grad, down_grad, head_grad = call(
        lambda *refs: scale_kernel(scale, *refs),
        [((C, 448), F32), ((128, 512), F32), ((128, 128), F32)],
        (mine, theirs),
        last=3,
    )
    return (
        latent.reshape(1, 512, 128), grad.reshape(SLOTS, C, 512), conv_grad, down_grad, head_grad,
    )


def solution(mesh):
    both = ("gx", "gy")
    placed = (
        P(both, None, None), P(both, None), P(both), P(), P(), P(), P(both, None),
        P(both, None, None),
    )
    return jax.shard_map(
        body,
        mesh=mesh,
        in_specs=placed,
        out_specs=(P(both, None, None), P(both, None, None), P(), P(), P()),
        check_vma=False,
    )
```

```python
import jax
import jax.numpy as jnp
from jax import lax
from jax.experimental import pallas as pl
from jax.experimental.pallas import tpu as pltpu
from jax.sharding import PartitionSpec as P

BF = jnp.bfloat16
F32 = jnp.float32
C = 64
SLOTS = 8
NT = (((1,), (1,)), ((), ()))
TN = (((0,), (0,)), ((), ()))


def one_hot(source, rows):
    row = lax.broadcasted_iota(jnp.int32, (rows, source.shape[1]), 0)
    return jnp.where(row == source, 1.0, 0.0).astype(BF)


def lanes_of(count):
    lane = lax.broadcasted_iota(jnp.int32, (1, count), 1)
    return lane, lane // 64 % 2, lane // 16 % 4, lane // 4 % 4, lane % 4


def cell(r, a, b, c):
    return r * 64 + (a + 4) % 4 * 16 + (b + 4) % 4 * 4 + (c + 4) % 4


def turn_z():
    lane, r, a, b, c = lanes_of(256)
    step = jnp.where(lane < 128, jnp.where(r == 0, -1, 0), jnp.where(r == 1, 1, 0))
    return one_hot(cell(1 - r, a, b, c + step), 128)


def turn_xy(k):
    lane, r, a, b, c = lanes_of(256)
    x = 1 - 2 * (k // 2)
    y = 1 - 2 * (k % 2)
    first = lane < 128
    return one_hot(cell(r, a + jnp.where(first, x, 0), b + jnp.where(first, 0, y), c), 128)


def spread(axis, want=None):
    lane, r, a, b, c = lanes_of(512)
    place, other = (a, b) if axis == 0 else (b, a)
    source = lane // 256 * 64 + lane // 128 % 2 * 32 + r * 16 + other * 4 + c
    if want is not None:
        source = jnp.where(place == want, source, -1)
    return one_hot(source, 128)


def pack(direction):
    lane = lanes_of(128)[0] % 64
    want = 3 * (1 - direction % 2)
    half, r, other, c = lane // 32, lane // 16 % 2, lane // 4 % 4, lane % 4
    a, b = (want, other) if direction < 2 else (other, want)
    return one_hot(half * 128 + cell(r, a, b, c), 256)


def regroup():
    lane = lanes_of(512)[0]
    return one_hot(lane % 8 * 64 + lane // 8, 512)


CONV, DOWN, DOWN_BACK, POOL, POOL_Z, XM, STORE = 0, 64, 192, 704, 1728, 2880, 3392


def pool_at(store, d, slot):
    rows = pl.ds(pl.multiple_of(POOL + (d // 2 * SLOTS + slot) * C, C), C)
    return store[rows, d % 2 * 256 : d % 2 * 256 + 256]


def pool_z_at(store, d, slot):
    return store[pl.ds(pl.multiple_of(POOL_Z + (d * 9 + slot) * C, C), C), :]


def dot(left, right, dims=None):
    if dims is None:
        return jnp.dot(left, right, preferred_element_type=F32)
    return lax.dot_general(left, right, dims, preferred_element_type=F32)


def lane_of(shape):
    return lax.broadcasted_iota(jnp.int32, shape, len(shape) - 1)


def parts(block, direction):
    if direction == 0:
        return block[:, 256:512]
    if direction == 1:
        return block[:, 0:256]
    first = 128 if direction == 2 else 0
    return jnp.concatenate([block[:, first : first + 128], block[:, first + 256 : first + 384]], 1)


def roll_blocks(source, put, put_z):
    up = turn_z()
    for k in range(4):
        chunk = source[:, k * 128 : (k + 1) * 128]
        moved = dot(chunk, turn_xy(k)).astype(BF)
        x_dir, y_dir = 1 - k // 2, 3 - k % 2
        put(x_dir, k % 2 * 128, moved[:, 0:128])
        put(y_dir, k // 2 * 128, moved[:, 128:256])
        moved = dot(chunk, up).astype(BF)
        put_z(0, k * 128, moved[:, 0:128])
        put_z(1, k * 128, moved[:, 128:256])


def rim_masks():
    lane = lane_of((C, 256))
    a, b = lane // 16 % 4, lane // 4 % 4
    masks = [a == 0, a == 3, b == 0, b == 3]
    lane = lane_of((C, 512))
    r, c = lane // 64 % 2, lane % 4
    return masks, [(r == 0) & (c == 0), (r == 1) & (c == 3)]


def weave(direction, moved, block):
    if direction == 0:
        return [moved[:, 0:128], moved[:, 128:256], block[:, 0:128], block[:, 128:256]]
    if direction == 1:
        return [block[:, 256:384], block[:, 384:512], moved[:, 0:128], moved[:, 128:256]]
    if direction == 2:
        return [moved[:, 0:128], block[:, 0:128], moved[:, 128:256], block[:, 256:384]]
    return [block[:, 128:256], moved[:, 0:128], block[:, 384:512], moved[:, 128:256]]


def parities():
    return lax.rem(lax.axis_index("gx"), 2), lax.rem(lax.axis_index("gy"), 2)


def load(pairs, sems):
    copies = [pltpu.make_async_copy(src, dst, sems.at[i]) for i, (src, dst) in enumerate(pairs)]
    for copy in copies:
        copy.start()
    return copies


def pack_kernel(
    cmap_hbm, x_hbm, lat_hbm,
    send_xa, send_xb, send_ya, send_yb,
    x_ref, cmap, sems,
):
    copies = load(
        [
            (cmap_hbm, cmap), (x_hbm, x_ref),
            (lat_hbm, send_xa.at[256:768]), (lat_hbm, send_ya.at[256:768]),
        ],
        sems,
    )
    px, py = parities()
    packs = [pack(d) for d in range(4)]
    for copy in copies[:2]:
        copy.wait()
    cube = x_ref[...]
    low = lane_of((256, 128)) < 64
    faces = []
    for d in range(4):
        packed = dot(parts(cube, d), packs[d])
        faces.append(jnp.where(low, packed[0:256], packed[256:512]))
    even = px == 0
    send_xa[0:256, :] = jnp.where(even, faces[0], faces[1]).astype(BF)
    send_xb[...] = jnp.where(even, faces[1], faces[0]).astype(BF)
    even = py == 0
    send_ya[0:256, :] = jnp.where(even, faces[2], faces[3]).astype(BF)
    send_yb[...] = jnp.where(even, faces[3], faces[2]).astype(BF)
    row = lax.broadcasted_iota(jnp.int32, (16, 128), 0)
    named = jnp.zeros((16, 128), jnp.int32)
    for k in range(8):
        named = jnp.where(row == k, cmap[0, k], named)
    named = named.astype(F32).astype(BF)
    send_xa[768:784, :] = named
    send_ya[768:784, :] = named
    for copy in copies[2:]:
        copy.wait()


def prep_kernel(counts, x_hbm, conv_hbm, down_hbm, head_hbm, store, conv, sems):
    copies = load(
        [
            (x_hbm, store.at[XM : XM + 512]),
            (down_hbm, store.at[DOWN : DOWN + 128]),
            (conv_hbm, conv),
            (head_hbm, store.at[DOWN_BACK : DOWN_BACK + 128, 128:256]),
        ],
        sems,
    )
    for d in range(2):
        start = POOL_Z + (d * 9 + SLOTS) * C
        store[start : start + C, :] = jnp.zeros((C, 512), BF)

    def put(d, lane, value):
        rows = slice(POOL + d // 2 * 512, POOL + d // 2 * 512 + 512)
        store[rows, d % 2 * 256 + lane : d % 2 * 256 + lane + 128] = value

    def put_z(d, lane, value):
        start = POOL_Z + d * 9 * C
        store[start : start + 512, lane : lane + 128] = value

    copies[0].wait()
    for b in range(1, SLOTS):
        @pl.when(b >= counts[0])
        def _():
            store[XM + b * C : XM + (b + 1) * C, :] = jnp.zeros((C, 512), BF)
    roll_blocks(store.at[XM : XM + 512], put, put_z)
    copies[1].wait()
    down = store[DOWN : DOWN + 128, :]
    table = regroup()
    store[DOWN : DOWN + 128, :] = dot(down, table, NT).astype(BF)
    store[DOWN_BACK : DOWN_BACK + 512, 0:128] = dot(table, down, NT).astype(BF)
    copies[2].wait()
    store[CONV : CONV + C, 0:448] = conv[...]
    copies[3].wait()


YA, OCT, XA, XB, YB, SEND = 0, 256, 768, 1024, 1280, 1536


def main_kernel(
    nb_hbm, cmap_hbm, lat_hbm,
    got_xa, got_xb, got_ya, got_yb, got_xy, store,
    hg_ref, mine_ref, other_ref, send,
    nb, cmap, sems, sums_ref, lat_ref, reach, taps, hg_row, slope, act2, routed, far, maps_v, maps_s, sem,
):
    px, py = parities()
    for j, got in enumerate((got_xa, got_ya, got_xy)):
        maps_v[j] = got[768:784, :].astype(F32).astype(jnp.int32)
    copy = pltpu.make_async_copy(maps_v, maps_s, sem)
    copy.start()
    copies = load([(nb_hbm, nb), (cmap_hbm, cmap), (lat_hbm, lat_ref)], sems)
    head = store[DOWN_BACK : DOWN_BACK + 128, 128:256]

    spreads = [spread(axis) for axis in range(2)]
    for got, axis, direction in (
        (got_xa, 0, 1 - px), (got_xb, 0, px), (got_ya, 1, 3 - py), (got_yb, 1, 2 + py),
    ):
        wide = dot(got[0:256, :], spreads[axis]).astype(BF)
        if got is got_xb or got is got_yb:
            wide = jnp.where(inner(("gx", "gy")[axis]), wide, jnp.zeros_like(wide))
        wide = wide.reshape(4, C, 512)
        reach[direction, 8:12] = wide[:, :, 0:256]
        reach[direction, 12:16] = wide[:, :, 256:512]
    for d in range(4):
        for b in range(SLOTS):
            reach[d, b] = pool_at(store, d, b)
        reach[d, 16] = jnp.zeros((C, 256), BF)

    masks, masks_z = rim_masks()
    low = lane_of((C, 128)) < 64
    copies[0].wait()
    conv = store[CONV : CONV + C, 0:448]
    for pair in range(SLOTS // 2):
        acts = []
        for b in (2 * pair, 2 * pair + 1):
            block = store[XM + b * C : XM + (b + 1) * C, :]
            at = b * 512
            taps[0:C, at : at + 512] = block
            for d in range(4):
                moved = jnp.where(masks[d], reach[d, nb[b, d]], reach[d, b])
                for k, piece in enumerate(weave(d, moved, block)):
                    lanes = slice(at + k * 128, at + (k + 1) * 128)
                    taps[(d + 1) * C : (d + 2) * C, lanes] = piece
            for d in range(2):
                near = jnp.minimum(nb[b, d + 4], SLOTS)
                taps[(d + 5) * C : (d + 6) * C, at : at + 512] = jnp.where(
                    masks_z[d], pool_z_at(store, d, near), pool_z_at(store, d, b)
                )
            hidden = dot(conv, taps[:, at : at + 512])
            gate = 0.5 * jnp.tanh(0.5 * hidden) + 0.5
            slope[b] = gate * (1.0 + hidden * (1.0 - gate))
            acts.append(hidden * gate)
        lanes = slice(pair * 128, (pair + 1) * 128)
        for k in range(4):
            one, two = (v[:, k * 128 : (k + 1) * 128] for v in acts)
            first = jnp.where(low, one, pltpu.roll(two, 64, 1))
            second = jnp.where(low, pltpu.roll(one, 64, 1), two)
            act2[2 * k * C : (2 * k + 1) * C, lanes] = first.astype(BF)
            act2[(2 * k + 1) * C : (2 * k + 2) * C, lanes] = second.astype(BF)

    octants = dot(store[DOWN : DOWN + 128, :], act2[...]).astype(BF).astype(F32)
    gate = 0.5 * jnp.tanh(0.5 * octants) + 0.5
    oct_act = (octants * gate).astype(BF)
    oct_slope = gate * (1.0 + octants * (1.0 - gate))
    projected = dot(head, oct_act).T.astype(BF)
    send[OCT : OCT + 512, :] = projected

    copy.wait()
    copies[1].wait()
    copies[2].wait()
    for s in range(SLOTS):
        routed[s] = jnp.zeros((C, 128), BF)
    for j, (got, start) in enumerate(((lat_ref, 0), (got_xa, 256), (got_ya, 256), (got_xy, 256))):
        for k in range(8):
            name = cmap[0, k] if j == 0 else maps_s[j - 1, k, 0]
            name = name - j * SLOTS
            name = jnp.where((name >= 0) & (name < SLOTS), name, SLOTS)
            routed[name] = got[start + k * C : start + (k + 1) * C, :]
    grad = routed[0:SLOTS].reshape(SLOTS * C, 128)
    head_back = head.astype(F32).T.astype(BF)
    oct_grad = (dot(head_back, grad, NT) * oct_slope).astype(BF)
    sums_ref[736:864, :] = dot(oct_act, grad).T
    down_sum = dot(oct_grad, act2[...], NT)
    for k in range(4):
        sums_ref[224 + k * 128 : 224 + (k + 1) * 128, :] = down_sum[:, k * 128 : (k + 1) * 128]
    for pair in range(SLOTS // 2):
        patch = dot(store[DOWN_BACK : DOWN_BACK + 512, 0:128], oct_grad[:, pair * 128 : (pair + 1) * 128])
        for side in range(2):
            b = 2 * pair + side
            for k in range(4):
                first = patch[2 * k * C : (2 * k + 1) * C]
                second = patch[(2 * k + 1) * C : (2 * k + 2) * C]
                if side == 0:
                    both = jnp.where(low, first, pltpu.roll(second, 64, 1))
                else:
                    both = jnp.where(low, pltpu.roll(first, 64, 1), second)
                lanes = slice(k * 128, (k + 1) * 128)
                both = (both * slope[b, :, lanes]).astype(BF)
                hg_ref[b * C : (b + 1) * C, lanes] = both
                hg_row[:, b * 512 + k * 128 : b * 512 + (k + 1) * 128] = both
    conv_sum = dot(hg_row[...], taps[...], NT)
    for k in range(3):
        sums_ref[k * C : (k + 1) * C, :] = conv_sum[:, k * 128 : (k + 1) * 128]
    sums_ref[192:224, :] = jnp.concatenate([conv_sum[0:32, 384:448], conv_sum[32:64, 384:448]], 1)

    first, second = sums_ref[0:432, :].astype(BF), sums_ref[432:864, :].astype(BF)
    even = parity() == 0
    mine_ref[...] = jnp.where(even, first, second)
    other_ref[...] = jnp.where(even, second, first)

    for d in range(4):
        for s in range(5):
            far[d, s] = jnp.zeros((C, 128), F32)
    high = lane_of((C, 128)) // 64
    for d in range(4):
        face = dot(parts(hg_ref[...], d ^ 1), pack(d ^ 1))
        for b in range(SLOTS):
            name = nb[b, d] - SLOTS
            away = (name >= 0) & (name < SLOTS)
            row = jnp.where(away, lax.rem(name, 4), 4)
            side = jnp.where(name >= 4, 1, 0)
            far[d, row] += jnp.where(high == side, face[b * C : (b + 1) * C, :], 0.0)
    for at, d in ((XA, 1 - px), (XB, px), (YA, 3 - py), (YB, 2 + py)):
        send[at : at + 256, :] = far[d, 0:4].reshape(256, 128).astype(BF)


def roll_kernel(nb_hbm, hg_ref, moved_ref, pool, pool_z, total, total_z, nb, sem):
    copy = pltpu.make_async_copy(nb_hbm, nb, sem)
    copy.start()

    def put(d, lane, value):
        pool[d, :, :, lane : lane + 128] = value.reshape(SLOTS, C, 128)

    def put_z(d, lane, value):
        pool_z[d, :, :, lane : lane + 128] = value.reshape(SLOTS, C, 128)

    roll_blocks(hg_ref, put, put_z)
    for s in range(SLOTS):
        for d in range(4):
            total[d, s] = jnp.zeros((C, 256), F32)
        for d in range(2):
            total_z[d, s] = jnp.zeros((C, 512), F32)
    copy.wait()
    for b in range(SLOTS):
        for d in range(4):
            slot = jnp.minimum(nb[b, d], SLOTS)
            total[d, slot] += pool[d ^ 1, b].astype(F32)
        for d in range(2):
            slot = jnp.minimum(nb[b, d + 4], SLOTS)
            total_z[d, slot] += pool_z[1 - d, b].astype(F32)
    masks, masks_z = rim_masks()
    for b in range(SLOTS):
        for d in range(4):
            rows = slice((d // 2 * SLOTS + b) * C, (d // 2 * SLOTS + b + 1) * C)
            moved_ref[rows, d % 2 * 256 : d % 2 * 256 + 256] = jnp.where(
                masks[d ^ 1], total[d, b].astype(BF), pool[d ^ 1, b]
            )
        for d in range(2):
            rows = slice(((d + 2) * SLOTS + b) * C, ((d + 2) * SLOTS + b + 1) * C)
            moved_ref[rows, :] = jnp.where(
                masks_z[1 - d], total_z[d, b].astype(BF), pool_z[1 - d, b]
            )


def near_kernel(hg_ref, moved_ref, conv_ref, near_ref, fields):
    conv = jnp.concatenate([conv_ref[:, d * C : (d + 1) * C] for d in range(7)], 0)
    for b in range(SLOTS):
        block = hg_ref[b * C : (b + 1) * C, :]
        fields[0:C, :] = block
        for d in range(4):
            rows = slice((d // 2 * SLOTS + b) * C, (d // 2 * SLOTS + b + 1) * C)
            moved = moved_ref[rows, d % 2 * 256 : d % 2 * 256 + 256]
            for k, piece in enumerate(weave(d ^ 1, moved, block)):
                fields[(d + 1) * C : (d + 2) * C, k * 128 : (k + 1) * 128] = piece
        for d in range(2):
            rows = slice(((d + 2) * SLOTS + b) * C, ((d + 2) * SLOTS + b + 1) * C)
            fields[(d + 5) * C : (d + 6) * C, :] = moved_ref[rows, :]
        near_ref[b * C : (b + 1) * C, :] = dot(conv, fields[...], TN)


def far_kernel(counts, near_ref, got_xa, got_xb, got_ya, got_yb, conv_ref, out_ref, rows):
    px, py = parities()
    for got, direction in ((got_xa, px), (got_xb, 1 - px), (got_ya, 2 + py), (got_yb, 3 - py)):
        value = got[0:256, :]
        if got is got_xb or got is got_yb:
            value = jnp.where(inner("gx" if got is got_xb else "gy"), value, jnp.zeros_like(value))
        rows[direction] = value
    fields = []
    for d in range(4):
        conv = conv_ref[:, (d + 1) * C : (d + 2) * C]
        moved = [dot(conv, rows[d, k * C : (k + 1) * C, :], TN).astype(BF) for k in range(4)]
        table = spread(d // 2, 3 * (1 - d % 2))
        fields.append(dot(jnp.concatenate(moved, 0), table))
    for b in range(SLOTS):
        x_low, x_high, y_low, y_high = (
            fields[d][b % 4 * C : (b % 4 + 1) * C, b // 4 * 256 : b // 4 * 256 + 256]
            for d in (1, 0, 3, 2)
        )
        for k in range(4):
            lanes = slice(k * 128, (k + 1) * 128)
            x, y = (x_low, x_high)[k // 2], (y_low, y_high)[k % 2]
            x, y = (v[:, i * 128 : (i + 1) * 128] for v, i in ((x, k % 2), (y, k // 2)))
            grad = near_ref[b * C : (b + 1) * C, lanes] + (x + y)
            out_ref[b * C : (b + 1) * C, lanes] = jnp.where(b < counts[0], grad, 0.0).astype(BF)


def latent_kernel(cmap, own, got_x, got_ya, got_xy, out_ref, rows):
    rows[0:8] = own[OCT : OCT + 512, :].reshape(8, C, 128)
    rows[8:16] = got_x[...].reshape(8, C, 128)
    rows[16:24] = got_ya[256:768, :].reshape(8, C, 128)
    rows[24:32] = got_xy[...].reshape(8, C, 128)
    rows[32] = jnp.zeros((C, 128), BF)
    for k in range(8):
        out_ref[k * C : (k + 1) * C, :] = rows[cmap[0, k]]


def scale_kernel(scale, mine, theirs, conv_out, down_out, head_out):
    even = parity() == 0
    conv_in = jnp.concatenate(
        [
            jnp.where(even, mine[...], theirs[...]),
            jnp.where(even, theirs[...], mine[...]),
        ],
        0,
    )
    for k in range(3):
        conv_out[:, k * 128 : (k + 1) * 128] = conv_in[k * C : (k + 1) * C, :].astype(F32) * scale
    last = conv_in[192:224, :].astype(F32) * scale
    conv_out[0:32, 384:448] = last[:, 0:64]
    conv_out[32:64, 384:448] = last[:, 64:128]
    down = jnp.concatenate([conv_in[224 + k * 128 : 352 + k * 128, :] for k in range(4)], 1)
    down_out[...] = dot(down, regroup()) * scale
    head_out[...] = conv_in[736:864, :].astype(F32) * scale


def route(there):
    nx, ny = lax.axis_size("gx"), lax.axis_size("gy")
    pairs = []
    for i in range(nx):
        for j in range(ny):
            x, y = there(i, j)
            pairs.append((i * ny + j, x * ny + y))
    return pairs


def send_to(value, there):
    return lax.ppermute(value, ("gx", "gy"), route(there))


def beside_x(value):
    return send_to(value, lambda i, j: (i ^ 1, j))


def beside_core(value):
    return send_to(value, lambda i, j: (i, j ^ 1))


def beside_both(value):
    return send_to(value, lambda i, j: (i ^ 1, j ^ 1))


def odd_partner(i, count):
    return min(max(i + 2 * (i % 2) - 1, -1), count)


def odd_x(value):
    nx = lax.axis_size("gx")
    return send_to(value, lambda i, j: (odd_partner(i, nx), j) if 0 < i < nx - 1 else (i, j ^ 1))


def odd_y(value):
    ny = lax.axis_size("gy")
    return send_to(value, lambda i, j: (i, odd_partner(j, ny) if 0 < j < ny - 1 else ny - 1 - j))


def inner(axis):
    at = lax.axis_index(axis)
    return (at > 0) & (at < lax.axis_size(axis) - 1)


def parity():
    bits = lax.axis_index("gx") * lax.axis_size("gy") + lax.axis_index("gy")
    count = 0
    for k in range((lax.axis_size("gx") * lax.axis_size("gy") - 1).bit_length()):
        count = count + lax.rem(lax.div(bits, 1 << k), 2)
    return lax.rem(count, 2)


def tie(value, *others):
    return lax.optimization_barrier((value, *others))[0]


def weight_sums(mine, other):
    bits = []
    for axis, first in (("gy", 2), ("gx", 1)):
        bit = first
        while bit < lax.axis_size(axis):
            bits.append((axis, bit))
            bit *= 2
    if len(bits) > 2:
        bits.insert(1, bits.pop(2))
    turned = []
    for at in range(0, len(bits) - 1, 2):
        turned += [bits[at + 1], bits[at]]
    turned += bits[len(turned) :]
    state = {"sum": mine}

    def there(at, i, j):
        axis, bit = (bits, turned)[(i.bit_count() + j.bit_count()) % 2][at]
        return (i ^ bit, j ^ 1) if axis == "gx" else (i, j ^ bit ^ 1)

    def step(at, waits):
        sent = tie(state["sum"], *waits) if waits else state["sum"]
        if at > len(bits):
            return sent, beside_core(sent)
        if at == 0:
            got = beside_core(other)
        else:
            got = send_to(sent, lambda i, j: there(at - 1, i, j))
        state["sum"] = (sent.astype(F32) + got.astype(F32)).astype(BF)
        return state["sum"]

    return step, len(bits) + 1


def call(kernel, outs, ins, spaces="", scratch=(), last=0, us=1.0):
    kinds = {"s": pltpu.SMEM, "h": pltpu.HBM, "v": pltpu.VMEM}
    spaces = spaces + "v" * (len(ins) - len(spaces))
    ins = [
        pltpu.with_memory_space_constraint(value, pltpu.HBM) if space == "h" else value
        for value, space in zip(ins, spaces)
    ]
    keep = len(outs) - last
    return pl.pallas_call(
        kernel,
        out_shape=[
            pltpu.VMEM(shape, kind) if at < keep else jax.ShapeDtypeStruct(shape, kind)
            for at, (shape, kind) in enumerate(outs)
        ],
        in_specs=[pl.BlockSpec(memory_space=kinds[k]) for k in spaces],
        out_specs=[pl.BlockSpec(memory_space=pltpu.VMEM)] * len(outs),
        scratch_shapes=list(scratch),
        compiler_params=pltpu.CompilerParams(vmem_limit_bytes=32 * 1024 * 1024),
        cost_estimate=pl.CostEstimate(
            flops=int(us * 1e9), bytes_accessed=int(us * 3e6), transcendentals=0
        ),
    )(*ins)


def body(
    features, neighbours, counts, conv_weight, down_weight, head_weight, coarse_map, latent_grad
):
    flat = features.reshape(SLOTS * C, 512)
    lat = latent_grad.reshape(512, 128)
    send_xa, send_xb, send_ya, send_yb = call(
        pack_kernel,
        [
            ((784, 128), BF), ((256, 128), BF), ((784, 128), BF), ((256, 128), BF),
        ],
        (coarse_map, flat, lat),
        "hhh",
        [pltpu.VMEM((512, 512), BF), pltpu.SMEM((1, 8), jnp.int32), pltpu.SemaphoreType.DMA((4,))],
        us=1.5,
    )
    got_xy = beside_both(send_xa)
    got_xb = odd_x(send_xb)
    got_ya = beside_core(send_ya)
    got_yb = odd_y(send_yb)
    (store,) = call(
        prep_kernel,
        [((STORE, 512), BF)],
        (counts, flat, conv_weight, down_weight, head_weight),
        "shhhh",
        [pltpu.VMEM((C, 448), BF), pltpu.SemaphoreType.DMA((4,))],
        us=1.5,
    )
    got_xa = beside_core(tie(got_xy, got_xb, got_yb, got_ya, store))
    hg, mine, other, send = call(
        main_kernel,
        [((512, 512), BF), ((432, 128), BF), ((432, 128), BF), ((SEND, 128), BF)],
        (neighbours, coarse_map, lat, got_xa, got_xb, got_ya, got_yb, got_xy, store),
        "hhh",
        [
            pltpu.SMEM((SLOTS, 6), jnp.int32),
            pltpu.SMEM((1, 8), jnp.int32),
            pltpu.SemaphoreType.DMA((3,)),
            pltpu.VMEM((864, 128), F32),
            pltpu.VMEM((512, 128), BF),
            pltpu.VMEM((4, 17, C, 256), BF),
            pltpu.VMEM((448, SLOTS * 512), BF),
            pltpu.VMEM((C, SLOTS * 512), BF),
            pltpu.VMEM((SLOTS, C, 512), F32),
            pltpu.VMEM((512, 512), BF),
            pltpu.VMEM((SLOTS + 1, C, 128), BF),
            pltpu.VMEM((4, 5, C, 128), F32),
            pltpu.VMEM((3, 16, 128), jnp.int32),
            pltpu.SMEM((3, 16, 128), jnp.int32),
            pltpu.SemaphoreType.DMA,
        ],
        us=6.0,
    )

    sum_step, steps = weight_sums(mine, other)
    mine = sum_step(0, ())
    got_xa = beside_x(tie(send[XA : XA + 256], mine))
    got_xb = odd_x(send[XB : XB + 256])
    got_yb = odd_y(tie(send[YB : YB + 256], mine))
    mine = sum_step(1, ())
    got_ya = beside_core(tie(send[YA : OCT + 512], mine))
    (moved,) = call(
        roll_kernel,
        [((2048, 512), BF)],
        (neighbours, tie(hg, mine, got_xb)),
        "h",
        [
            pltpu.VMEM((4, 8, C, 256), BF),
            pltpu.VMEM((2, 8, C, 512), BF),
            pltpu.VMEM((4, 9, C, 256), F32),
            pltpu.VMEM((2, 9, C, 512), F32),
            pltpu.SMEM((SLOTS, 6), jnp.int32),
            pltpu.SemaphoreType.DMA,
        ],
        us=2.5,
    )
    mine = sum_step(2, ())
    (near,) = call(
        near_kernel,
        [((512, 512), F32)],
        (hg, tie(moved, mine), conv_weight),
        "",
        [pltpu.VMEM((448, 512), BF)],
        us=1.0,
    )
    got_xy = beside_both(tie(send[OCT : OCT + 512], near))
    mine = sum_step(3, (moved, got_ya, got_xa, got_yb, got_xb,))
    (grad,) = call(
        far_kernel,
        [((512, 512), BF)],
        (counts, tie(near, mine), got_xa, got_xb, got_ya, got_yb, conv_weight),
        "s",
        [pltpu.VMEM((4, 256, 128), BF)],
        1,
        us=1.8,
    )
    got_x = beside_core(tie(got_xy, mine))
    (latent,) = call(
        latent_kernel,
        [((512, 128), BF)],
        (coarse_map, send, got_x, got_ya, got_xy),
        "s",
        [pltpu.VMEM((33, C, 128), BF)],
        1,
        us=1.2,
    )
    mine = sum_step(4, (near,))
    for at in range(5, steps):
        mine = sum_step(at, ())
    mine, theirs = sum_step(steps, (grad, got_x,))
    scale = float(SLOTS * lax.axis_size("gx") * lax.axis_size("gy")) ** (-0.5)
    conv_grad, down_grad, head_grad = call(
        lambda *refs: scale_kernel(scale, *refs),
        [((C, 448), F32), ((128, 512), F32), ((128, 128), F32)],
        (mine, theirs),
        last=3,
    )
    return (
        latent.reshape(1, 512, 128), grad.reshape(SLOTS, C, 512), conv_grad, down_grad, head_grad,
    )


def solution(mesh):
    both = ("gx", "gy")
    placed = (
        P(both, None, None), P(both, None), P(both), P(), P(), P(), P(both, None),
        P(both, None, None),
    )
    return jax.shard_map(
        body,
        mesh=mesh,
        in_specs=placed,
        out_specs=(P(both, None, None), P(both, None, None), P(), P(), P()),
        check_vma=False,
    )
```

```python
import jax
import jax.numpy as jnp
from jax import lax
from jax.experimental import pallas as pl
from jax.experimental.pallas import tpu as pltpu
from jax.sharding import PartitionSpec as P

BF = jnp.bfloat16
F32 = jnp.float32
C = 64
SLOTS = 8
NT = (((1,), (1,)), ((), ()))
TN = (((0,), (0,)), ((), ()))


def one_hot(source, rows):
    row = lax.broadcasted_iota(jnp.int32, (rows, source.shape[1]), 0)
    return jnp.where(row == source, 1.0, 0.0).astype(BF)


def lanes_of(count):
    lane = lax.broadcasted_iota(jnp.int32, (1, count), 1)
    return lane, lane // 64 % 2, lane // 16 % 4, lane // 4 % 4, lane % 4


def cell(r, a, b, c):
    return r * 64 + (a + 4) % 4 * 16 + (b + 4) % 4 * 4 + (c + 4) % 4


def turn_z():
    lane, r, a, b, c = lanes_of(256)
    step = jnp.where(lane < 128, jnp.where(r == 0, -1, 0), jnp.where(r == 1, 1, 0))
    return one_hot(cell(1 - r, a, b, c + step), 128)


def turn_xy(k):
    lane, r, a, b, c = lanes_of(256)
    x = 1 - 2 * (k // 2)
    y = 1 - 2 * (k % 2)
    first = lane < 128
    return one_hot(cell(r, a + jnp.where(first, x, 0), b + jnp.where(first, 0, y), c), 128)


def spread(axis, want=None):
    lane, r, a, b, c = lanes_of(512)
    place, other = (a, b) if axis == 0 else (b, a)
    source = lane // 256 * 64 + lane // 128 % 2 * 32 + r * 16 + other * 4 + c
    if want is not None:
        source = jnp.where(place == want, source, -1)
    return one_hot(source, 128)


def pack(direction):
    lane = lanes_of(128)[0] % 64
    want = 3 * (1 - direction % 2)
    half, r, other, c = lane // 32, lane // 16 % 2, lane // 4 % 4, lane % 4
    a, b = (want, other) if direction < 2 else (other, want)
    return one_hot(half * 128 + cell(r, a, b, c), 256)


def regroup():
    lane = lanes_of(512)[0]
    return one_hot(lane % 8 * 64 + lane // 8, 512)


CONV, DOWN, DOWN_BACK, POOL, POOL_Z, XM, STORE = 0, 64, 192, 704, 1728, 2880, 3392


def pool_at(store, d, slot):
    rows = pl.ds(pl.multiple_of(POOL + (d // 2 * SLOTS + slot) * C, C), C)
    return store[rows, d % 2 * 256 : d % 2 * 256 + 256]


def pool_z_at(store, d, slot):
    return store[pl.ds(pl.multiple_of(POOL_Z + (d * 9 + slot) * C, C), C), :]


def dot(left, right, dims=None):
    if dims is None:
        return jnp.dot(left, right, preferred_element_type=F32)
    return lax.dot_general(left, right, dims, preferred_element_type=F32)


def lane_of(shape):
    return lax.broadcasted_iota(jnp.int32, shape, len(shape) - 1)


def parts(block, direction):
    if direction == 0:
        return block[:, 256:512]
    if direction == 1:
        return block[:, 0:256]
    first = 128 if direction == 2 else 0
    return jnp.concatenate([block[:, first : first + 128], block[:, first + 256 : first + 384]], 1)


def roll_blocks(source, put, put_z):
    up = turn_z()
    for k in range(4):
        chunk = source[:, k * 128 : (k + 1) * 128]
        moved = dot(chunk, turn_xy(k)).astype(BF)
        x_dir, y_dir = 1 - k // 2, 3 - k % 2
        put(x_dir, k % 2 * 128, moved[:, 0:128])
        put(y_dir, k // 2 * 128, moved[:, 128:256])
        moved = dot(chunk, up).astype(BF)
        put_z(0, k * 128, moved[:, 0:128])
        put_z(1, k * 128, moved[:, 128:256])


def rim_masks():
    lane = lane_of((C, 256))
    a, b = lane // 16 % 4, lane // 4 % 4
    masks = [a == 0, a == 3, b == 0, b == 3]
    lane = lane_of((C, 512))
    r, c = lane // 64 % 2, lane % 4
    return masks, [(r == 0) & (c == 0), (r == 1) & (c == 3)]


def weave(direction, moved, block):
    if direction == 0:
        return [moved[:, 0:128], moved[:, 128:256], block[:, 0:128], block[:, 128:256]]
    if direction == 1:
        return [block[:, 256:384], block[:, 384:512], moved[:, 0:128], moved[:, 128:256]]
    if direction == 2:
        return [moved[:, 0:128], block[:, 0:128], moved[:, 128:256], block[:, 256:384]]
    return [block[:, 128:256], moved[:, 0:128], block[:, 384:512], moved[:, 128:256]]


def parities():
    return lax.rem(lax.axis_index("gx"), 2), lax.rem(lax.axis_index("gy"), 2)


def load(pairs, sems):
    copies = [pltpu.make_async_copy(src, dst, sems.at[i]) for i, (src, dst) in enumerate(pairs)]
    for copy in copies:
        copy.start()
    return copies


def pack_kernel(
    cmap_hbm, x_hbm, lat_hbm,
    send_xa, send_xb, send_ya, send_yb,
    x_ref, cmap, sems,
):
    copies = load(
        [
            (cmap_hbm, cmap), (x_hbm, x_ref),
            (lat_hbm, send_xa.at[256:768]), (lat_hbm, send_ya.at[256:768]),
        ],
        sems,
    )
    px, py = parities()
    packs = [pack(d) for d in range(4)]
    for copy in copies[:2]:
        copy.wait()
    cube = x_ref[...]
    low = lane_of((256, 128)) < 64
    faces = []
    for d in range(4):
        packed = dot(parts(cube, d), packs[d])
        faces.append(jnp.where(low, packed[0:256], packed[256:512]))
    even = px == 0
    send_xa[0:256, :] = jnp.where(even, faces[0], faces[1]).astype(BF)
    send_xb[...] = jnp.where(even, faces[1], faces[0]).astype(BF)
    even = py == 0
    send_ya[0:256, :] = jnp.where(even, faces[2], faces[3]).astype(BF)
    send_yb[...] = jnp.where(even, faces[3], faces[2]).astype(BF)
    row = lax.broadcasted_iota(jnp.int32, (16, 128), 0)
    named = jnp.zeros((16, 128), jnp.int32)
    for k in range(8):
        named = jnp.where(row == k, cmap[0, k], named)
    named = named.astype(F32).astype(BF)
    send_xa[768:784, :] = named
    send_ya[768:784, :] = named
    for copy in copies[2:]:
        copy.wait()


def prep_kernel(counts, x_hbm, conv_hbm, down_hbm, head_hbm, store, conv, sems):
    copies = load(
        [
            (x_hbm, store.at[XM : XM + 512]),
            (down_hbm, store.at[DOWN : DOWN + 128]),
            (conv_hbm, conv),
            (head_hbm, store.at[DOWN_BACK : DOWN_BACK + 128, 128:256]),
        ],
        sems,
    )
    for d in range(2):
        start = POOL_Z + (d * 9 + SLOTS) * C
        store[start : start + C, :] = jnp.zeros((C, 512), BF)

    def put(d, lane, value):
        rows = slice(POOL + d // 2 * 512, POOL + d // 2 * 512 + 512)
        store[rows, d % 2 * 256 + lane : d % 2 * 256 + lane + 128] = value

    def put_z(d, lane, value):
        start = POOL_Z + d * 9 * C
        store[start : start + 512, lane : lane + 128] = value

    copies[0].wait()
    for b in range(1, SLOTS):
        @pl.when(b >= counts[0])
        def _():
            store[XM + b * C : XM + (b + 1) * C, :] = jnp.zeros((C, 512), BF)
    roll_blocks(store.at[XM : XM + 512], put, put_z)
    copies[1].wait()
    down = store[DOWN : DOWN + 128, :]
    table = regroup()
    store[DOWN : DOWN + 128, :] = dot(down, table, NT).astype(BF)
    store[DOWN_BACK : DOWN_BACK + 512, 0:128] = dot(table, down, NT).astype(BF)
    copies[2].wait()
    store[CONV : CONV + C, 0:448] = conv[...]
    copies[3].wait()


YA, OCT, XA, XB, YB, SEND = 0, 256, 768, 1024, 1280, 1536


def main_kernel(
    nb_hbm, cmap_hbm, lat_hbm,
    got_xa, got_xb, got_ya, got_yb, got_xy, store,
    hg_ref, mine_ref, other_ref, send,
    nb, cmap, sems, sums_ref, lat_ref, reach, taps, hg_row, slope, act2, routed, far, maps_v, maps_s, sem,
):
    px, py = parities()
    for j, got in enumerate((got_xa, got_ya, got_xy)):
        maps_v[j] = got[768:784, :].astype(F32).astype(jnp.int32)
    copy = pltpu.make_async_copy(maps_v, maps_s, sem)
    copy.start()
    copies = load([(nb_hbm, nb), (cmap_hbm, cmap), (lat_hbm, lat_ref)], sems)
    head = store[DOWN_BACK : DOWN_BACK + 128, 128:256]

    spreads = [spread(axis) for axis in range(2)]
    for got, axis, direction in (
        (got_xa, 0, 1 - px), (got_xb, 0, px), (got_ya, 1, 3 - py), (got_yb, 1, 2 + py),
    ):
        wide = dot(got[0:256, :], spreads[axis]).astype(BF)
        if got is got_xb or got is got_yb:
            wide = jnp.where(inner(("gx", "gy")[axis]), wide, jnp.zeros_like(wide))
        wide = wide.reshape(4, C, 512)
        reach[direction, 8:12] = wide[:, :, 0:256]
        reach[direction, 12:16] = wide[:, :, 256:512]
    for d in range(4):
        for b in range(SLOTS):
            reach[d, b] = pool_at(store, d, b)
        reach[d, 16] = jnp.zeros((C, 256), BF)

    masks, masks_z = rim_masks()
    low = lane_of((C, 128)) < 64
    copies[0].wait()
    conv = store[CONV : CONV + C, 0:448]
    for pair in range(SLOTS // 2):
        acts = []
        for b in (2 * pair, 2 * pair + 1):
            block = store[XM + b * C : XM + (b + 1) * C, :]
            at = b * 512
            taps[0:C, at : at + 512] = block
            for d in range(4):
                moved = jnp.where(masks[d], reach[d, nb[b, d]], reach[d, b])
                for k, piece in enumerate(weave(d, moved, block)):
                    lanes = slice(at + k * 128, at + (k + 1) * 128)
                    taps[(d + 1) * C : (d + 2) * C, lanes] = piece
            for d in range(2):
                near = jnp.minimum(nb[b, d + 4], SLOTS)
                taps[(d + 5) * C : (d + 6) * C, at : at + 512] = jnp.where(
                    masks_z[d], pool_z_at(store, d, near), pool_z_at(store, d, b)
                )
        both = dot(conv, taps[:, pair * 1024 : pair * 1024 + 1024])
        for b in (2 * pair, 2 * pair + 1):
            hidden = both[:, b % 2 * 512 : b % 2 * 512 + 512]
            gate = 0.5 * jnp.tanh(0.5 * hidden) + 0.5
            slope[b] = gate * (1.0 + hidden * (1.0 - gate))
            acts.append(hidden * gate)
        lanes = slice(pair * 128, (pair + 1) * 128)
        for k in range(4):
            one, two = (v[:, k * 128 : (k + 1) * 128] for v in acts)
            first = jnp.where(low, one, pltpu.roll(two, 64, 1))
            second = jnp.where(low, pltpu.roll(one, 64, 1), two)
            act2[2 * k * C : (2 * k + 1) * C, lanes] = first.astype(BF)
            act2[(2 * k + 1) * C : (2 * k + 2) * C, lanes] = second.astype(BF)

    octants = dot(store[DOWN : DOWN + 128, :], act2[...]).astype(BF).astype(F32)
    gate = 0.5 * jnp.tanh(0.5 * octants) + 0.5
    oct_act = (octants * gate).astype(BF)
    oct_slope = gate * (1.0 + octants * (1.0 - gate))
    projected = dot(head, oct_act).T.astype(BF)
    send[OCT : OCT + 512, :] = projected

    copy.wait()
    copies[1].wait()
    copies[2].wait()
    for s in range(SLOTS):
        routed[s] = jnp.zeros((C, 128), BF)
    for j, (got, start) in enumerate(((lat_ref, 0), (got_xa, 256), (got_ya, 256), (got_xy, 256))):
        for k in range(8):
            name = cmap[0, k] if j == 0 else maps_s[j - 1, k, 0]
            name = name - j * SLOTS
            name = jnp.where((name >= 0) & (name < SLOTS), name, SLOTS)
            routed[name] = got[start + k * C : start + (k + 1) * C, :]
    grad = routed[0:SLOTS].reshape(SLOTS * C, 128)
    head_back = head.astype(F32).T.astype(BF)
    oct_grad = (dot(head_back, grad, NT) * oct_slope).astype(BF)
    sums_ref[768:896, :] = dot(oct_act, grad).T
    down_sum = dot(oct_grad, act2[...], NT)
    for k in range(4):
        sums_ref[256 + k * 128 : 256 + (k + 1) * 128, :] = down_sum[:, k * 128 : (k + 1) * 128]
    for pair in range(SLOTS // 2):
        patch = dot(store[DOWN_BACK : DOWN_BACK + 512, 0:128], oct_grad[:, pair * 128 : (pair + 1) * 128])
        for side in range(2):
            b = 2 * pair + side
            for k in range(4):
                first = patch[2 * k * C : (2 * k + 1) * C]
                second = patch[(2 * k + 1) * C : (2 * k + 2) * C]
                if side == 0:
                    both = jnp.where(low, first, pltpu.roll(second, 64, 1))
                else:
                    both = jnp.where(low, pltpu.roll(first, 64, 1), second)
                lanes = slice(k * 128, (k + 1) * 128)
                both = (both * slope[b, :, lanes]).astype(BF)
                hg_ref[b * C : (b + 1) * C, lanes] = both
                hg_row[:, b * 512 + k * 128 : b * 512 + (k + 1) * 128] = both
    conv_sum = dot(hg_row[...], taps[...], NT)
    for k in range(3):
        sums_ref[k * C : (k + 1) * C, :] = conv_sum[:, k * 128 : (k + 1) * 128]
    sums_ref[3 * C : 4 * C, 0:C] = conv_sum[:, 384:448]
    sums_ref[3 * C : 4 * C, C:128] = jnp.zeros((C, C), F32)

    first, second = sums_ref[0:448, :].astype(BF), sums_ref[448:896, :].astype(BF)
    even = parity() == 0
    mine_ref[...] = jnp.where(even, first, second)
    other_ref[...] = jnp.where(even, second, first)

    for d in range(4):
        for s in range(5):
            far[d, s] = jnp.zeros((C, 128), F32)
    high = lane_of((C, 128)) // 64
    for d in range(4):
        face = dot(parts(hg_ref[...], d ^ 1), pack(d ^ 1))
        for b in range(SLOTS):
            name = nb[b, d] - SLOTS
            away = (name >= 0) & (name < SLOTS)
            row = jnp.where(away, lax.rem(name, 4), 4)
            side = jnp.where(name >= 4, 1, 0)
            far[d, row] += jnp.where(high == side, face[b * C : (b + 1) * C, :], 0.0)
    for at, d in ((XA, 1 - px), (XB, px), (YA, 3 - py), (YB, 2 + py)):
        send[at : at + 256, :] = far[d, 0:4].reshape(256, 128).astype(BF)


def roll_kernel(nb_hbm, hg_ref, moved_ref, pool, pool_z, total, total_z, nb, sem):
    copy = pltpu.make_async_copy(nb_hbm, nb, sem)
    copy.start()

    def put(d, lane, value):
        pool[d, :, :, lane : lane + 128] = value.reshape(SLOTS, C, 128)

    def put_z(d, lane, value):
        pool_z[d, :, :, lane : lane + 128] = value.reshape(SLOTS, C, 128)

    roll_blocks(hg_ref, put, put_z)
    for s in range(SLOTS):
        for d in range(4):
            total[d, s] = jnp.zeros((C, 256), F32)
        for d in range(2):
            total_z[d, s] = jnp.zeros((C, 512), F32)
    copy.wait()
    for b in range(SLOTS):
        for d in range(4):
            slot = jnp.minimum(nb[b, d], SLOTS)
            total[d, slot] += pool[d ^ 1, b].astype(F32)
        for d in range(2):
            slot = jnp.minimum(nb[b, d + 4], SLOTS)
            total_z[d, slot] += pool_z[1 - d, b].astype(F32)
    masks, masks_z = rim_masks()
    for b in range(SLOTS):
        for d in range(4):
            rows = slice((d // 2 * SLOTS + b) * C, (d // 2 * SLOTS + b + 1) * C)
            moved_ref[rows, d % 2 * 256 : d % 2 * 256 + 256] = jnp.where(
                masks[d ^ 1], total[d, b].astype(BF), pool[d ^ 1, b]
            )
        for d in range(2):
            rows = slice(((d + 2) * SLOTS + b) * C, ((d + 2) * SLOTS + b + 1) * C)
            moved_ref[rows, :] = jnp.where(
                masks_z[1 - d], total_z[d, b].astype(BF), pool_z[1 - d, b]
            )


def near_kernel(hg_ref, moved_ref, conv_ref, near_ref, fields):
    conv = jnp.concatenate([conv_ref[:, d * C : (d + 1) * C] for d in range(7)], 0)
    for b in range(SLOTS):
        block = hg_ref[b * C : (b + 1) * C, :]
        fields[0:C, :] = block
        for d in range(4):
            rows = slice((d // 2 * SLOTS + b) * C, (d // 2 * SLOTS + b + 1) * C)
            moved = moved_ref[rows, d % 2 * 256 : d % 2 * 256 + 256]
            for k, piece in enumerate(weave(d ^ 1, moved, block)):
                fields[(d + 1) * C : (d + 2) * C, k * 128 : (k + 1) * 128] = piece
        for d in range(2):
            rows = slice(((d + 2) * SLOTS + b) * C, ((d + 2) * SLOTS + b + 1) * C)
            fields[(d + 5) * C : (d + 6) * C, :] = moved_ref[rows, :]
        near_ref[b * C : (b + 1) * C, :] = dot(conv, fields[...], TN)


def far_kernel(counts, near_ref, got_xa, got_xb, got_ya, got_yb, conv_ref, out_ref, rows):
    px, py = parities()
    for got, direction in ((got_xa, px), (got_xb, 1 - px), (got_ya, 2 + py), (got_yb, 3 - py)):
        value = got[0:256, :]
        if got is got_xb or got is got_yb:
            value = jnp.where(inner("gx" if got is got_xb else "gy"), value, jnp.zeros_like(value))
        rows[direction] = value
    fields = []
    for d in range(4):
        conv = conv_ref[:, (d + 1) * C : (d + 2) * C]
        moved = [dot(conv, rows[d, k * C : (k + 1) * C, :], TN).astype(BF) for k in range(4)]
        table = spread(d // 2, 3 * (1 - d % 2))
        fields.append(dot(jnp.concatenate(moved, 0), table))
    for b in range(SLOTS):
        x_low, x_high, y_low, y_high = (
            fields[d][b % 4 * C : (b % 4 + 1) * C, b // 4 * 256 : b // 4 * 256 + 256]
            for d in (1, 0, 3, 2)
        )
        for k in range(4):
            lanes = slice(k * 128, (k + 1) * 128)
            x, y = (x_low, x_high)[k // 2], (y_low, y_high)[k % 2]
            x, y = (v[:, i * 128 : (i + 1) * 128] for v, i in ((x, k % 2), (y, k // 2)))
            grad = near_ref[b * C : (b + 1) * C, lanes] + (x + y)
            out_ref[b * C : (b + 1) * C, lanes] = jnp.where(b < counts[0], grad, 0.0).astype(BF)


def latent_kernel(cmap, own, got_x, got_ya, got_xy, out_ref, rows):
    rows[0:8] = own[OCT : OCT + 512, :].reshape(8, C, 128)
    rows[8:16] = got_x[...].reshape(8, C, 128)
    rows[16:24] = got_ya[256:768, :].reshape(8, C, 128)
    rows[24:32] = got_xy[...].reshape(8, C, 128)
    rows[32] = jnp.zeros((C, 128), BF)
    for k in range(8):
        out_ref[k * C : (k + 1) * C, :] = rows[cmap[0, k]]


def scale_kernel(scale, mine, theirs, conv_out, down_out, head_out):
    even = parity() == 0
    conv_in = jnp.concatenate(
        [
            jnp.where(even, mine[...], theirs[...]),
            jnp.where(even, theirs[...], mine[...]),
        ],
        0,
    )
    for k in range(3):
        conv_out[:, k * 128 : (k + 1) * 128] = conv_in[k * C : (k + 1) * C, :].astype(F32) * scale
    conv_out[:, 384:448] = conv_in[3 * C : 4 * C, 0:C].astype(F32) * scale
    down = jnp.concatenate([conv_in[256 + k * 128 : 384 + k * 128, :] for k in range(4)], 1)
    down_out[...] = dot(down, regroup()) * scale
    head_out[...] = conv_in[768:896, :].astype(F32) * scale


def route(there):
    nx, ny = lax.axis_size("gx"), lax.axis_size("gy")
    pairs = []
    for i in range(nx):
        for j in range(ny):
            x, y = there(i, j)
            pairs.append((i * ny + j, x * ny + y))
    return pairs


def send_to(value, there):
    return lax.ppermute(value, ("gx", "gy"), route(there))


def beside_x(value):
    return send_to(value, lambda i, j: (i ^ 1, j))


def beside_core(value):
    return send_to(value, lambda i, j: (i, j ^ 1))


def beside_both(value):
    return send_to(value, lambda i, j: (i ^ 1, j ^ 1))


def odd_partner(i, count):
    return min(max(i + 2 * (i % 2) - 1, -1), count)


def odd_x(value):
    nx = lax.axis_size("gx")
    return send_to(value, lambda i, j: (odd_partner(i, nx), j) if 0 < i < nx - 1 else (i, j ^ 1))


def odd_y(value):
    ny = lax.axis_size("gy")
    return send_to(value, lambda i, j: (i, odd_partner(j, ny) if 0 < j < ny - 1 else ny - 1 - j))


def inner(axis):
    at = lax.axis_index(axis)
    return (at > 0) & (at < lax.axis_size(axis) - 1)


def parity():
    bits = lax.axis_index("gx") * lax.axis_size("gy") + lax.axis_index("gy")
    count = 0
    for k in range((lax.axis_size("gx") * lax.axis_size("gy") - 1).bit_length()):
        count = count + lax.rem(lax.div(bits, 1 << k), 2)
    return lax.rem(count, 2)


def tie(value, *others):
    return lax.optimization_barrier((value, *others))[0]


def weight_sums(mine, other):
    bits = []
    for axis, first in (("gy", 2), ("gx", 1)):
        bit = first
        while bit < lax.axis_size(axis):
            bits.append((axis, bit))
            bit *= 2
    if len(bits) > 2:
        bits.insert(1, bits.pop(2))
    turned = []
    for at in range(0, len(bits) - 1, 2):
        turned += [bits[at + 1], bits[at]]
    turned += bits[len(turned) :]
    state = {"sum": mine}

    def there(at, i, j):
        axis, bit = (bits, turned)[(i.bit_count() + j.bit_count()) % 2][at]
        return (i ^ bit, j ^ 1) if axis == "gx" else (i, j ^ bit ^ 1)

    def step(at, waits):
        sent = tie(state["sum"], *waits) if waits else state["sum"]
        if at > len(bits):
            return sent, beside_core(sent)
        if at == 0:
            got = beside_core(other)
        else:
            got = send_to(sent, lambda i, j: there(at - 1, i, j))
        state["sum"] = (sent.astype(F32) + got.astype(F32)).astype(BF)
        return state["sum"]

    return step, len(bits) + 1


def call(kernel, outs, ins, spaces="", scratch=(), last=0, us=1.0):
    kinds = {"s": pltpu.SMEM, "h": pltpu.HBM, "v": pltpu.VMEM}
    spaces = spaces + "v" * (len(ins) - len(spaces))
    ins = [
        pltpu.with_memory_space_constraint(value, pltpu.HBM) if space == "h" else value
        for value, space in zip(ins, spaces)
    ]
    keep = len(outs) - last
    return pl.pallas_call(
        kernel,
        out_shape=[
            pltpu.VMEM(shape, kind) if at < keep else jax.ShapeDtypeStruct(shape, kind)
            for at, (shape, kind) in enumerate(outs)
        ],
        in_specs=[pl.BlockSpec(memory_space=kinds[k]) for k in spaces],
        out_specs=[pl.BlockSpec(memory_space=pltpu.VMEM)] * len(outs),
        scratch_shapes=list(scratch),
        compiler_params=pltpu.CompilerParams(vmem_limit_bytes=32 * 1024 * 1024),
        cost_estimate=pl.CostEstimate(
            flops=int(us * 1e9), bytes_accessed=int(us * 3e6), transcendentals=0
        ),
    )(*ins)


def body(
    features, neighbours, counts, conv_weight, down_weight, head_weight, coarse_map, latent_grad
):
    flat = features.reshape(SLOTS * C, 512)
    lat = latent_grad.reshape(512, 128)
    send_xa, send_xb, send_ya, send_yb = call(
        pack_kernel,
        [
            ((784, 128), BF), ((256, 128), BF), ((784, 128), BF), ((256, 128), BF),
        ],
        (coarse_map, flat, lat),
        "hhh",
        [pltpu.VMEM((512, 512), BF), pltpu.SMEM((1, 8), jnp.int32), pltpu.SemaphoreType.DMA((4,))],
        us=1.5,
    )
    got_xy = beside_both(send_xa)
    got_xb = odd_x(send_xb)
    got_ya = beside_core(send_ya)
    got_yb = odd_y(send_yb)
    (store,) = call(
        prep_kernel,
        [((STORE, 512), BF)],
        (counts, flat, conv_weight, down_weight, head_weight),
        "shhhh",
        [pltpu.VMEM((C, 448), BF), pltpu.SemaphoreType.DMA((4,))],
        us=1.5,
    )
    got_xa = beside_core(tie(got_xy, got_xb, got_yb, got_ya, store))
    hg, mine, other, send = call(
        main_kernel,
        [((512, 512), BF), ((448, 128), BF), ((448, 128), BF), ((SEND, 128), BF)],
        (neighbours, coarse_map, lat, got_xa, got_xb, got_ya, got_yb, got_xy, store),
        "hhh",
        [
            pltpu.SMEM((SLOTS, 6), jnp.int32),
            pltpu.SMEM((1, 8), jnp.int32),
            pltpu.SemaphoreType.DMA((3,)),
            pltpu.VMEM((896, 128), F32),
            pltpu.VMEM((512, 128), BF),
            pltpu.VMEM((4, 17, C, 256), BF),
            pltpu.VMEM((448, SLOTS * 512), BF),
            pltpu.VMEM((C, SLOTS * 512), BF),
            pltpu.VMEM((SLOTS, C, 512), F32),
            pltpu.VMEM((512, 512), BF),
            pltpu.VMEM((SLOTS + 1, C, 128), BF),
            pltpu.VMEM((4, 5, C, 128), F32),
            pltpu.VMEM((3, 16, 128), jnp.int32),
            pltpu.SMEM((3, 16, 128), jnp.int32),
            pltpu.SemaphoreType.DMA,
        ],
        us=6.0,
    )

    sum_step, steps = weight_sums(mine, other)
    mine = sum_step(0, ())
    got_xa = beside_x(tie(send[XA : XA + 256], mine))
    got_xb = odd_x(send[XB : XB + 256])
    got_yb = odd_y(tie(send[YB : YB + 256], mine))
    mine = sum_step(1, ())
    got_ya = beside_core(tie(send[YA : OCT + 512], mine))
    (moved,) = call(
        roll_kernel,
        [((2048, 512), BF)],
        (neighbours, tie(hg, mine, got_xb)),
        "h",
        [
            pltpu.VMEM((4, 8, C, 256), BF),
            pltpu.VMEM((2, 8, C, 512), BF),
            pltpu.VMEM((4, 9, C, 256), F32),
            pltpu.VMEM((2, 9, C, 512), F32),
            pltpu.SMEM((SLOTS, 6), jnp.int32),
            pltpu.SemaphoreType.DMA,
        ],
        us=2.5,
    )
    mine = sum_step(2, ())
    (near,) = call(
        near_kernel,
        [((512, 512), F32)],
        (hg, tie(moved, mine), conv_weight),
        "",
        [pltpu.VMEM((448, 512), BF)],
        us=1.0,
    )
    got_xy = beside_both(tie(send[OCT : OCT + 512], near))
    mine = sum_step(3, (moved, got_ya, got_xa, got_yb, got_xb,))
    (grad,) = call(
        far_kernel,
        [((512, 512), BF)],
        (counts, tie(near, mine), got_xa, got_xb, got_ya, got_yb, conv_weight),
        "s",
        [pltpu.VMEM((4, 256, 128), BF)],
        1,
        us=1.8,
    )
    got_x = beside_core(tie(got_xy, mine))
    (latent,) = call(
        latent_kernel,
        [((512, 128), BF)],
        (coarse_map, send, got_x, got_ya, got_xy),
        "s",
        [pltpu.VMEM((33, C, 128), BF)],
        1,
        us=1.2,
    )
    mine = sum_step(4, (near,))
    for at in range(5, steps):
        mine = sum_step(at, ())
    mine, theirs = sum_step(steps, (grad, got_x,))
    scale = float(SLOTS * lax.axis_size("gx") * lax.axis_size("gy")) ** (-0.5)
    conv_grad, down_grad, head_grad = call(
        lambda *refs: scale_kernel(scale, *refs),
        [((C, 448), F32), ((128, 512), F32), ((128, 128), F32)],
        (mine, theirs),
        last=3,
    )
    return (
        latent.reshape(1, 512, 128), grad.reshape(SLOTS, C, 512), conv_grad, down_grad, head_grad,
    )


def solution(mesh):
    both = ("gx", "gy")
    placed = (
        P(both, None, None), P(both, None), P(both), P(), P(), P(), P(both, None),
        P(both, None, None),
    )
    return jax.shard_map(
        body,
        mesh=mesh,
        in_specs=placed,
        out_specs=(P(both, None, None), P(both, None, None), P(), P(), P()),
        check_vma=False,
    )
```
